128 devices in a mesh: seq: 32 (over z, x, core), head: 4 (over y).
Axes of the slice: x: 4, y: 4, z: 4, core: 2. Of those that a mesh axis runs over, the one named last changes fastest.
Arguments:
- projections: bfloat16 [16384, 3, 4096], P('seq', None, 'head'), may hold values from -53 to 53
- output_gradient: bfloat16 [16384, 5120], P('seq', 'head'), may hold values from -0.75 to 0.75
- output_projection_weight: bfloat16 [5120, 4096], P(None, 'head'), may hold values from -0.625 to 0.625
- kept_token_indices: int32 [32, 192], P('seq'), may hold values from -1 to 511, as said below
- surviving_token_count: int32 [32], replicated, may hold values from 64 to 192, as said below
Outputs:
- projection_grad: bfloat16 [16384, 3, 4096], P('seq', None, 'head')
- weight_grad: float32 [5120, 4096], P('seq', 'head')
The draws below stay inside these ranges and needn't reach their ends.
Inputs may be any that keep to these rules, and one draw needn't show every extreme that they name: `kept_token_indices`: row s holds, in its first surviving_token_count[s] entries, distinct indices 0 to 511 in ascending order; its other entries are -1. Every shard that keeps 192 tokens keeps its last token. `surviving_token_count`: some shard keeps exactly 192 tokens and some other keeps exactly 64.
All inputs are finite; a program needn't handle non-finite values.
Results may differ from the reference program's by a relative error of at most 0.0099.
Values may be sent and summed in bfloat16 or wider, within the bound.
A program may use at most 128 MiB of HBM per device.

```python
import math
import jax
import jax.numpy as jnp
from jax import lax

D = 5120
DH = 128
HEADS = 32
TOK_DEV = 512
TOKENS = 16384
CAP = 192
N_SEQ = 32


def shared_counts(key):
    inner_key = jax.random.fold_in(key, 101)
    first_key, second_key, third_key = jax.random.split(inner_key, 3)
    floor_count = CAP // 3
    drawn_counts = jax.random.randint(first_key, (N_SEQ,), floor_count, CAP + 1)
    full_shard = jax.random.randint(second_key, (), 0, N_SEQ)
    low_shard = (full_shard + 1 + jax.random.randint(third_key, (), 0, N_SEQ - 1)) % N_SEQ
    drawn_counts = drawn_counts.at[full_shard].set(CAP).at[low_shard].set(floor_count)
    return drawn_counts.astype(jnp.int32)


def draw_surviving_token_count(key, part):
    return shared_counts(key)


def draw_kept_token_indices(key, part):
    live_counts = shared_counts(key)
    key = jax.random.fold_in(key, 3)
    shard_keys = jax.random.split(key, N_SEQ)
    orders = jax.vmap(lambda single: jax.random.permutation(single, TOK_DEV))(shard_keys)
    chosen = orders[:, :CAP].astype(jnp.int32)
    last_index = jnp.int32(TOK_DEV - 1)
    holds_last = jnp.any(chosen == last_index, axis=1)
    needs_last = (live_counts == CAP) & jnp.logical_not(holds_last)
    chosen = chosen.at[:, 0].set(jnp.where(needs_last, last_index, chosen[:, 0]))
    slot_ids = jnp.arange(CAP, dtype=jnp.int32)[None, :]
    marked = jnp.where(slot_ids < live_counts[:, None], chosen, TOK_DEV)
    ordered = jnp.sort(marked, axis=1)
    return jnp.where(ordered == TOK_DEV, -1, ordered).astype(jnp.int32)


def draw_projections(key, part):
    key = jax.random.fold_in(key, 7)
    base_key = jax.random.fold_in(key, 0)
    full_shape = (TOKENS, 3, HEADS * DH)
    return jax.random.normal(base_key, full_shape, jnp.float32).astype(jnp.bfloat16)


def with_spikes(values, rng, source, target, shards_of, factor):
    owner, partner = [(jnp.arange(values.shape[dim]) // (values.shape[dim] // shards_of)).reshape([-1 if axis == dim else 1 for axis in range(values.ndim)]) for dim in (source, target)]
    chosen = jax.random.permutation(rng, shards_of)[partner]
    strong = (owner == chosen) | (owner == (partner + shards_of // 2) % shards_of)
    return jnp.where(strong, factor * values, values)


def levels(rng, extent, cuts, least, top_value):
    level = 1.0
    for axis_at, blocks in cuts:
        steps = jax.random.uniform(jax.random.fold_in(jax.random.fold_in(rng, 6), axis_at), (blocks,), jnp.float32, least / len(cuts), top_value / len(cuts))
        level = level * jnp.repeat(jnp.exp(steps), extent[axis_at] // blocks).reshape((-1,) + (1,) * (len(extent) - 1 - axis_at))
    return level


def scatter_about(own_key, shape, scale, limit, cuts=(), held_as=jnp.bfloat16):
    level = levels(own_key, shape, cuts, -0.22, 0.18) if cuts else 1.0
    drawn = jax.random.normal(own_key, shape, jnp.float32) * scale * level
    return jnp.minimum(jnp.maximum(drawn, -limit), limit).astype(held_as)


def bell_draw_with(rng, extent, scale, reach, cuts, heavy, held_as=jnp.bfloat16):
    entries = scale * jax.random.normal(rng, extent, jnp.float32)
    if cuts:
        entries = entries * levels(rng, extent, cuts, -0.22, 0.18)
    return jnp.clip(with_spikes(entries, jax.random.fold_in(rng, 3), *heavy), -reach, reach).astype(held_as)


def setup_inputs(seed: int = 0) -> dict:
    seeds = jax.random.split(jax.random.key(seed), 6)
    return {
        "projections": draw_projections(jax.random.fold_in(seeds[5], 71), 0),
        "output_gradient": bell_draw_with(seeds[1], (TOKENS, D), 0.125, 0.75, ((0, 32), (1, 4)), (0, 1, 32, 2.75)),
        "output_projection_weight": scatter_about(seeds[2], (D, HEADS * DH), (D // 64) ** -0.5, 0.625, ((1, 4),)),
        "kept_token_indices": draw_kept_token_indices(jax.random.fold_in(seeds[5], 71), 0),
        "surviving_token_count": draw_surviving_token_count(jax.random.fold_in(seeds[5], 71), 0),
    }


def head_major(matrix):
    return matrix.reshape(matrix.shape[0], HEADS, DH).transpose(1, 0, 2)

def reference(projections, output_gradient, output_projection_weight, kept_token_indices, surviving_token_count):
    slot_total = N_SEQ * CAP
    slot_index = jnp.arange(slot_total, dtype=jnp.int32)
    owning_shard = slot_index // CAP
    inside_shard_index = slot_index % CAP
    slot_is_alive = inside_shard_index < surviving_token_count[owning_shard]
    local_index = kept_token_indices.reshape(slot_total).astype(jnp.int32)
    token_row = owning_shard * TOK_DEV + jnp.maximum(local_index, 0)
    packed = jnp.where(slot_is_alive[:, None, None], projections[token_row], jnp.zeros((), jnp.bfloat16))
    grad_rows = jnp.where(slot_is_alive[:, None], output_gradient[token_row], jnp.zeros((), jnp.bfloat16))
    grad_attn = jnp.dot(grad_rows, output_projection_weight, preferred_element_type=jnp.float32).astype(jnp.bfloat16)
    allowed = slot_is_alive[None, :] & (slot_index[None, :] <= slot_index[:, None])
    score_scale = 1.0 / math.sqrt(DH)

    def per_head(operands):
        query, key_mat, value_mat, grad_head = operands
        scores = jnp.dot(query, key_mat.T, preferred_element_type=jnp.float32) * score_scale
        scores = jnp.where(allowed, scores, -1e+30)
        row_peak = lax.optimization_barrier(jnp.max(scores, axis=1, keepdims=True))
        weights = jnp.where(allowed, jnp.exp(scores - row_peak), 0.0)
        probabilities = weights / lax.optimization_barrier(jnp.sum(weights, axis=1, keepdims=True))
        probs_low = probabilities.astype(jnp.bfloat16)
        attended = jnp.dot(probs_low, value_mat, preferred_element_type=jnp.float32)
        grad_probs = jnp.dot(grad_head, value_mat.T, preferred_element_type=jnp.float32)
        row_dot = lax.optimization_barrier(jnp.sum(grad_head.astype(jnp.float32) * attended, axis=1, keepdims=True))
        grad_scores = (probabilities * (grad_probs - row_dot)).astype(jnp.bfloat16)
        grad_query = (jnp.dot(grad_scores, key_mat, preferred_element_type=jnp.float32) * score_scale).astype(jnp.bfloat16)
        grad_key = (jnp.dot(grad_scores.T, query, preferred_element_type=jnp.float32) * score_scale).astype(jnp.bfloat16)
        grad_value = jnp.dot(probs_low.T, grad_head, preferred_element_type=jnp.float32).astype(jnp.bfloat16)
        return (grad_query, grad_key, grad_value, attended.astype(jnp.bfloat16))
    results = lax.map(per_head, (head_major(packed[:, 0]), head_major(packed[:, 1]), head_major(packed[:, 2]), head_major(grad_attn)))

    def to_rows_layout(stacked):
        return stacked.transpose(1, 0, 2).reshape(slot_total, HEADS * DH)
    grad_query = to_rows_layout(results[0])
    grad_key = to_rows_layout(results[1])
    grad_value = to_rows_layout(results[2])
    attended_low = to_rows_layout(results[3])
    weight_grad = jnp.dot(grad_rows.T, attended_low, preferred_element_type=jnp.float32)
    grad_packed = jnp.stack([grad_query, grad_key, grad_value], axis=1)
    target = jnp.where(slot_is_alive, token_row, N_SEQ * TOK_DEV).astype(jnp.int32)
    projection_grad = jnp.zeros((N_SEQ * TOK_DEV, 3, HEADS * DH), jnp.bfloat16).at[target].set(grad_packed, mode='drop')
    return (projection_grad, weight_grad)
```

```python
import math

import jax
import jax.numpy as jnp
from jax import lax
from jax.experimental import pallas as pl
from jax.experimental.pallas import tpu as pltpu
from jax.sharding import PartitionSpec as P

DH = 128
BQ = 256
BK = 512
GROUP = 16
NEG = -1e30


def contract_rows(left, right):
    return lax.dot_general(
        left, right, (((0,), (0,)), ((), ())), preferred_element_type=jnp.float32
    )


def contract_cols(left, right):
    return lax.dot_general(
        left, right, (((1,), (1,)), ((), ())), preferred_element_type=jnp.float32
    )


def wide(column, width):
    return jnp.concatenate([column] * (width // DH), axis=1)


def attend_kernel(
    count_ref,
    quarter_ref,
    q_ref,
    k_ref,
    bias_ref,
    q_out,
    k_out,
    qc,
    gc,
    kc,
    vc,
    dkc,
    dvc,
    oc,
    s_scr,
    qpos,
    peak,
    total,
    acc,
    group_pos,
):
    shards, part_rows, _ = q_ref.shape
    slots = k_ref.shape[1]
    quarter = quarter_ref[0]
    groups = part_rows // GROUP
    score_scale = 1.0 / math.sqrt(DH)
    log2e = score_scale * math.log2(math.e)

    def pack(s, carry):
        at_k, at_q = carry
        live = (count_ref[s] + GROUP - 1) // GROUP
        first = lax.rem(quarter + s, 4)
        at_k = pl.multiple_of(at_k, GROUP)
        at_q = pl.multiple_of(at_q, GROUP)
        kc[pl.ds(at_k, slots), :] = k_ref[s, :, :DH]
        vc[pl.ds(at_k, slots), :] = k_ref[s, :, DH:]
        qc[pl.ds(at_q, part_rows), :] = q_ref[s, :, :DH]
        gc[pl.ds(at_q, part_rows), :] = q_ref[s, :, DH:]
        rows = lax.broadcasted_iota(jnp.int32, (GROUP, DH), 0)
        for i in range(groups):
            base = at_k + (first + 4 * i) * GROUP
            qpos[pl.ds(at_q + i * GROUP, GROUP), :] = base + rows
            group_pos[at_q // GROUP + i] = base
        return at_k + live * GROUP, at_q + (live - first + 3) // 4 * GROUP

    end_k, end_q = lax.fori_loop(0, shards, pack, (jnp.int32(0), jnp.int32(0)))
    end_k = pl.multiple_of(end_k, GROUP)
    end_q = pl.multiple_of(end_q, GROUP)
    kc[pl.ds(end_k, BK), :] = jnp.zeros((BK, DH), jnp.bfloat16)
    vc[pl.ds(end_k, BK), :] = jnp.zeros((BK, DH), jnp.bfloat16)
    qc[pl.ds(end_q, BQ), :] = jnp.zeros((BQ, DH), jnp.bfloat16)
    gc[pl.ds(end_q, BQ), :] = jnp.zeros((BQ, DH), jnp.bfloat16)
    qpos[pl.ds(end_q, BQ), :] = jnp.zeros((BQ, DH), jnp.int32)
    blocks = (end_q + BQ - 1) // BQ
    oc[pl.ds(pl.multiple_of(blocks * BQ, BQ), part_rows), :] = jnp.zeros(
        (part_rows, 2 * DH), jnp.bfloat16
    )

    def clear(i, carry):
        rows = pl.ds(pl.multiple_of(i * slots, slots), slots)
        dkc[rows, :] = jnp.zeros((slots, DH), jnp.float32)
        dvc[rows, :] = jnp.zeros((slots, DH), jnp.float32)
        return carry

    lax.fori_loop(0, shards, clear, 0)

    def block(b, carry):
        rows = pl.ds(pl.multiple_of(b * BQ, BQ), BQ)
        last_group = jnp.minimum((b + 1) * (BQ // GROUP), end_q // GROUP) - 1
        chunks = (group_pos[last_group] + GROUP + BK - 1) // BK
        clear_chunks = (group_pos[b * (BQ // GROUP)] + 1) // BK

        def score(c, masked):
            at = pl.multiple_of(c * BK, BK)
            keys = pl.ds(at, BK)
            s = contract_cols(qc[rows, :], kc[keys, :]) + bias_ref[:, keys]
            if masked:
                column = at + lax.broadcasted_iota(jnp.int32, (BQ, BK), 1)
                s = jnp.where(column <= wide(qpos[rows, :], BK), s, NEG)
            s_scr[:, keys] = s
            top = peak[...]
            for i in range(BK // DH):
                top = jnp.maximum(top, s[:, i * DH : (i + 1) * DH])
            peak[...] = top

        peak[...] = jnp.full((BQ, DH), NEG, jnp.float32)

        def score_clear(c, carry):
            score(c, False)
            return carry

        def score_masked(c, carry):
            score(c, True)
            return carry

        lax.fori_loop(0, clear_chunks, score_clear, 0)
        lax.fori_loop(clear_chunks, chunks, score_masked, 0)
        peak[...] = jnp.broadcast_to(jnp.max(peak[...], axis=1, keepdims=True), (BQ, DH))
        total[...] = jnp.zeros((BQ, DH), jnp.float32)
        acc[...] = jnp.zeros((BQ, DH), jnp.float32)

        def weigh(c, carry):
            keys = pl.ds(pl.multiple_of(c * BK, BK), BK)
            p = jnp.exp2((s_scr[:, keys] - wide(peak[...], BK)) * log2e)
            s_scr[:, keys] = p
            add = total[...]
            for i in range(BK // DH):
                add = add + p[:, i * DH : (i + 1) * DH]
            total[...] = add
            acc[...] += jnp.dot(
                p.astype(jnp.bfloat16), vc[keys, :], preferred_element_type=jnp.float32
            )
            return carry

        lax.fori_loop(0, chunks, weigh, 0)
        inverse = 1.0 / jnp.broadcast_to(
            jnp.sum(total[...], axis=1, keepdims=True), (BQ, DH)
        )
        total[...] = inverse
        attended = acc[...] * inverse
        oc[rows, DH:] = attended.astype(jnp.bfloat16)
        peak[...] = jnp.broadcast_to(
            jnp.sum(gc[rows, :].astype(jnp.float32) * attended, axis=1, keepdims=True), (BQ, DH)
        )
        acc[...] = jnp.zeros((BQ, DH), jnp.float32)

        def back(c, carry):
            keys = pl.ds(pl.multiple_of(c * BK, BK), BK)
            p = s_scr[:, keys] * wide(total[...], BK)
            grad_probs = contract_cols(gc[rows, :], vc[keys, :])
            ds = (p * (grad_probs - wide(peak[...], BK))).astype(jnp.bfloat16)
            acc[...] += jnp.dot(ds, kc[keys, :], preferred_element_type=jnp.float32)
            dkc[keys, :] += contract_rows(ds, qc[rows, :])
            dvc[keys, :] += contract_rows(p.astype(jnp.bfloat16), gc[rows, :])
            return carry

        lax.fori_loop(0, chunks, back, 0)
        oc[rows, :DH] = (acc[...] * score_scale).astype(jnp.bfloat16)
        return carry

    lax.fori_loop(0, blocks, block, 0)

    def unpack(s, carry):
        at_k, at_q = carry
        live = (count_ref[s] + GROUP - 1) // GROUP
        first = lax.rem(quarter + s, 4)
        at_k = pl.multiple_of(at_k, GROUP)
        at_q = pl.multiple_of(at_q, GROUP)
        q_out[s] = oc[pl.ds(at_q, part_rows), :]
        k_out[s, :, :DH] = (dkc[pl.ds(at_k, slots), :] * score_scale).astype(jnp.bfloat16)
        k_out[s, :, DH:] = dvc[pl.ds(at_k, slots), :].astype(jnp.bfloat16)
        return at_k + live * GROUP, at_q + (live - first + 3) // 4 * GROUP

    lax.fori_loop(0, shards, unpack, (jnp.int32(0), jnp.int32(0)))


def attend(counts, quarter, query_in, key_in):
    shards, part_rows, _ = query_in.shape
    slots = key_in.shape[1]
    keys = shards * slots
    queries = shards * part_rows
    rounded = (counts + GROUP - 1) // GROUP * GROUP
    start = jnp.cumsum(rounded) - rounded
    place = jnp.arange(keys, dtype=jnp.int32)[None, :]
    live = jnp.any(
        (place >= start[:, None]) & (place < (start + counts)[:, None]), axis=0, keepdims=True
    )
    bias = jnp.where(live, 0.0, NEG).astype(jnp.float32)
    vmem = pl.BlockSpec(memory_space=pltpu.VMEM)
    smem = pl.BlockSpec(memory_space=pltpu.SMEM)
    return pl.pallas_call(
        attend_kernel,
        out_shape=(
            jax.ShapeDtypeStruct(query_in.shape, jnp.bfloat16),
            jax.ShapeDtypeStruct(key_in.shape, jnp.bfloat16),
        ),
        in_specs=[smem, smem, vmem, vmem, vmem],
        out_specs=(vmem, vmem),
        scratch_shapes=[
            pltpu.VMEM((queries + BQ, DH), jnp.bfloat16),
            pltpu.VMEM((queries + BQ, DH), jnp.bfloat16),
            pltpu.VMEM((keys + BK, DH), jnp.bfloat16),
            pltpu.VMEM((keys + BK, DH), jnp.bfloat16),
            pltpu.VMEM((keys, DH), jnp.float32),
            pltpu.VMEM((keys, DH), jnp.float32),
            pltpu.VMEM((queries + BQ, 2 * DH), jnp.bfloat16),
            pltpu.VMEM((BQ, keys), jnp.float32),
            pltpu.VMEM((queries + BQ, DH), jnp.int32),
            pltpu.VMEM((BQ, DH), jnp.float32),
            pltpu.VMEM((BQ, DH), jnp.float32),
            pltpu.VMEM((BQ, DH), jnp.float32),
            pltpu.SMEM((queries // GROUP + 8,), jnp.int32),
        ],
        compiler_params=pltpu.CompilerParams(vmem_limit_bytes=48 * 1024 * 1024),
        cost_estimate=pl.CostEstimate(
            flops=6 * queries * keys * DH, bytes_accessed=16 * 1024 * 1024, transcendentals=0
        ),
        name="attend",
    )(counts, quarter, query_in, key_in, bias)


def on_device(
    projections,
    output_gradient,
    output_projection_weight,
    kept_token_indices,
    surviving_token_count,
):
    tok_dev = projections.shape[0]
    group_width = projections.shape[2]
    slots = kept_token_indices.shape[1]
    heads_local = group_width // DH
    seq_count = lax.axis_size("seq")
    quarters = seq_count // heads_local
    part_rows = slots // quarters
    me = lax.axis_index("seq")
    my_quarter = (me % quarters).astype(jnp.int32)[None]

    kept = kept_token_indices[0]
    dealt = kept.reshape(part_rows // GROUP, quarters, GROUP).transpose(1, 0, 2)
    dealt = lax.dynamic_slice_in_dim(
        jnp.concatenate([dealt, dealt], axis=0), me % quarters, quarters, axis=0
    ).reshape(slots)
    token = jnp.arange(tok_dev, dtype=jnp.int32)[None, :]
    selector = (kept[:, None] == token).astype(jnp.bfloat16)
    dealt_selector = (dealt[:, None] == token).astype(jnp.bfloat16)

    def pick(which, values):
        return jnp.dot(which, values, preferred_element_type=jnp.float32).astype(jnp.bfloat16)

    grad_local = pick(dealt_selector, output_gradient)
    grad_rows = lax.all_gather(grad_local, "head", axis=1, tiled=True)
    query = pick(dealt_selector, projections[:, 0])
    key = pick(selector, projections[:, 1])
    value = pick(selector, projections[:, 2])

    def head_major(matrix):
        return matrix.reshape(slots, heads_local, DH).transpose(1, 0, 2)

    key_side = jnp.concatenate([head_major(key), head_major(value)], axis=2)
    key_side = jnp.broadcast_to(key_side[:, None], (heads_local, quarters, slots, 2 * DH))
    key_side = key_side.reshape(seq_count, slots, 2 * DH)
    key_in = lax.all_to_all(key_side, "seq", split_axis=0, concat_axis=0, tiled=True)
    grad_attn = jnp.dot(
        grad_rows, output_projection_weight, preferred_element_type=jnp.float32
    ).astype(jnp.bfloat16)
    query_side = jnp.concatenate([head_major(query), head_major(grad_attn)], axis=2)
    query_side = query_side.reshape(seq_count, part_rows, 2 * DH)
    query_in = lax.all_to_all(query_side, "seq", split_axis=0, concat_axis=0, tiled=True)

    query_back, key_back = attend(surviving_token_count, my_quarter, query_in, key_in)

    query_home = lax.all_to_all(query_back, "seq", split_axis=0, concat_axis=0, tiled=True)
    query_home = query_home.reshape(heads_local, slots, 2 * DH)
    attended_low = query_home[:, :, DH:].transpose(1, 0, 2).reshape(slots, group_width)
    weight_grad = lax.psum_scatter(
        contract_rows(grad_rows, attended_low).astype(jnp.bfloat16),
        "seq",
        scatter_dimension=0,
        tiled=True,
    ).astype(jnp.float32)
    key_home = lax.all_to_all(key_back, "seq", split_axis=0, concat_axis=0, tiled=True)
    key_home = jnp.sum(
        key_home.reshape(heads_local, quarters, slots, 2 * DH).astype(jnp.float32), axis=1
    ).astype(jnp.bfloat16)

    def rows_major(part):
        return part.transpose(1, 0, 2).reshape(slots, group_width)

    projection_grad = jnp.stack(
        [
            contract_rows(dealt_selector, rows_major(query_home[:, :, :DH])).astype(jnp.bfloat16),
            contract_rows(selector, rows_major(key_home[:, :, :DH])).astype(jnp.bfloat16),
            contract_rows(selector, rows_major(key_home[:, :, DH:])).astype(jnp.bfloat16),
        ],
        axis=1,
    )
    return (projection_grad, weight_grad)


def solution(mesh):
    return jax.shard_map(
        on_device,
        mesh=mesh,
        in_specs=(P("seq", None, "head"), P("seq", "head"), P(None, "head"), P("seq", None), P()),
        out_specs=(P("seq", None, "head"), P("seq", "head")),
        check_vma=False,
    )
```

```python
import math

import jax
import jax.numpy as jnp
from jax import lax
from jax.experimental import pallas as pl
from jax.experimental.pallas import tpu as pltpu
from jax.sharding import PartitionSpec as P

DH = 128
BQ = 256
BK = 512
GROUP = 16
NEG = -1e30


def contract_rows(left, right):
    return lax.dot_general(
        left, right, (((0,), (0,)), ((), ())), preferred_element_type=jnp.float32
    )


def contract_cols(left, right):
    return lax.dot_general(
        left, right, (((1,), (1,)), ((), ())), preferred_element_type=jnp.float32
    )


def wide(column, width):
    return jnp.concatenate([column] * (width // DH), axis=1)


def attend_kernel(
    count_ref,
    quarter_ref,
    q_ref,
    k_ref,
    bias_ref,
    dq_out,
    o_out,
    k_out,
    qc,
    gc,
    kc,
    vc,
    dkc,
    dvc,
    oc,
    s_scr,
    qpos,
    peak,
    total,
    acc,
    group_pos,
):
    shards, part_rows, _ = q_ref.shape
    slots = k_ref.shape[1]
    quarter = quarter_ref[0]
    groups = part_rows // GROUP
    score_scale = 1.0 / math.sqrt(DH)
    log2e = score_scale * math.log2(math.e)

    def pack(s, carry):
        at_k, at_q = carry
        live = (count_ref[s] + GROUP - 1) // GROUP
        first = lax.rem(quarter + s, 4)
        at_k = pl.multiple_of(at_k, GROUP)
        at_q = pl.multiple_of(at_q, GROUP)
        kc[pl.ds(at_k, slots), :] = k_ref[s, :, :DH]
        vc[pl.ds(at_k, slots), :] = k_ref[s, :, DH:]
        qc[pl.ds(at_q, part_rows), :] = q_ref[s, :, :DH]
        gc[pl.ds(at_q, part_rows), :] = q_ref[s, :, DH:]
        rows = lax.broadcasted_iota(jnp.int32, (GROUP, DH), 0)
        for i in range(groups):
            base = at_k + (first + 4 * i) * GROUP
            qpos[pl.ds(at_q + i * GROUP, GROUP), :] = base + rows
            group_pos[at_q // GROUP + i] = base
        return at_k + live * GROUP, at_q + (live - first + 3) // 4 * GROUP

    end_k, end_q = lax.fori_loop(0, shards, pack, (jnp.int32(0), jnp.int32(0)))
    end_k = pl.multiple_of(end_k, GROUP)
    end_q = pl.multiple_of(end_q, GROUP)
    kc[pl.ds(end_k, BK), :] = jnp.zeros((BK, DH), jnp.bfloat16)
    vc[pl.ds(end_k, BK), :] = jnp.zeros((BK, DH), jnp.bfloat16)
    qc[pl.ds(end_q, BQ), :] = jnp.zeros((BQ, DH), jnp.bfloat16)
    gc[pl.ds(end_q, BQ), :] = jnp.zeros((BQ, DH), jnp.bfloat16)
    qpos[pl.ds(end_q, BQ), :] = jnp.zeros((BQ, DH), jnp.int32)
    blocks = (end_q + BQ - 1) // BQ
    oc[pl.ds(pl.multiple_of(blocks * BQ, BQ), part_rows), :] = jnp.zeros(
        (part_rows, 2 * DH), jnp.bfloat16
    )

    def clear(i, carry):
        rows = pl.ds(pl.multiple_of(i * slots, slots), slots)
        dkc[rows, :] = jnp.zeros((slots, DH), jnp.float32)
        dvc[rows, :] = jnp.zeros((slots, DH), jnp.float32)
        return carry

    lax.fori_loop(0, shards, clear, 0)

    def block(b, carry):
        rows = pl.ds(pl.multiple_of(b * BQ, BQ), BQ)
        last_group = jnp.minimum((b + 1) * (BQ // GROUP), end_q // GROUP) - 1
        chunks = (group_pos[last_group] + GROUP + BK - 1) // BK
        clear_chunks = (group_pos[b * (BQ // GROUP)] + 1) // BK

        def score(c, masked):
            at = pl.multiple_of(c * BK, BK)
            keys = pl.ds(at, BK)
            s = contract_cols(qc[rows, :], kc[keys, :]) + bias_ref[:, keys]
            if masked:
                column = at + lax.broadcasted_iota(jnp.int32, (BQ, BK), 1)
                s = jnp.where(column <= wide(qpos[rows, :], BK), s, NEG)
            s_scr[:, keys] = s
            top = peak[...]
            for i in range(BK // DH):
                top = jnp.maximum(top, s[:, i * DH : (i + 1) * DH])
            peak[...] = top

        peak[...] = jnp.full((BQ, DH), NEG, jnp.float32)

        def score_clear(c, carry):
            score(c, False)
            return carry

        def score_masked(c, carry):
            score(c, True)
            return carry

        lax.fori_loop(0, clear_chunks, score_clear, 0)
        lax.fori_loop(clear_chunks, chunks, score_masked, 0)
        peak[...] = jnp.broadcast_to(jnp.max(peak[...], axis=1, keepdims=True), (BQ, DH))
        total[...] = jnp.zeros((BQ, DH), jnp.float32)
        acc[...] = jnp.zeros((BQ, DH), jnp.float32)

        def weigh(c, carry):
            keys = pl.ds(pl.multiple_of(c * BK, BK), BK)
            p = jnp.exp2((s_scr[:, keys] - wide(peak[...], BK)) * log2e)
            s_scr[:, keys] = p
            add = total[...]
            for i in range(BK // DH):
                add = add + p[:, i * DH : (i + 1) * DH]
            total[...] = add
            acc[...] += jnp.dot(
                p.astype(jnp.bfloat16), vc[keys, :], preferred_element_type=jnp.float32
            )
            return carry

        lax.fori_loop(0, chunks, weigh, 0)
        inverse = 1.0 / jnp.broadcast_to(
            jnp.sum(total[...], axis=1, keepdims=True), (BQ, DH)
        )
        total[...] = inverse
        attended = acc[...] * inverse
        oc[rows, DH:] = attended.astype(jnp.bfloat16)
        peak[...] = jnp.broadcast_to(
            jnp.sum(gc[rows, :].astype(jnp.float32) * attended, axis=1, keepdims=True), (BQ, DH)
        )
        acc[...] = jnp.zeros((BQ, DH), jnp.float32)

        def back(c, carry):
            keys = pl.ds(pl.multiple_of(c * BK, BK), BK)
            p = s_scr[:, keys] * wide(total[...], BK)
            grad_probs = contract_cols(gc[rows, :], vc[keys, :])
            ds = (p * (grad_probs - wide(peak[...], BK))).astype(jnp.bfloat16)
            acc[...] += jnp.dot(ds, kc[keys, :], preferred_element_type=jnp.float32)
            dkc[keys, :] += contract_rows(ds, qc[rows, :])
            dvc[keys, :] += contract_rows(p.astype(jnp.bfloat16), gc[rows, :])
            return carry

        lax.fori_loop(0, chunks, back, 0)
        oc[rows, :DH] = (acc[...] * score_scale).astype(jnp.bfloat16)
        return carry

    lax.fori_loop(0, blocks, block, 0)

    def unpack(s, carry):
        at_k, at_q = carry
        live = (count_ref[s] + GROUP - 1) // GROUP
        first = lax.rem(quarter + s, 4)
        at_k = pl.multiple_of(at_k, GROUP)
        at_q = pl.multiple_of(at_q, GROUP)
        dq_out[s] = oc[pl.ds(at_q, part_rows), :DH]
        o_out[s] = oc[pl.ds(at_q, part_rows), DH:]
        k_out[s, :, :DH] = (dkc[pl.ds(at_k, slots), :] * score_scale).astype(jnp.bfloat16)
        k_out[s, :, DH:] = dvc[pl.ds(at_k, slots), :].astype(jnp.bfloat16)
        return at_k + live * GROUP, at_q + (live - first + 3) // 4 * GROUP

    lax.fori_loop(0, shards, unpack, (jnp.int32(0), jnp.int32(0)))


def attend(counts, quarter, query_in, key_in):
    shards, part_rows, _ = query_in.shape
    slots = key_in.shape[1]
    keys = shards * slots
    queries = shards * part_rows
    rounded = (counts + GROUP - 1) // GROUP * GROUP
    start = jnp.cumsum(rounded) - rounded
    place = jnp.arange(keys, dtype=jnp.int32)[None, :]
    live = jnp.any(
        (place >= start[:, None]) & (place < (start + counts)[:, None]), axis=0, keepdims=True
    )
    bias = jnp.where(live, 0.0, NEG).astype(jnp.float32)
    vmem = pl.BlockSpec(memory_space=pltpu.VMEM)
    smem = pl.BlockSpec(memory_space=pltpu.SMEM)
    return pl.pallas_call(
        attend_kernel,
        out_shape=(
            jax.ShapeDtypeStruct((shards, part_rows, DH), jnp.bfloat16),
            jax.ShapeDtypeStruct((shards, part_rows, DH), jnp.bfloat16),
            jax.ShapeDtypeStruct(key_in.shape, jnp.bfloat16),
        ),
        in_specs=[smem, smem, vmem, vmem, vmem],
        out_specs=(vmem, vmem, vmem),
        scratch_shapes=[
            pltpu.VMEM((queries + BQ, DH), jnp.bfloat16),
            pltpu.VMEM((queries + BQ, DH), jnp.bfloat16),
            pltpu.VMEM((keys + BK, DH), jnp.bfloat16),
            pltpu.VMEM((keys + BK, DH), jnp.bfloat16),
            pltpu.VMEM((keys, DH), jnp.float32),
            pltpu.VMEM((keys, DH), jnp.float32),
            pltpu.VMEM((queries + BQ, 2 * DH), jnp.bfloat16),
            pltpu.VMEM((BQ, keys), jnp.float32),
            pltpu.VMEM((queries + BQ, DH), jnp.int32),
            pltpu.VMEM((BQ, DH), jnp.float32),
            pltpu.VMEM((BQ, DH), jnp.float32),
            pltpu.VMEM((BQ, DH), jnp.float32),
            pltpu.SMEM((queries // GROUP + 8,), jnp.int32),
        ],
        compiler_params=pltpu.CompilerParams(vmem_limit_bytes=48 * 1024 * 1024),
        cost_estimate=pl.CostEstimate(
            flops=6 * queries * keys * DH, bytes_accessed=16 * 1024 * 1024, transcendentals=0
        ),
        name="attend",
    )(counts, quarter, query_in, key_in, bias)


def block_bytes_wait(ref, sem):
    pltpu.make_async_copy(ref, ref, sem).wait()


def greet(peers, peer_of):
    barrier = pltpu.get_barrier_semaphore()

    def signal(k, carry):
        pl.semaphore_signal(
            barrier, inc=1, device_id={"seq": peer_of(k)}, device_id_type=pl.DeviceIdType.MESH
        )
        return carry

    lax.fori_loop(1, peers + 1, signal, 0)
    pl.semaphore_wait(barrier, peers)


def send(src, dst, send_sem, recv_sem, target):
    copy = pltpu.make_async_remote_copy(
        src_ref=src,
        dst_ref=dst,
        send_sem=send_sem,
        recv_sem=recv_sem,
        device_id={"seq": target},
        device_id_type=pl.DeviceIdType.MESH,
    )
    copy.start()
    return copy


def home_kernel(
    o_ref,
    dq_ref,
    k_ref,
    g0_ref,
    g1_ref,
    g2_ref,
    g3_ref,
    dq_home,
    gk_home,
    gv_home,
    wg_out,
    oz,
    kx,
    ks,
    kin,
    part,
    px,
    rs,
    rin,
    send_sem,
    recv_sem,
):
    shards, part_rows, _ = o_ref.shape
    slots = k_ref.shape[1]
    me = lax.axis_index("seq")
    core = me % 2
    sibling = me + 1 - 2 * core
    chip = me // 2
    chips = shards // 2
    head = me // 4
    quarter = me % 4
    plane_x = chip % 4
    out_rows = wg_out.shape[0]
    my_rows = pl.ds(pl.multiple_of(quarter * part_rows, GROUP), part_rows)
    my_cols = pl.ds(pl.multiple_of(head * DH, DH), DH)

    greet(shards - 1, lambda k: lax.rem(me + k, shards))

    def send_o(k, carry):
        t = lax.rem(me + k, shards)
        send(o_ref.at[t], oz.at[0, my_rows, my_cols], send_sem.at[0], recv_sem.at[0], t)
        return carry

    lax.fori_loop(1, shards, send_o, 0)
    swap = send(k_ref.at[:, 1 - core], kx, send_sem.at[1], recv_sem.at[1], sibling)
    oz[0, my_rows, my_cols] = o_ref[me]
    dq_home[my_rows, my_cols] = dq_ref[me]
    block_bytes_wait(o_ref.at[pl.ds(0, shards - 1)], recv_sem.at[0])

    along_z = [
        send(oz.at[0], oz.at[k], send_sem.at[1 + k], recv_sem.at[1 + k], lax.rem(me + 8 * k, shards))
        for k in (1, 2, 3)
    ]
    swap.wait()

    def send_k(k, carry):
        t = lax.rem(chip + k, chips)
        ks[t] = (k_ref[t, core].astype(jnp.float32) + kx[t].astype(jnp.float32)).astype(
            jnp.bfloat16
        )
        send(ks.at[t], kin.at[chip], send_sem.at[5], recv_sem.at[5], 2 * t + core)
        return carry

    lax.fori_loop(1, chips, send_k, 0)
    kin[chip] = (k_ref[chip, core].astype(jnp.float32) + kx[chip].astype(jnp.float32)).astype(
        jnp.bfloat16
    )
    for copy in along_z:
        copy.wait()

    width = 256

    def multiply(j, carry):
        cols = pl.ds(pl.multiple_of(j * width, width), width)
        total = contract_rows(g0_ref[:, cols], oz[0])
        total += contract_rows(g1_ref[:, cols], oz[1])
        total += contract_rows(g2_ref[:, cols], oz[2])
        total += contract_rows(g3_ref[:, cols], oz[3])
        part[cols, :] = total.astype(jnp.bfloat16)
        return carry

    lax.fori_loop(0, part.shape[0] // width, multiply, 0)

    def piece(x, c):
        return pl.ds(pl.multiple_of((2 * x + c) * out_rows, 32), out_rows)

    swaps = [
        send(part.at[piece(x, 1 - core)], px.at[x], send_sem.at[6 + x], recv_sem.at[6 + x], sibling)
        for x in range(4)
    ]

    def send_dq(k, carry):
        t = lax.rem(me + k, shards)
        send(dq_ref.at[t], dq_home.at[my_rows, my_cols], send_sem.at[10], recv_sem.at[10], t)
        return carry

    for copy in swaps:
        copy.wait()

    def pair_sum(x):
        return part[piece(x, core), :].astype(jnp.float32) + px[x].astype(jnp.float32)

    along_x = []
    for k in (1, 2, 3):
        x = lax.rem(plane_x + k, 4)
        rs[k - 1] = pair_sum(x).astype(jnp.bfloat16)
        along_x.append(
            send(
                rs.at[k - 1],
                rin.at[k - 1],
                send_sem.at[10 + k],
                recv_sem.at[10 + k],
                me + 2 * (x - plane_x),
            )
        )
    lax.fori_loop(1, shards, send_dq, 0)
    wg_out[...] = pair_sum(plane_x)

    block_bytes_wait(kin.at[pl.ds(0, chips - 1)], recv_sem.at[5])
    for h in range(chips // 2):
        pair = kin[2 * h].astype(jnp.float32) + kin[2 * h + 1].astype(jnp.float32)
        pair = pair.astype(jnp.bfloat16)
        gk_home[:, h * DH : (h + 1) * DH] = pair[:, :DH]
        gv_home[:, h * DH : (h + 1) * DH] = pair[:, DH:]
    for copy in along_x:
        copy.wait()
    wg_out[...] += (
        rin[0].astype(jnp.float32) + rin[1].astype(jnp.float32) + rin[2].astype(jnp.float32)
    )
    block_bytes_wait(dq_ref.at[pl.ds(0, shards - 1)], recv_sem.at[10])
    block_bytes_wait(o_ref.at[pl.ds(0, shards - 1)], send_sem.at[0])
    block_bytes_wait(ks.at[pl.ds(0, chips - 1)], send_sem.at[5])
    block_bytes_wait(dq_ref.at[pl.ds(0, shards - 1)], send_sem.at[10])


def bring_home(o_back, dq_back, key_back, grad_parts, out_rows):
    shards, part_rows, _ = o_back.shape
    slots = key_back.shape[1]
    chips = shards // 2
    width = shards // 4 * DH
    rows = grad_parts[0].shape[1]
    key_back = key_back.reshape(chips, 2, slots, 2 * DH)
    vmem = pl.BlockSpec(memory_space=pltpu.VMEM)
    bf16 = jnp.bfloat16
    return pl.pallas_call(
        home_kernel,
        out_shape=(
            jax.ShapeDtypeStruct((slots, width), bf16),
            jax.ShapeDtypeStruct((slots, width), bf16),
            jax.ShapeDtypeStruct((slots, width), bf16),
            jax.ShapeDtypeStruct((out_rows, width), jnp.float32),
        ),
        in_specs=[vmem] * 7,
        out_specs=(vmem,) * 4,
        scratch_shapes=[
            pltpu.VMEM((4, slots, width), bf16),
            pltpu.VMEM((chips, slots, 2 * DH), bf16),
            pltpu.VMEM((chips, slots, 2 * DH), bf16),
            pltpu.VMEM((chips, slots, 2 * DH), bf16),
            pltpu.VMEM((rows, width), bf16),
            pltpu.VMEM((4, out_rows, width), bf16),
            pltpu.VMEM((3, out_rows, width), bf16),
            pltpu.VMEM((3, out_rows, width), bf16),
            pltpu.SemaphoreType.DMA((14,)),
            pltpu.SemaphoreType.DMA((14,)),
        ],
        compiler_params=pltpu.CompilerParams(
            collective_id=1, has_side_effects=True, vmem_limit_bytes=48 * 1024 * 1024
        ),
        name="home",
    )(o_back, dq_back, key_back, *grad_parts)


def on_device(
    projections,
    output_gradient,
    output_projection_weight,
    kept_token_indices,
    surviving_token_count,
):
    tok_dev = projections.shape[0]
    group_width = projections.shape[2]
    slots = kept_token_indices.shape[1]
    heads_local = group_width // DH
    seq_count = lax.axis_size("seq")
    quarters = seq_count // heads_local
    part_rows = slots // quarters
    me = lax.axis_index("seq")
    my_quarter = (me % quarters).astype(jnp.int32)[None]

    kept = kept_token_indices[0]
    dealt = kept.reshape(part_rows // GROUP, quarters, GROUP).transpose(1, 0, 2)
    dealt = lax.dynamic_slice_in_dim(
        jnp.concatenate([dealt, dealt], axis=0), me % quarters, quarters, axis=0
    ).reshape(slots)
    token = jnp.arange(tok_dev, dtype=jnp.int32)[None, :]
    selector = (kept[:, None] == token).astype(jnp.bfloat16)
    dealt_selector = (dealt[:, None] == token).astype(jnp.bfloat16)

    def pick(which, values):
        return jnp.dot(which, values, preferred_element_type=jnp.float32).astype(jnp.bfloat16)

    grad_local = pick(dealt_selector, output_gradient)
    grad_rows = lax.all_gather(grad_local, "head", axis=1, tiled=True)
    query = pick(dealt_selector, projections[:, 0])
    key = pick(selector, projections[:, 1])
    value = pick(selector, projections[:, 2])

    def head_major(matrix):
        return matrix.reshape(slots, heads_local, DH).transpose(1, 0, 2)

    key_side = jnp.concatenate([head_major(key), head_major(value)], axis=2)
    key_side = jnp.broadcast_to(key_side[:, None], (heads_local, quarters, slots, 2 * DH))
    key_side = key_side.reshape(seq_count, slots, 2 * DH)
    key_in = lax.all_to_all(key_side, "seq", split_axis=0, concat_axis=0, tiled=True)
    grad_attn = jnp.dot(
        grad_rows, output_projection_weight, preferred_element_type=jnp.float32
    ).astype(jnp.bfloat16)
    query_side = jnp.concatenate([head_major(query), head_major(grad_attn)], axis=2)
    query_side = query_side.reshape(seq_count, part_rows, 2 * DH)
    query_in = lax.all_to_all(query_side, "seq", split_axis=0, concat_axis=0, tiled=True)

    blocks = grad_rows.reshape(slots, 4, -1)
    my_z = me // 8

    def along_z(k):
        block = lax.dynamic_index_in_dim(blocks, (my_z + k) % 4, axis=1, keepdims=False)
        if k == 0:
            return block
        return lax.ppermute(
            block, "seq", [(i, (i + 8 * k) % seq_count) for i in range(seq_count)]
        )

    grad_parts = [along_z(k) for k in range(4)]
    dq_back, o_back, key_back = attend(
        surviving_token_count, my_quarter, query_in, key_in
    )
    out_rows = output_projection_weight.shape[0] // seq_count
    grad_query, grad_key, grad_value, weight_grad = bring_home(
        o_back, dq_back, key_back, grad_parts, out_rows
    )
    projection_grad = jnp.stack(
        [
            contract_rows(dealt_selector, grad_query).astype(jnp.bfloat16),
            contract_rows(selector, grad_key).astype(jnp.bfloat16),
            contract_rows(selector, grad_value).astype(jnp.bfloat16),
        ],
        axis=1,
    )
    return (projection_grad, weight_grad)


def solution(mesh):
    return jax.shard_map(
        on_device,
        mesh=mesh,
        in_specs=(P("seq", None, "head"), P("seq", "head"), P(None, "head"), P("seq", None), P()),
        out_specs=(P("seq", None, "head"), P("seq", "head")),
        check_vma=False,
    )
```

```python
import math

import jax
import jax.numpy as jnp
from jax import lax
from jax.experimental import pallas as pl
from jax.experimental.pallas import tpu as pltpu
from jax.sharding import PartitionSpec as P

DH = 128
BQ = 256
BK = 512
GROUP = 16
NEG = -1e30


def contract_rows(left, right):
    return lax.dot_general(
        left, right, (((0,), (0,)), ((), ())), preferred_element_type=jnp.float32
    )


def contract_cols(left, right):
    return lax.dot_general(
        left, right, (((1,), (1,)), ((), ())), preferred_element_type=jnp.float32
    )


def wide(column, width):
    return jnp.concatenate([column] * (width // DH), axis=1)


def attend_kernel(
    count_ref,
    quarter_ref,
    q_ref,
    g_ref,
    k_ref,
    v_ref,
    bias_ref,
    dq_out,
    o_out,
    k_out,
    qc,
    gc,
    kc,
    vc,
    dkc,
    dvc,
    oc,
    s_scr,
    qpos,
    peak,
    total,
    acc,
    group_pos,
):
    shards, part_rows, _ = q_ref.shape
    slots = k_ref.shape[1]
    quarter = quarter_ref[0]
    groups = part_rows // GROUP
    score_scale = 1.0 / math.sqrt(DH)
    log2e = score_scale * math.log2(math.e)

    def pack(s, carry):
        at_k, at_q = carry
        live = (count_ref[s] + GROUP - 1) // GROUP
        first = lax.rem(quarter + s, 4)
        at_k = pl.multiple_of(at_k, GROUP)
        at_q = pl.multiple_of(at_q, GROUP)
        kc[pl.ds(at_k, slots), :] = k_ref[s]
        vc[pl.ds(at_k, slots), :] = v_ref[s]
        qc[pl.ds(at_q, part_rows), :] = q_ref[s]
        gc[pl.ds(at_q, part_rows), :] = g_ref[s]
        rows = lax.broadcasted_iota(jnp.int32, (GROUP, DH), 0)
        for i in range(groups):
            base = at_k + (first + 4 * i) * GROUP
            qpos[pl.ds(at_q + i * GROUP, GROUP), :] = base + rows
            group_pos[at_q // GROUP + i] = base
        return at_k + live * GROUP, at_q + (live - first + 3) // 4 * GROUP

    end_k, end_q = lax.fori_loop(0, shards, pack, (jnp.int32(0), jnp.int32(0)))
    end_k = pl.multiple_of(end_k, GROUP)
    end_q = pl.multiple_of(end_q, GROUP)
    kc[pl.ds(end_k, BK), :] = jnp.zeros((BK, DH), jnp.bfloat16)
    vc[pl.ds(end_k, BK), :] = jnp.zeros((BK, DH), jnp.bfloat16)
    qc[pl.ds(end_q, BQ), :] = jnp.zeros((BQ, DH), jnp.bfloat16)
    gc[pl.ds(end_q, BQ), :] = jnp.zeros((BQ, DH), jnp.bfloat16)
    qpos[pl.ds(end_q, BQ), :] = jnp.zeros((BQ, DH), jnp.int32)
    blocks = (end_q + BQ - 1) // BQ
    oc[pl.ds(pl.multiple_of(blocks * BQ, BQ), part_rows), :] = jnp.zeros(
        (part_rows, 2 * DH), jnp.bfloat16
    )

    def clear(i, carry):
        rows = pl.ds(pl.multiple_of(i * slots, slots), slots)
        dkc[rows, :] = jnp.zeros((slots, DH), jnp.float32)
        dvc[rows, :] = jnp.zeros((slots, DH), jnp.float32)
        return carry

    lax.fori_loop(0, shards, clear, 0)

    def block(b, carry):
        rows = pl.ds(pl.multiple_of(b * BQ, BQ), BQ)
        last_group = jnp.minimum((b + 1) * (BQ // GROUP), end_q // GROUP) - 1
        chunks = (group_pos[last_group] + GROUP + BK - 1) // BK
        clear_chunks = (group_pos[b * (BQ // GROUP)] + 1) // BK

        def score(c, masked):
            at = pl.multiple_of(c * BK, BK)
            keys = pl.ds(at, BK)
            s = contract_cols(qc[rows, :], kc[keys, :]) + bias_ref[:, keys]
            if masked:
                column = at + lax.broadcasted_iota(jnp.int32, (BQ, BK), 1)
                s = jnp.where(column <= wide(qpos[rows, :], BK), s, NEG)
            s_scr[:, keys] = s
            top = peak[...]
            for i in range(BK // DH):
                top = jnp.maximum(top, s[:, i * DH : (i + 1) * DH])
            peak[...] = top

        peak[...] = jnp.full((BQ, DH), NEG, jnp.float32)

        def score_clear(c, carry):
            score(c, False)
            return carry

        def score_masked(c, carry):
            score(c, True)
            return carry

        lax.fori_loop(0, clear_chunks, score_clear, 0)
        lax.fori_loop(clear_chunks, chunks, score_masked, 0)
        peak[...] = jnp.broadcast_to(jnp.max(peak[...], axis=1, keepdims=True), (BQ, DH))
        total[...] = jnp.zeros((BQ, DH), jnp.float32)
        acc[...] = jnp.zeros((BQ, DH), jnp.float32)

        def weigh(c, carry):
            keys = pl.ds(pl.multiple_of(c * BK, BK), BK)
            p = jnp.exp2((s_scr[:, keys] - wide(peak[...], BK)) * log2e)
            s_scr[:, keys] = p
            add = total[...]
            for i in range(BK // DH):
                add = add + p[:, i * DH : (i + 1) * DH]
            total[...] = add
            acc[...] += jnp.dot(
                p.astype(jnp.bfloat16), vc[keys, :], preferred_element_type=jnp.float32
            )
            return carry

        lax.fori_loop(0, chunks, weigh, 0)
        inverse = 1.0 / jnp.broadcast_to(
            jnp.sum(total[...], axis=1, keepdims=True), (BQ, DH)
        )
        total[...] = inverse
        attended = acc[...] * inverse
        oc[rows, DH:] = attended.astype(jnp.bfloat16)
        peak[...] = jnp.broadcast_to(
            jnp.sum(gc[rows, :].astype(jnp.float32) * attended, axis=1, keepdims=True), (BQ, DH)
        )
        acc[...] = jnp.zeros((BQ, DH), jnp.float32)

        def back(c, carry):
            keys = pl.ds(pl.multiple_of(c * BK, BK), BK)
            p = s_scr[:, keys] * wide(total[...], BK)
            grad_probs = contract_cols(gc[rows, :], vc[keys, :])
            ds = (p * (grad_probs - wide(peak[...], BK))).astype(jnp.bfloat16)
            acc[...] += jnp.dot(ds, kc[keys, :], preferred_element_type=jnp.float32)
            dkc[keys, :] += contract_rows(ds, qc[rows, :])
            dvc[keys, :] += contract_rows(p.astype(jnp.bfloat16), gc[rows, :])
            return carry

        lax.fori_loop(0, chunks, back, 0)
        oc[rows, :DH] = (acc[...] * score_scale).astype(jnp.bfloat16)
        return carry

    lax.fori_loop(0, blocks, block, 0)

    def unpack(s, carry):
        at_k, at_q = carry
        live = (count_ref[s] + GROUP - 1) // GROUP
        first = lax.rem(quarter + s, 4)
        at_k = pl.multiple_of(at_k, GROUP)
        at_q = pl.multiple_of(at_q, GROUP)
        dq_out[s] = oc[pl.ds(at_q, part_rows), :DH]
        o_out[s] = oc[pl.ds(at_q, part_rows), DH:]
        k_out[s, :, :DH] = (dkc[pl.ds(at_k, slots), :] * score_scale).astype(jnp.bfloat16)
        k_out[s, :, DH:] = dvc[pl.ds(at_k, slots), :].astype(jnp.bfloat16)
        return at_k + live * GROUP, at_q + (live - first + 3) // 4 * GROUP

    lax.fori_loop(0, shards, unpack, (jnp.int32(0), jnp.int32(0)))


def attend(counts, quarter, query_in, grad_in, key_in, value_in):
    shards, part_rows, _ = query_in.shape
    slots = key_in.shape[1]
    keys = shards * slots
    queries = shards * part_rows
    rounded = (counts + GROUP - 1) // GROUP * GROUP
    start = jnp.cumsum(rounded) - rounded
    place = jnp.arange(keys, dtype=jnp.int32)[None, :]
    live = jnp.any(
        (place >= start[:, None]) & (place < (start + counts)[:, None]), axis=0, keepdims=True
    )
    bias = jnp.where(live, 0.0, NEG).astype(jnp.float32)
    vmem = pl.BlockSpec(memory_space=pltpu.VMEM)
    smem = pl.BlockSpec(memory_space=pltpu.SMEM)
    return pl.pallas_call(
        attend_kernel,
        out_shape=(
            jax.ShapeDtypeStruct((shards, part_rows, DH), jnp.bfloat16),
            jax.ShapeDtypeStruct((shards, part_rows, DH), jnp.bfloat16),
            jax.ShapeDtypeStruct((shards, slots, 2 * DH), jnp.bfloat16),
        ),
        in_specs=[smem, smem, vmem, vmem, vmem, vmem, vmem],
        out_specs=(vmem, vmem, vmem),
        scratch_shapes=[
            pltpu.VMEM((queries + BQ, DH), jnp.bfloat16),
            pltpu.VMEM((queries + BQ, DH), jnp.bfloat16),
            pltpu.VMEM((keys + BK, DH), jnp.bfloat16),
            pltpu.VMEM((keys + BK, DH), jnp.bfloat16),
            pltpu.VMEM((keys, DH), jnp.float32),
            pltpu.VMEM((keys, DH), jnp.float32),
            pltpu.VMEM((queries + BQ, 2 * DH), jnp.bfloat16),
            pltpu.VMEM((BQ, keys), jnp.float32),
            pltpu.VMEM((queries + BQ, DH), jnp.int32),
            pltpu.VMEM((BQ, DH), jnp.float32),
            pltpu.VMEM((BQ, DH), jnp.float32),
            pltpu.VMEM((BQ, DH), jnp.float32),
            pltpu.SMEM((queries // GROUP + 8,), jnp.int32),
        ],
        compiler_params=pltpu.CompilerParams(vmem_limit_bytes=48 * 1024 * 1024),
        cost_estimate=pl.CostEstimate(
            flops=6 * queries * keys * DH, bytes_accessed=16 * 1024 * 1024, transcendentals=0
        ),
        name="attend",
    )(counts, quarter, query_in, grad_in, key_in, value_in, bias)


def block_bytes_wait(ref, sem):
    pltpu.make_async_copy(ref, ref, sem).wait()


def greet(peers, peer_of, ring=0):
    barrier = pltpu.get_barrier_semaphore()

    def signal(k, carry):
        pl.semaphore_signal(
            barrier, inc=1, device_id={"seq": peer_of(k)}, device_id_type=pl.DeviceIdType.MESH
        )
        return carry

    lax.fori_loop(1, peers + 1, signal, 0)
    if ring:
        row = lax.axis_index("head")
        for k in range(1, ring):
            pl.semaphore_signal(
                barrier,
                inc=1,
                device_id={"head": lax.rem(row + k, ring)},
                device_id_type=pl.DeviceIdType.MESH,
            )
        peers = peers + ring - 1
    pl.semaphore_wait(barrier, peers)


def send(src, dst, send_sem, recv_sem, target, axis="seq"):
    copy = pltpu.make_async_remote_copy(
        src_ref=src,
        dst_ref=dst,
        send_sem=send_sem,
        recv_sem=recv_sem,
        device_id={axis: target},
        device_id_type=pl.DeviceIdType.MESH,
    )
    copy.start()
    return copy


def spread_kernel(
    grad_ref,
    q_ref,
    k_ref,
    v_ref,
    w_hbm,
    gblk,
    q_in,
    g_in,
    k_in,
    v_in,
    w_ref,
    acc,
    g_local,
    w_sem,
    y_send,
    y_recv,
    kv_send,
    kv_recv,
    pass_send,
    pass_recv,
    q_send,
    q_recv,
):
    shards, part_rows, _ = q_in.shape
    slots, cols = grad_ref.shape
    half = cols // 2
    me = lax.axis_index("seq")
    row = lax.axis_index("head")
    core = me % 2
    sibling = me + 1 - 2 * core
    chip = me // 2
    chips = shards // 2
    my_z = me // 8
    my_head = me // 4
    my_rows = pl.ds(pl.multiple_of((me % 4) * part_rows, GROUP), part_rows)

    load_w = pltpu.make_async_copy(w_hbm, w_ref, w_sem)
    load_w.start()
    greet(shards - 1, lambda k: lax.rem(me + k, shards), 4)

    def head_cols(head):
        return pl.ds(pl.multiple_of(head * DH, DH), DH)

    def slot_of(y):
        return lax.rem(y - my_z + 4, 4)

    right, left, across = lax.rem(row + 1, 4), lax.rem(row + 3, 4), lax.rem(row + 2, 4)
    to_right = send(grad_ref, gblk.at[slot_of(row)], y_send.at[0], y_recv.at[0], right, "head")
    to_left = send(grad_ref, gblk.at[slot_of(row)], y_send.at[1], y_recv.at[1], left, "head")

    def send_kv(k, carry):
        t = lax.rem(chip + k, chips)
        source = head_cols(t // 2)
        target = 2 * t + core
        send(k_ref.at[:, source], k_in.at[me], kv_send.at[0], kv_recv.at[k], target)
        send(v_ref.at[:, source], v_in.at[me], kv_send.at[1], kv_recv.at[chips + k], target)
        return carry

    lax.fori_loop(1, chips, send_kv, 0)
    own = head_cols(my_head)
    send(k_ref.at[:, own], k_in.at[me], pass_send.at[0], pass_recv.at[0], sibling)
    send(v_ref.at[:, own], v_in.at[me], pass_send.at[1], pass_recv.at[1], sibling)
    k_in[me] = k_ref[:, own]
    v_in[me] = v_ref[:, own]

    def send_q(k, carry):
        t = lax.rem(me + k, shards)
        rows = pl.ds(pl.multiple_of((t % 4) * part_rows, GROUP), part_rows)
        send(q_ref.at[rows, head_cols(t // 4)], q_in.at[me], q_send.at[0], q_recv.at[0], t)
        return carry

    lax.fori_loop(1, shards, send_q, 0)
    q_in[me] = q_ref[my_rows, own]

    width = 256
    tiles = acc.shape[1] // width
    gblk[slot_of(row)] = grad_ref[...]
    load_w.wait()

    def multiply(y, first):
        def tile(j, carry):
            at = pl.ds(pl.multiple_of(j * width, width), width)
            rows = pl.ds(pl.multiple_of(y * cols, width), cols)
            part = jnp.dot(gblk[slot_of(y)], w_ref[rows, at], preferred_element_type=jnp.float32)
            acc[:, at] = part if first else acc[:, at] + part
            return carry

        lax.fori_loop(0, tiles, tile, 0)

    multiply(row, True)
    to_right.wait_recv()
    from_left = gblk.at[slot_of(left), :, pl.ds(0, half)]
    on_right = send(from_left, from_left, y_send.at[2], y_recv.at[2], right, "head")
    to_left.wait_recv()
    from_right = gblk.at[slot_of(right), :, pl.ds(half, half)]
    on_left = send(from_right, from_right, y_send.at[3], y_recv.at[3], left, "head")
    multiply(left, False)
    multiply(right, False)

    def pass_on(k, carry):
        s = 2 * lax.rem(chip - k + chips, chips) + core
        block_bytes_wait(k_in.at[s], kv_recv.at[k])
        send(k_in.at[s], k_in.at[s], pass_send.at[0], pass_recv.at[0], sibling)
        block_bytes_wait(v_in.at[s], kv_recv.at[chips + k])
        send(v_in.at[s], v_in.at[s], pass_send.at[1], pass_recv.at[1], sibling)
        return carry

    lax.fori_loop(1, chips, pass_on, 0)
    on_right.wait_recv()
    on_left.wait_recv()

    def finish(step, carry):
        j = lax.rem(my_head // 2 + step, tiles)
        at = pl.ds(pl.multiple_of(j * width, width), width)
        rows = pl.ds(pl.multiple_of(across * cols, width), cols)
        part = jnp.dot(gblk[slot_of(across)], w_ref[rows, at], preferred_element_type=jnp.float32)
        g_local[:, at] = (acc[:, at] + part).astype(jnp.bfloat16)
        for i in range(8):
            t = j * 8 + i
            part_at = (i % 4) * part_rows

            @pl.when(t != me)
            def _():
                send(
                    g_local.at[pl.ds(part_at, part_rows), head_cols(t // 4)],
                    g_in.at[me],
                    q_send.at[1],
                    q_recv.at[1],
                    t,
                )

        return carry

    lax.fori_loop(0, tiles, finish, 0)
    g_in[me] = g_local[my_rows, own]

    others = pl.ds(0, shards - 1)
    block_bytes_wait(q_in.at[others], q_recv.at[0])
    block_bytes_wait(q_in.at[others], q_send.at[0])
    passed = pl.ds(0, chips)
    block_bytes_wait(k_in.at[passed], pass_recv.at[0])
    block_bytes_wait(v_in.at[passed], pass_recv.at[1])
    block_bytes_wait(k_in.at[passed], pass_send.at[0])
    block_bytes_wait(v_in.at[passed], pass_send.at[1])
    sent = pl.ds(0, chips - 1)
    block_bytes_wait(k_in.at[sent], kv_send.at[0])
    block_bytes_wait(v_in.at[sent], kv_send.at[1])
    for copy in (to_right, to_left, on_right, on_left):
        copy.wait_send()
    block_bytes_wait(g_in.at[others], q_recv.at[1])
    block_bytes_wait(g_in.at[others], q_send.at[1])


def spread(grad_local, query, key, value, weight, shards):
    slots, cols = grad_local.shape
    depth, width = weight.shape
    part_rows = slots // 4
    bf16 = jnp.bfloat16
    vmem = pl.BlockSpec(memory_space=pltpu.VMEM)
    return pl.pallas_call(
        spread_kernel,
        out_shape=(
            jax.ShapeDtypeStruct((4, slots, cols), bf16),
            jax.ShapeDtypeStruct((shards, part_rows, DH), bf16),
            jax.ShapeDtypeStruct((shards, part_rows, DH), bf16),
            jax.ShapeDtypeStruct((shards, slots, DH), bf16),
            jax.ShapeDtypeStruct((shards, slots, DH), bf16),
        ),
        in_specs=[vmem] * 4 + [pl.BlockSpec(memory_space=pl.ANY)],
        out_specs=(vmem,) * 5,
        scratch_shapes=[
            pltpu.VMEM((depth, width), bf16),
            pltpu.VMEM((slots, width), jnp.float32),
            pltpu.VMEM((slots, width), bf16),
            pltpu.SemaphoreType.DMA,
            pltpu.SemaphoreType.DMA((4,)),
            pltpu.SemaphoreType.DMA((4,)),
            pltpu.SemaphoreType.DMA((2,)),
            pltpu.SemaphoreType.DMA((shards,)),
            pltpu.SemaphoreType.DMA((2,)),
            pltpu.SemaphoreType.DMA((2,)),
            pltpu.SemaphoreType.DMA((2,)),
            pltpu.SemaphoreType.DMA((2,)),
        ],
        compiler_params=pltpu.CompilerParams(
            collective_id=2, has_side_effects=True, vmem_limit_bytes=48 * 1024 * 1024
        ),
        name="spread",
    )(grad_local, query, key, value, weight)


def home_kernel(
    o_ref,
    dq_ref,
    k_ref,
    g0_ref,
    g1_ref,
    g2_ref,
    g3_ref,
    dq_home,
    gk_home,
    gv_home,
    wg_out,
    oz,
    kx,
    ks,
    kin,
    part,
    px,
    rs,
    rin,
    send_sem,
    recv_sem,
):
    shards, part_rows, _ = o_ref.shape
    slots = k_ref.shape[1]
    me = lax.axis_index("seq")
    core = me % 2
    sibling = me + 1 - 2 * core
    chip = me // 2
    chips = shards // 2
    head = me // 4
    quarter = me % 4
    plane_x = chip % 4
    out_rows = wg_out.shape[0]
    my_rows = pl.ds(pl.multiple_of(quarter * part_rows, GROUP), part_rows)
    my_cols = pl.ds(pl.multiple_of(head * DH, DH), DH)

    greet(shards - 1, lambda k: lax.rem(me + k, shards))

    def send_o(k, carry):
        t = lax.rem(me + k, shards)
        send(o_ref.at[t], oz.at[0, my_rows, my_cols], send_sem.at[0], recv_sem.at[0], t)
        return carry

    lax.fori_loop(1, shards, send_o, 0)
    swap = send(k_ref.at[:, 1 - core], kx, send_sem.at[1], recv_sem.at[1], sibling)
    oz[0, my_rows, my_cols] = o_ref[me]
    dq_home[my_rows, my_cols] = dq_ref[me]
    block_bytes_wait(o_ref.at[pl.ds(0, shards - 1)], recv_sem.at[0])

    along_z = [
        send(oz.at[0], oz.at[k], send_sem.at[1 + k], recv_sem.at[1 + k], lax.rem(me + 8 * k, shards))
        for k in (1, 2, 3)
    ]
    swap.wait()

    def send_k(k, carry):
        t = lax.rem(chip + k, chips)
        ks[t] = (k_ref[t, core].astype(jnp.float32) + kx[t].astype(jnp.float32)).astype(
            jnp.bfloat16
        )
        send(ks.at[t], kin.at[chip], send_sem.at[5], recv_sem.at[5], 2 * t + core)
        return carry

    lax.fori_loop(1, chips, send_k, 0)
    kin[chip] = (k_ref[chip, core].astype(jnp.float32) + kx[chip].astype(jnp.float32)).astype(
        jnp.bfloat16
    )
    for copy in along_z:
        copy.wait()

    width = 256

    def multiply(j, carry):
        cols = pl.ds(pl.multiple_of(j * width, width), width)
        total = contract_rows(g0_ref[:, cols], oz[0])
        total += contract_rows(g1_ref[:, cols], oz[1])
        total += contract_rows(g2_ref[:, cols], oz[2])
        total += contract_rows(g3_ref[:, cols], oz[3])
        part[cols, :] = total.astype(jnp.bfloat16)
        return carry

    lax.fori_loop(0, part.shape[0] // width, multiply, 0)

    def piece(x, c):
        return pl.ds(pl.multiple_of((2 * x + c) * out_rows, 32), out_rows)

    swaps = [
        send(part.at[piece(x, 1 - core)], px.at[x], send_sem.at[6 + x], recv_sem.at[6 + x], sibling)
        for x in range(4)
    ]

    def send_dq(k, carry):
        t = lax.rem(me + k, shards)
        send(dq_ref.at[t], dq_home.at[my_rows, my_cols], send_sem.at[10], recv_sem.at[10], t)
        return carry

    for copy in swaps:
        copy.wait()

    def pair_sum(x):
        return part[piece(x, core), :].astype(jnp.float32) + px[x].astype(jnp.float32)

    along_x = []
    for k in (1, 2, 3):
        x = lax.rem(plane_x + k, 4)
        rs[k - 1] = pair_sum(x).astype(jnp.bfloat16)
        along_x.append(
            send(
                rs.at[k - 1],
                rin.at[k - 1],
                send_sem.at[10 + k],
                recv_sem.at[10 + k],
                me + 2 * (x - plane_x),
            )
        )
    lax.fori_loop(1, shards, send_dq, 0)
    wg_out[...] = pair_sum(plane_x)

    block_bytes_wait(kin.at[pl.ds(0, chips - 1)], recv_sem.at[5])
    for h in range(chips // 2):
        pair = kin[2 * h].astype(jnp.float32) + kin[2 * h + 1].astype(jnp.float32)
        pair = pair.astype(jnp.bfloat16)
        gk_home[:, h * DH : (h + 1) * DH] = pair[:, :DH]
        gv_home[:, h * DH : (h + 1) * DH] = pair[:, DH:]
    for copy in along_x:
        copy.wait()
    wg_out[...] += (
        rin[0].astype(jnp.float32) + rin[1].astype(jnp.float32) + rin[2].astype(jnp.float32)
    )
    block_bytes_wait(dq_ref.at[pl.ds(0, shards - 1)], recv_sem.at[10])
    block_bytes_wait(o_ref.at[pl.ds(0, shards - 1)], send_sem.at[0])
    block_bytes_wait(ks.at[pl.ds(0, chips - 1)], send_sem.at[5])
    block_bytes_wait(dq_ref.at[pl.ds(0, shards - 1)], send_sem.at[10])


def bring_home(o_back, dq_back, key_back, grad_parts, out_rows):
    shards, part_rows, _ = o_back.shape
    slots = key_back.shape[1]
    chips = shards // 2
    width = shards // 4 * DH
    rows = grad_parts[0].shape[1]
    key_back = key_back.reshape(chips, 2, slots, 2 * DH)
    vmem = pl.BlockSpec(memory_space=pltpu.VMEM)
    bf16 = jnp.bfloat16
    return pl.pallas_call(
        home_kernel,
        out_shape=(
            jax.ShapeDtypeStruct((slots, width), bf16),
            jax.ShapeDtypeStruct((slots, width), bf16),
            jax.ShapeDtypeStruct((slots, width), bf16),
            jax.ShapeDtypeStruct((out_rows, width), jnp.float32),
        ),
        in_specs=[vmem] * 7,
        out_specs=(vmem,) * 4,
        scratch_shapes=[
            pltpu.VMEM((4, slots, width), bf16),
            pltpu.VMEM((chips, slots, 2 * DH), bf16),
            pltpu.VMEM((chips, slots, 2 * DH), bf16),
            pltpu.VMEM((chips, slots, 2 * DH), bf16),
            pltpu.VMEM((rows, width), bf16),
            pltpu.VMEM((4, out_rows, width), bf16),
            pltpu.VMEM((3, out_rows, width), bf16),
            pltpu.VMEM((3, out_rows, width), bf16),
            pltpu.SemaphoreType.DMA((14,)),
            pltpu.SemaphoreType.DMA((14,)),
        ],
        compiler_params=pltpu.CompilerParams(
            collective_id=1, has_side_effects=True, vmem_limit_bytes=48 * 1024 * 1024
        ),
        name="home",
    )(o_back, dq_back, key_back, *grad_parts)


def on_device(
    projections,
    output_gradient,
    output_projection_weight,
    kept_token_indices,
    surviving_token_count,
):
    tok_dev = projections.shape[0]
    group_width = projections.shape[2]
    slots = kept_token_indices.shape[1]
    heads_local = group_width // DH
    seq_count = lax.axis_size("seq")
    quarters = seq_count // heads_local
    part_rows = slots // quarters
    me = lax.axis_index("seq")
    my_quarter = (me % quarters).astype(jnp.int32)[None]

    kept = kept_token_indices[0]
    dealt = kept.reshape(part_rows // GROUP, quarters, GROUP).transpose(1, 0, 2)
    dealt = lax.dynamic_slice_in_dim(
        jnp.concatenate([dealt, dealt], axis=0), me % quarters, quarters, axis=0
    ).reshape(slots)
    token = jnp.arange(tok_dev, dtype=jnp.int32)[None, :]
    selector = (kept[:, None] == token).astype(jnp.bfloat16)
    dealt_selector = (dealt[:, None] == token).astype(jnp.bfloat16)

    def pick(which, values):
        return jnp.dot(which, values, preferred_element_type=jnp.float32).astype(jnp.bfloat16)

    grad_local = pick(dealt_selector, output_gradient)
    query = pick(dealt_selector, projections[:, 0])
    key = pick(selector, projections[:, 1])
    value = pick(selector, projections[:, 2])

    blocks, query_in, grad_in, key_in, value_in = spread(
        grad_local, query, key, value, output_projection_weight, seq_count
    )

    def along_z(k):
        if k == 0:
            return blocks[0]
        return lax.ppermute(
            blocks[k], "seq", [(i, (i + 8 * k) % seq_count) for i in range(seq_count)]
        )

    grad_parts = [along_z(k) for k in range(4)]
    dq_back, o_back, key_back = attend(
        surviving_token_count, my_quarter, query_in, grad_in, key_in, value_in
    )
    out_rows = output_projection_weight.shape[0] // seq_count
    grad_query, grad_key, grad_value, weight_grad = bring_home(
        o_back, dq_back, key_back, grad_parts, out_rows
    )
    projection_grad = jnp.stack(
        [
            contract_rows(dealt_selector, grad_query).astype(jnp.bfloat16),
            contract_rows(selector, grad_key).astype(jnp.bfloat16),
            contract_rows(selector, grad_value).astype(jnp.bfloat16),
        ],
        axis=1,
    )
    return (projection_grad, weight_grad)


def solution(mesh):
    return jax.shard_map(
        on_device,
        mesh=mesh,
        in_specs=(P("seq", None, "head"), P("seq", "head"), P(None, "head"), P("seq", None), P()),
        out_specs=(P("seq", None, "head"), P("seq", "head")),
        check_vma=False,
    )
```

```python
import math

import jax
import jax.numpy as jnp
from jax import lax
from jax.experimental import pallas as pl
from jax.experimental.pallas import tpu as pltpu
from jax.sharding import PartitionSpec as P

DH = 128
BQ = 256
BK = 1536
GROUP = 16
NEG = -1e30


def contract_rows(left, right):
    return lax.dot_general(
        left, right, (((0,), (0,)), ((), ())), preferred_element_type=jnp.float32
    )


def attend_kernel(
    count_ref,
    quarter_ref,
    q_hbm,
    g_hbm,
    k_hbm,
    v_hbm,
    dq_out,
    o_out,
    k_out,
    q_ref,
    g_ref,
    k_ref,
    v_ref,
    qc,
    gc,
    kc,
    vc,
    k_turned,
    v_turned,
    q_turned,
    dkc,
    dvc,
    oc,
    s_scr,
    p_scr,
    qpos,
    acc,
    group_pos,
    load_sem,
):
    shards, part_rows, _ = q_ref.shape
    slots = k_ref.shape[1]
    quarter = quarter_ref[0]
    groups = part_rows // GROUP
    score_scale = 1.0 / math.sqrt(DH)
    log2e = score_scale * math.log2(math.e)
    bf16 = jnp.bfloat16
    loads = [
        pltpu.make_async_copy(src, dst, load_sem.at[i])
        for i, (src, dst) in enumerate(
            ((q_hbm, q_ref), (g_hbm, g_ref), (k_hbm, k_ref), (v_hbm, v_ref))
        )
    ]
    for load in loads:
        load.start()

    def clear(i, carry):
        rows = pl.ds(pl.multiple_of(i * slots, slots), slots)
        dkc[rows, :] = jnp.zeros((slots, DH), jnp.float32)
        dvc[rows, :] = jnp.zeros((slots, DH), jnp.float32)
        return carry

    lax.fori_loop(0, shards, clear, 0)
    q_turned[DH:, :] = jnp.where(
        lax.broadcasted_iota(jnp.int32, (DH, BQ), 0) == 0, 1.0, 0.0
    ).astype(bf16)
    for load in loads:
        load.wait()

    def dead_marks(rows, live):
        row = lax.broadcasted_iota(jnp.int32, (rows, DH), 0)
        lane = lax.broadcasted_iota(jnp.int32, (rows, DH), 1)
        return jnp.where((row >= live) & (lane == 0), NEG, 0.0).astype(bf16)

    def pack(s, carry):
        at_k, at_q = carry
        live = (count_ref[s] + GROUP - 1) // GROUP
        first = lax.rem(quarter + s, 4)
        at_k = pl.multiple_of(at_k, GROUP)
        at_q = pl.multiple_of(at_q, GROUP)
        kc[pl.ds(at_k, slots), :DH] = k_ref[s]
        kc[pl.ds(at_k, slots), DH:] = dead_marks(slots, count_ref[s])
        vc[pl.ds(at_k, slots), :] = v_ref[s]
        qc[pl.ds(at_q, part_rows), :] = q_ref[s]
        gc[pl.ds(at_q, part_rows), :] = g_ref[s]
        rows = lax.broadcasted_iota(jnp.int32, (GROUP, DH), 0)
        for i in range(groups):
            base = at_k + (first + 4 * i) * GROUP
            qpos[pl.ds(at_q + i * GROUP, GROUP), :] = base + rows
            group_pos[at_q // GROUP + i] = base
        return at_k + live * GROUP, at_q + (live - first + 3) // 4 * GROUP

    end_k, end_q = lax.fori_loop(0, shards, pack, (jnp.int32(0), jnp.int32(0)))
    end_k = pl.multiple_of(end_k, GROUP)
    end_q = pl.multiple_of(end_q, GROUP)
    kc[pl.ds(end_k, BK), :DH] = jnp.zeros((BK, DH), bf16)
    kc[pl.ds(end_k, BK), DH:] = dead_marks(BK, 0)
    vc[pl.ds(end_k, BK), :] = jnp.zeros((BK, DH), bf16)
    qc[pl.ds(end_q, BQ), :] = jnp.zeros((BQ, DH), bf16)
    gc[pl.ds(end_q, BQ), :] = jnp.zeros((BQ, DH), bf16)
    qpos[pl.ds(end_q, BQ), :] = jnp.zeros((BQ, DH), jnp.int32)
    blocks = (end_q + BQ - 1) // BQ
    oc[pl.ds(pl.multiple_of(blocks * BQ, BQ), part_rows), :] = jnp.zeros(
        (part_rows, 2 * DH), bf16
    )

    def turn(c, carry):
        keys = pl.ds(pl.multiple_of(c * BK, BK), BK)
        k_turned[:, keys] = kc[keys, :DH].T
        v_turned[:, keys] = vc[keys, :].T
        return carry

    lax.fori_loop(0, (end_k + BK - 1) // BK, turn, 0)

    def block(b, carry):
        rows = pl.ds(pl.multiple_of(b * BQ, BQ), BQ)
        last_group = jnp.minimum((b + 1) * (BQ // GROUP), end_q // GROUP) - 1
        chunks = (group_pos[last_group] + GROUP + BK - 1) // BK
        clear_chunks = (group_pos[b * (BQ // GROUP)] + 1) // BK
        q_turned[:DH, :] = qc[rows, :].T
        last_key = qpos[rows, :].T[0:1, :]

        def score(c, top, masked):
            at = pl.multiple_of(c * BK, BK)
            keys = pl.ds(at, BK)
            s = jnp.dot(kc[keys, :], q_turned[...], preferred_element_type=jnp.float32)
            if masked:
                key = at + lax.broadcasted_iota(jnp.int32, (BK, BQ), 0)
                s = jnp.where(key <= last_key, s, NEG)
            s_scr[keys, :] = s
            return jnp.maximum(top, jnp.max(s, axis=0, keepdims=True))

        top = jnp.full((1, BQ), NEG, jnp.float32)
        top = lax.fori_loop(0, clear_chunks, lambda c, t: score(c, t, False), top)
        top = lax.fori_loop(clear_chunks, chunks, lambda c, t: score(c, t, True), top)
        acc[...] = jnp.zeros((DH, BQ), jnp.float32)

        def weigh(c, total):
            keys = pl.ds(pl.multiple_of(c * BK, BK), BK)
            p = jnp.exp2((s_scr[keys, :] - top) * log2e)
            p_low = p.astype(bf16)
            p_scr[keys, :] = p_low
            acc[...] += jnp.dot(v_turned[:, keys], p_low, preferred_element_type=jnp.float32)
            return total + jnp.sum(p, axis=0, keepdims=True)

        total = lax.fori_loop(0, chunks, weigh, jnp.zeros((1, BQ), jnp.float32))
        inverse = 1.0 / total
        attended = acc[...] * inverse
        oc[rows, DH:] = attended.T.astype(bf16)
        g_turned = (gc[rows, :].astype(jnp.float32).T * inverse).astype(bf16)
        row_dot = jnp.sum(g_turned.astype(jnp.float32) * attended, axis=0, keepdims=True)
        g_part = g_turned.T
        acc[...] = jnp.zeros((DH, BQ), jnp.float32)

        def back(c, carry):
            keys = pl.ds(pl.multiple_of(c * BK, BK), BK)
            p_low = p_scr[keys, :]
            grad_probs = jnp.dot(vc[keys, :], g_turned, preferred_element_type=jnp.float32)
            ds = (p_low.astype(jnp.float32) * (grad_probs - row_dot)).astype(bf16)
            acc[...] += jnp.dot(k_turned[:, keys], ds, preferred_element_type=jnp.float32)
            dkc[keys, :] += jnp.dot(ds, qc[rows, :], preferred_element_type=jnp.float32)
            dvc[keys, :] += jnp.dot(p_low, g_part, preferred_element_type=jnp.float32)
            return carry

        lax.fori_loop(0, chunks, back, 0)
        oc[rows, :DH] = (acc[...] * score_scale).T.astype(bf16)
        return carry

    lax.fori_loop(0, blocks, block, 0)

    def unpack(s, carry):
        at_k, at_q = carry
        live = (count_ref[s] + GROUP - 1) // GROUP
        first = lax.rem(quarter + s, 4)
        at_k = pl.multiple_of(at_k, GROUP)
        at_q = pl.multiple_of(at_q, GROUP)
        dq_out[s] = oc[pl.ds(at_q, part_rows), :DH]
        o_out[s] = oc[pl.ds(at_q, part_rows), DH:]
        k_out[s, :, :DH] = (dkc[pl.ds(at_k, slots), :] * score_scale).astype(bf16)
        k_out[s, :, DH:] = dvc[pl.ds(at_k, slots), :].astype(bf16)
        return at_k + live * GROUP, at_q + (live - first + 3) // 4 * GROUP

    lax.fori_loop(0, shards, unpack, (jnp.int32(0), jnp.int32(0)))


def attend(counts, quarter, query_in, grad_in, key_in, value_in):
    shards, part_rows, _ = query_in.shape
    slots = key_in.shape[1]
    keys = shards * slots
    queries = shards * part_rows
    bf16 = jnp.bfloat16
    vmem = pl.BlockSpec(memory_space=pltpu.VMEM)
    smem = pl.BlockSpec(memory_space=pltpu.SMEM)
    hbm = pl.BlockSpec(memory_space=pl.ANY)
    return pl.pallas_call(
        attend_kernel,
        out_shape=(
            jax.ShapeDtypeStruct((shards, part_rows, DH), bf16),
            jax.ShapeDtypeStruct((shards, part_rows, DH), bf16),
            jax.ShapeDtypeStruct((shards, slots, 2 * DH), bf16),
        ),
        in_specs=[smem, smem, hbm, hbm, hbm, hbm],
        out_specs=(vmem, vmem, vmem),
        scratch_shapes=[
            pltpu.VMEM((shards, part_rows, DH), bf16),
            pltpu.VMEM((shards, part_rows, DH), bf16),
            pltpu.VMEM((shards, slots, DH), bf16),
            pltpu.VMEM((shards, slots, DH), bf16),
            pltpu.VMEM((queries + BQ, DH), bf16),
            pltpu.VMEM((queries + BQ, DH), bf16),
            pltpu.VMEM((keys + BK, 2 * DH), bf16),
            pltpu.VMEM((keys + BK, DH), bf16),
            pltpu.VMEM((DH, keys), bf16),
            pltpu.VMEM((DH, keys), bf16),
            pltpu.VMEM((2 * DH, BQ), bf16),
            pltpu.VMEM((keys, DH), jnp.float32),
            pltpu.VMEM((keys, DH), jnp.float32),
            pltpu.VMEM((queries + BQ, 2 * DH), bf16),
            pltpu.VMEM((keys, BQ), jnp.float32),
            pltpu.VMEM((keys, BQ), bf16),
            pltpu.VMEM((queries + BQ, DH), jnp.int32),
            pltpu.VMEM((DH, BQ), jnp.float32),
            pltpu.SMEM((queries // GROUP + 8,), jnp.int32),
            pltpu.SemaphoreType.DMA((4,)),
        ],
        compiler_params=pltpu.CompilerParams(vmem_limit_bytes=52 * 1024 * 1024),
        cost_estimate=pl.CostEstimate(
            flops=6 * queries * keys * DH, bytes_accessed=16 * 1024 * 1024, transcendentals=0
        ),
        name="attend",
    )(counts, quarter, query_in, grad_in, key_in, value_in)


def block_bytes_wait(ref, sem):
    pltpu.make_async_copy(ref, ref, sem).wait()


def greet(peers, peer_of, ring=0):
    barrier = pltpu.get_barrier_semaphore()

    def signal(k, carry):
        pl.semaphore_signal(
            barrier, inc=1, device_id={"seq": peer_of(k)}, device_id_type=pl.DeviceIdType.MESH
        )
        return carry

    lax.fori_loop(1, peers + 1, signal, 0)
    if ring:
        row = lax.axis_index("head")
        for k in range(1, ring):
            pl.semaphore_signal(
                barrier,
                inc=1,
                device_id={"head": lax.rem(row + k, ring)},
                device_id_type=pl.DeviceIdType.MESH,
            )
        peers = peers + ring - 1
    pl.semaphore_wait(barrier, peers)


def send(src, dst, send_sem, recv_sem, target, axis="seq"):
    copy = pltpu.make_async_remote_copy(
        src_ref=src,
        dst_ref=dst,
        send_sem=send_sem,
        recv_sem=recv_sem,
        device_id={axis: target},
        device_id_type=pl.DeviceIdType.MESH,
    )
    copy.start()
    return copy


def spread_kernel(
    grad_ref,
    q_ref,
    k_ref,
    v_ref,
    w_hbm,
    g0_out,
    g1_out,
    g2_out,
    g3_out,
    q_in,
    g_in,
    k_in,
    v_in,
    w_ref,
    acc,
    g_local,
    gblk,
    w_sem,
    copy_sem,
    y_send,
    y_recv,
    kv_send,
    kv_recv,
    pass_send,
    pass_recv,
    q_send,
    q_recv,
):
    shards, part_rows, _ = q_in.shape
    slots, cols = grad_ref.shape
    half = cols // 2
    me = lax.axis_index("seq")
    row = lax.axis_index("head")
    core = me % 2
    sibling = me + 1 - 2 * core
    chip = me // 2
    chips = shards // 2
    my_z = me // 8
    my_head = me // 4
    my_rows = pl.ds(pl.multiple_of((me % 4) * part_rows, GROUP), part_rows)

    load_w = pltpu.make_async_copy(w_hbm, w_ref, w_sem)
    load_w.start()
    greet(shards - 1, lambda k: lax.rem(me + k, shards), 4)

    def head_cols(head):
        return pl.ds(pl.multiple_of(head * DH, DH), DH)

    def slot_of(y):
        return lax.rem(y - my_z + 4, 4)

    right, left, across = lax.rem(row + 1, 4), lax.rem(row + 3, 4), lax.rem(row + 2, 4)
    to_right = send(grad_ref, gblk.at[slot_of(row)], y_send.at[0], y_recv.at[0], right, "head")
    to_left = send(grad_ref, gblk.at[slot_of(row)], y_send.at[1], y_recv.at[1], left, "head")

    def send_kv(k, carry):
        t = lax.rem(chip + k, chips)
        source = head_cols(t // 2)
        target = 2 * t + core
        send(k_ref.at[:, source], k_in.at[me], kv_send.at[0], kv_recv.at[k], target)
        send(v_ref.at[:, source], v_in.at[me], kv_send.at[1], kv_recv.at[chips + k], target)
        return carry

    lax.fori_loop(1, chips, send_kv, 0)
    own = head_cols(my_head)
    send(k_ref.at[:, own], k_in.at[me], pass_send.at[0], pass_recv.at[0], sibling)
    send(v_ref.at[:, own], v_in.at[me], pass_send.at[1], pass_recv.at[1], sibling)
    k_in[me] = k_ref[:, own]
    v_in[me] = v_ref[:, own]

    def send_q(k, carry):
        t = lax.rem(me + k, shards)
        rows = pl.ds(pl.multiple_of((t % 4) * part_rows, GROUP), part_rows)
        send(q_ref.at[rows, head_cols(t // 4)], q_in.at[me], q_send.at[0], q_recv.at[0], t)
        return carry

    lax.fori_loop(1, shards, send_q, 0)
    q_in[me] = q_ref[my_rows, own]

    width = 256
    tiles = acc.shape[1] // width
    gblk[slot_of(row)] = grad_ref[...]
    load_w.wait()

    def multiply(y, first):
        def tile(j, carry):
            at = pl.ds(pl.multiple_of(j * width, width), width)
            rows = pl.ds(pl.multiple_of(y * cols, width), cols)
            part = jnp.dot(gblk[slot_of(y)], w_ref[rows, at], preferred_element_type=jnp.float32)
            acc[:, at] = part if first else acc[:, at] + part
            return carry

        lax.fori_loop(0, tiles, tile, 0)

    multiply(row, True)
    to_right.wait_recv()
    from_left = gblk.at[slot_of(left), :, pl.ds(0, half)]
    on_right = send(from_left, from_left, y_send.at[2], y_recv.at[2], right, "head")
    to_left.wait_recv()
    from_right = gblk.at[slot_of(right), :, pl.ds(half, half)]
    on_left = send(from_right, from_right, y_send.at[3], y_recv.at[3], left, "head")
    multiply(left, False)
    multiply(right, False)

    def pass_on(k, carry):
        s = 2 * lax.rem(chip - k + chips, chips) + core
        block_bytes_wait(k_in.at[s], kv_recv.at[k])
        send(k_in.at[s], k_in.at[s], pass_send.at[0], pass_recv.at[0], sibling)
        block_bytes_wait(v_in.at[s], kv_recv.at[chips + k])
        send(v_in.at[s], v_in.at[s], pass_send.at[1], pass_recv.at[1], sibling)
        return carry

    lax.fori_loop(1, chips, pass_on, 0)
    on_right.wait_recv()
    on_left.wait_recv()

    def finish(step, carry):
        j = lax.rem(my_head // 2 + step, tiles)
        at = pl.ds(pl.multiple_of(j * width, width), width)
        rows = pl.ds(pl.multiple_of(across * cols, width), cols)
        part = jnp.dot(gblk[slot_of(across)], w_ref[rows, at], preferred_element_type=jnp.float32)
        g_local[:, at] = (acc[:, at] + part).astype(jnp.bfloat16)
        for i in range(8):
            t = j * 8 + i
            part_at = (i % 4) * part_rows

            @pl.when(t != me)
            def _():
                send(
                    g_local.at[pl.ds(part_at, part_rows), head_cols(t // 4)],
                    g_in.at[me],
                    q_send.at[1],
                    q_recv.at[1],
                    t,
                )

        return carry

    lax.fori_loop(0, tiles, finish, 0)
    g_in[me] = g_local[my_rows, own]
    copies = [
        pltpu.make_async_copy(gblk.at[k], out, copy_sem.at[k])
        for k, out in enumerate((g0_out, g1_out, g2_out, g3_out))
    ]
    for copy in copies:
        copy.start()
    for copy in copies:
        copy.wait()

    others = pl.ds(0, shards - 1)
    block_bytes_wait(q_in.at[others], q_recv.at[0])
    block_bytes_wait(q_in.at[others], q_send.at[0])
    passed = pl.ds(0, chips)
    block_bytes_wait(k_in.at[passed], pass_recv.at[0])
    block_bytes_wait(v_in.at[passed], pass_recv.at[1])
    block_bytes_wait(k_in.at[passed], pass_send.at[0])
    block_bytes_wait(v_in.at[passed], pass_send.at[1])
    sent = pl.ds(0, chips - 1)
    block_bytes_wait(k_in.at[sent], kv_send.at[0])
    block_bytes_wait(v_in.at[sent], kv_send.at[1])
    for copy in (to_right, to_left, on_right, on_left):
        copy.wait_send()
    block_bytes_wait(g_in.at[others], q_recv.at[1])
    block_bytes_wait(g_in.at[others], q_send.at[1])


def spread(grad_local, query, key, value, weight, shards):
    slots, cols = grad_local.shape
    depth, width = weight.shape
    part_rows = slots // 4
    bf16 = jnp.bfloat16
    vmem = pl.BlockSpec(memory_space=pltpu.VMEM)
    return pl.pallas_call(
        spread_kernel,
        out_shape=(
            jax.ShapeDtypeStruct((slots, cols), bf16),
            jax.ShapeDtypeStruct((slots, cols), bf16),
            jax.ShapeDtypeStruct((slots, cols), bf16),
            jax.ShapeDtypeStruct((slots, cols), bf16),
            jax.ShapeDtypeStruct((shards, part_rows, DH), bf16),
            jax.ShapeDtypeStruct((shards, part_rows, DH), bf16),
            jax.ShapeDtypeStruct((shards, slots, DH), bf16),
            jax.ShapeDtypeStruct((shards, slots, DH), bf16),
        ),
        in_specs=[vmem] * 4 + [pl.BlockSpec(memory_space=pl.ANY)],
        out_specs=(pl.BlockSpec(memory_space=pl.ANY),) * 4 + (vmem,) * 4,
        scratch_shapes=[
            pltpu.VMEM((depth, width), bf16),
            pltpu.VMEM((slots, width), jnp.float32),
            pltpu.VMEM((slots, width), bf16),
            pltpu.VMEM((4, slots, cols), bf16),
            pltpu.SemaphoreType.DMA,
            pltpu.SemaphoreType.DMA((4,)),
            pltpu.SemaphoreType.DMA((4,)),
            pltpu.SemaphoreType.DMA((4,)),
            pltpu.SemaphoreType.DMA((2,)),
            pltpu.SemaphoreType.DMA((shards,)),
            pltpu.SemaphoreType.DMA((2,)),
            pltpu.SemaphoreType.DMA((2,)),
            pltpu.SemaphoreType.DMA((2,)),
            pltpu.SemaphoreType.DMA((2,)),
        ],
        compiler_params=pltpu.CompilerParams(
            collective_id=2, has_side_effects=True, vmem_limit_bytes=48 * 1024 * 1024
        ),
        name="spread",
    )(grad_local, query, key, value, weight)


def home_kernel(
    o_ref,
    dq_ref,
    k_ref,
    g0_ref,
    g1_ref,
    g2_ref,
    g3_ref,
    dq_home,
    gk_home,
    gv_home,
    wg_out,
    oz,
    kx,
    ks,
    kin,
    part,
    px,
    rs,
    rin,
    send_sem,
    recv_sem,
):
    shards, part_rows, _ = o_ref.shape
    slots = k_ref.shape[1]
    me = lax.axis_index("seq")
    core = me % 2
    sibling = me + 1 - 2 * core
    chip = me // 2
    chips = shards // 2
    head = me // 4
    quarter = me % 4
    plane_x = chip % 4
    out_rows = wg_out.shape[0]
    my_rows = pl.ds(pl.multiple_of(quarter * part_rows, GROUP), part_rows)
    my_cols = pl.ds(pl.multiple_of(head * DH, DH), DH)

    greet(shards - 1, lambda k: lax.rem(me + k, shards))

    def send_o(k, carry):
        t = lax.rem(me + k, shards)
        send(o_ref.at[t], oz.at[0, my_rows, my_cols], send_sem.at[0], recv_sem.at[0], t)
        return carry

    lax.fori_loop(1, shards, send_o, 0)
    swap = send(k_ref.at[:, 1 - core], kx, send_sem.at[1], recv_sem.at[1], sibling)
    oz[0, my_rows, my_cols] = o_ref[me]
    dq_home[my_rows, my_cols] = dq_ref[me]
    block_bytes_wait(o_ref.at[pl.ds(0, shards - 1)], recv_sem.at[0])

    along_z = [
        send(oz.at[0], oz.at[k], send_sem.at[1 + k], recv_sem.at[1 + k], lax.rem(me + 8 * k, shards))
        for k in (1, 2, 3)
    ]
    swap.wait()

    def send_k(k, carry):
        t = lax.rem(chip + k, chips)
        ks[t] = (k_ref[t, core].astype(jnp.float32) + kx[t].astype(jnp.float32)).astype(
            jnp.bfloat16
        )
        send(ks.at[t], kin.at[chip], send_sem.at[5], recv_sem.at[5], 2 * t + core)
        return carry

    lax.fori_loop(1, chips, send_k, 0)
    kin[chip] = (k_ref[chip, core].astype(jnp.float32) + kx[chip].astype(jnp.float32)).astype(
        jnp.bfloat16
    )
    for copy in along_z:
        copy.wait()

    width = 256

    def multiply(j, carry):
        cols = pl.ds(pl.multiple_of(j * width, width), width)
        total = contract_rows(g0_ref[:, cols], oz[0])
        total += contract_rows(g1_ref[:, cols], oz[1])
        total += contract_rows(g2_ref[:, cols], oz[2])
        total += contract_rows(g3_ref[:, cols], oz[3])
        part[cols, :] = total.astype(jnp.bfloat16)
        return carry

    lax.fori_loop(0, part.shape[0] // width, multiply, 0)

    def piece(x, c):
        return pl.ds(pl.multiple_of((2 * x + c) * out_rows, 32), out_rows)

    swaps = [
        send(part.at[piece(x, 1 - core)], px.at[x], send_sem.at[6 + x], recv_sem.at[6 + x], sibling)
        for x in range(4)
    ]

    def send_dq(k, carry):
        t = lax.rem(me + k, shards)
        send(dq_ref.at[t], dq_home.at[my_rows, my_cols], send_sem.at[10], recv_sem.at[10], t)
        return carry

    for copy in swaps:
        copy.wait()

    def pair_sum(x):
        return part[piece(x, core), :].astype(jnp.float32) + px[x].astype(jnp.float32)

    along_x = []
    for k in (1, 2, 3):
        x = lax.rem(plane_x + k, 4)
        rs[k - 1] = pair_sum(x).astype(jnp.bfloat16)
        along_x.append(
            send(
                rs.at[k - 1],
                rin.at[k - 1],
                send_sem.at[10 + k],
                recv_sem.at[10 + k],
                me + 2 * (x - plane_x),
            )
        )
    lax.fori_loop(1, shards, send_dq, 0)
    wg_out[...] = pair_sum(plane_x)

    block_bytes_wait(kin.at[pl.ds(0, chips - 1)], recv_sem.at[5])
    for h in range(chips // 2):
        pair = kin[2 * h].astype(jnp.float32) + kin[2 * h + 1].astype(jnp.float32)
        pair = pair.astype(jnp.bfloat16)
        gk_home[:, h * DH : (h + 1) * DH] = pair[:, :DH]
        gv_home[:, h * DH : (h + 1) * DH] = pair[:, DH:]
    for copy in along_x:
        copy.wait()
    wg_out[...] += (
        rin[0].astype(jnp.float32) + rin[1].astype(jnp.float32) + rin[2].astype(jnp.float32)
    )
    block_bytes_wait(dq_ref.at[pl.ds(0, shards - 1)], recv_sem.at[10])
    block_bytes_wait(o_ref.at[pl.ds(0, shards - 1)], send_sem.at[0])
    block_bytes_wait(ks.at[pl.ds(0, chips - 1)], send_sem.at[5])
    block_bytes_wait(dq_ref.at[pl.ds(0, shards - 1)], send_sem.at[10])


def bring_home(o_back, dq_back, key_back, grad_parts, out_rows):
    shards, part_rows, _ = o_back.shape
    slots = key_back.shape[1]
    chips = shards // 2
    width = shards // 4 * DH
    rows = grad_parts[0].shape[1]
    key_back = key_back.reshape(chips, 2, slots, 2 * DH)
    vmem = pl.BlockSpec(memory_space=pltpu.VMEM)
    bf16 = jnp.bfloat16
    return pl.pallas_call(
        home_kernel,
        out_shape=(
            jax.ShapeDtypeStruct((slots, width), bf16),
            jax.ShapeDtypeStruct((slots, width), bf16),
            jax.ShapeDtypeStruct((slots, width), bf16),
            jax.ShapeDtypeStruct((out_rows, width), jnp.float32),
        ),
        in_specs=[vmem] * 7,
        out_specs=(vmem,) * 4,
        scratch_shapes=[
            pltpu.VMEM((4, slots, width), bf16),
            pltpu.VMEM((chips, slots, 2 * DH), bf16),
            pltpu.VMEM((chips, slots, 2 * DH), bf16),
            pltpu.VMEM((chips, slots, 2 * DH), bf16),
            pltpu.VMEM((rows, width), bf16),
            pltpu.VMEM((4, out_rows, width), bf16),
            pltpu.VMEM((3, out_rows, width), bf16),
            pltpu.VMEM((3, out_rows, width), bf16),
            pltpu.SemaphoreType.DMA((14,)),
            pltpu.SemaphoreType.DMA((14,)),
        ],
        compiler_params=pltpu.CompilerParams(
            collective_id=1, has_side_effects=True, vmem_limit_bytes=48 * 1024 * 1024
        ),
        name="home",
    )(o_back, dq_back, key_back, *grad_parts)


def on_device(
    projections,
    output_gradient,
    output_projection_weight,
    kept_token_indices,
    surviving_token_count,
):
    tok_dev = projections.shape[0]
    group_width = projections.shape[2]
    slots = kept_token_indices.shape[1]
    heads_local = group_width // DH
    seq_count = lax.axis_size("seq")
    quarters = seq_count // heads_local
    part_rows = slots // quarters
    me = lax.axis_index("seq")
    my_quarter = (me % quarters).astype(jnp.int32)[None]

    kept = kept_token_indices[0]
    dealt = kept.reshape(part_rows // GROUP, quarters, GROUP).transpose(1, 0, 2)
    dealt = lax.dynamic_slice_in_dim(
        jnp.concatenate([dealt, dealt], axis=0), me % quarters, quarters, axis=0
    ).reshape(slots)
    token = jnp.arange(tok_dev, dtype=jnp.int32)[None, :]
    selector = (kept[:, None] == token).astype(jnp.bfloat16)
    dealt_selector = (dealt[:, None] == token).astype(jnp.bfloat16)

    def pick(which, values):
        return jnp.dot(which, values, preferred_element_type=jnp.float32).astype(jnp.bfloat16)

    grad_local = pick(dealt_selector, output_gradient)
    query = pick(dealt_selector, projections[:, 0])
    key = pick(selector, projections[:, 1])
    value = pick(selector, projections[:, 2])

    *blocks, query_in, grad_in, key_in, value_in = spread(
        grad_local, query, key, value, output_projection_weight, seq_count
    )

    def along_z(k):
        if k == 0:
            return blocks[0]
        return lax.ppermute(
            blocks[k], "seq", [(i, (i + 8 * k) % seq_count) for i in range(seq_count)]
        )

    grad_parts = [along_z(k) for k in range(4)]
    dq_back, o_back, key_back = attend(
        surviving_token_count, my_quarter, query_in, grad_in, key_in, value_in
    )
    out_rows = output_projection_weight.shape[0] // seq_count
    grad_query, grad_key, grad_value, weight_grad = bring_home(
        o_back, dq_back, key_back, grad_parts, out_rows
    )
    projection_grad = jnp.stack(
        [
            contract_rows(dealt_selector, grad_query).astype(jnp.bfloat16),
            contract_rows(selector, grad_key).astype(jnp.bfloat16),
            contract_rows(selector, grad_value).astype(jnp.bfloat16),
        ],
        axis=1,
    )
    return (projection_grad, weight_grad)


def solution(mesh):
    return jax.shard_map(
        on_device,
        mesh=mesh,
        in_specs=(P("seq", None, "head"), P("seq", "head"), P(None, "head"), P("seq", None), P()),
        out_specs=(P("seq", None, "head"), P("seq", "head")),
        check_vma=False,
    )
```

```python
import math

import jax
import jax.numpy as jnp
from jax import lax
from jax.experimental import pallas as pl
from jax.experimental.pallas import tpu as pltpu
from jax.sharding import PartitionSpec as P

DH = 128
BQ = 256
BK = 1536
GROUP = 16
NEG = -1e30
CHUNKS = 4
K_STEP = 4
DQ_STEP = 4


def contract_rows(left, right):
    return lax.dot_general(
        left, right, (((0,), (0,)), ((), ())), preferred_element_type=jnp.float32
    )


def attend_kernel(
    count_ref,
    quarter_ref,
    q_hbm,
    g_hbm,
    k_hbm,
    v_hbm,
    dq_out,
    o_out,
    k_out,
    q_ref,
    g_ref,
    k_ref,
    v_ref,
    qc,
    gc,
    kc,
    vc,
    k_turned,
    v_turned,
    q_turned,
    dkc,
    dvc,
    oc,
    s_scr,
    p_scr,
    qpos,
    acc,
    group_pos,
    load_sem,
):
    shards, part_rows, _ = q_ref.shape
    slots = k_ref.shape[1]
    quarter = quarter_ref[0]
    groups = part_rows // GROUP
    score_scale = 1.0 / math.sqrt(DH)
    log2e = score_scale * math.log2(math.e)
    bf16 = jnp.bfloat16
    loads = [
        pltpu.make_async_copy(src, dst, load_sem.at[i])
        for i, (src, dst) in enumerate(
            ((q_hbm, q_ref), (g_hbm, g_ref), (k_hbm, k_ref), (v_hbm, v_ref))
        )
    ]
    for load in loads:
        load.start()

    def clear(i, carry):
        rows = pl.ds(pl.multiple_of(i * slots, slots), slots)
        dkc[rows, :] = jnp.zeros((slots, DH), jnp.float32)
        dvc[rows, :] = jnp.zeros((slots, DH), jnp.float32)
        return carry

    lax.fori_loop(0, shards, clear, 0)
    q_turned[DH:, :] = jnp.where(
        lax.broadcasted_iota(jnp.int32, (DH, BQ), 0) == 0, 1.0, 0.0
    ).astype(bf16)
    for load in loads:
        load.wait()

    def dead_marks(rows, live):
        row = lax.broadcasted_iota(jnp.int32, (rows, DH), 0)
        lane = lax.broadcasted_iota(jnp.int32, (rows, DH), 1)
        return jnp.where((row >= live) & (lane == 0), NEG, 0.0).astype(bf16)

    def pack(s, carry):
        at_k, at_q = carry
        live = (count_ref[s] + GROUP - 1) // GROUP
        first = lax.rem(quarter + s, 4)
        at_k = pl.multiple_of(at_k, GROUP)
        at_q = pl.multiple_of(at_q, GROUP)
        kc[pl.ds(at_k, slots), :DH] = k_ref[s]
        kc[pl.ds(at_k, slots), DH:] = dead_marks(slots, count_ref[s])
        vc[pl.ds(at_k, slots), :] = v_ref[s]
        qc[pl.ds(at_q, part_rows), :] = q_ref[s]
        gc[pl.ds(at_q, part_rows), :] = g_ref[s]
        rows = lax.broadcasted_iota(jnp.int32, (GROUP, DH), 0)
        for i in range(groups):
            base = at_k + (first + 4 * i) * GROUP
            qpos[pl.ds(at_q + i * GROUP, GROUP), :] = base + rows
            group_pos[at_q // GROUP + i] = base
        return at_k + live * GROUP, at_q + (live - first + 3) // 4 * GROUP

    end_k, end_q = lax.fori_loop(0, shards, pack, (jnp.int32(0), jnp.int32(0)))
    end_k = pl.multiple_of(end_k, GROUP)
    end_q = pl.multiple_of(end_q, GROUP)
    kc[pl.ds(end_k, BK), :DH] = jnp.zeros((BK, DH), bf16)
    kc[pl.ds(end_k, BK), DH:] = dead_marks(BK, 0)
    vc[pl.ds(end_k, BK), :] = jnp.zeros((BK, DH), bf16)
    qc[pl.ds(end_q, BQ), :] = jnp.zeros((BQ, DH), bf16)
    gc[pl.ds(end_q, BQ), :] = jnp.zeros((BQ, DH), bf16)
    qpos[pl.ds(end_q, BQ), :] = jnp.zeros((BQ, DH), jnp.int32)
    blocks = (end_q + BQ - 1) // BQ
    oc[pl.ds(pl.multiple_of(blocks * BQ, BQ), part_rows), :] = jnp.zeros(
        (part_rows, 2 * DH), bf16
    )

    def turn(c, carry):
        keys = pl.ds(pl.multiple_of(c * BK, BK), BK)
        k_turned[:, keys] = kc[keys, :DH].T
        v_turned[:, keys] = vc[keys, :].T
        return carry

    lax.fori_loop(0, (end_k + BK - 1) // BK, turn, 0)

    def block(b, carry):
        rows = pl.ds(pl.multiple_of(b * BQ, BQ), BQ)
        last_group = jnp.minimum((b + 1) * (BQ // GROUP), end_q // GROUP) - 1
        chunks = (group_pos[last_group] + GROUP + BK - 1) // BK
        clear_chunks = (group_pos[b * (BQ // GROUP)] + 1) // BK
        q_turned[:DH, :] = qc[rows, :].T
        last_key = qpos[rows, :].T[0:1, :]

        def score(c, top, masked):
            at = pl.multiple_of(c * BK, BK)
            keys = pl.ds(at, BK)
            s = jnp.dot(kc[keys, :], q_turned[...], preferred_element_type=jnp.float32)
            if masked:
                key = at + lax.broadcasted_iota(jnp.int32, (BK, BQ), 0)
                s = jnp.where(key <= last_key, s, NEG)
            s_scr[keys, :] = s
            return jnp.maximum(top, jnp.max(s, axis=0, keepdims=True))

        top = jnp.full((1, BQ), NEG, jnp.float32)
        top = lax.fori_loop(0, clear_chunks, lambda c, t: score(c, t, False), top)
        top = lax.fori_loop(clear_chunks, chunks, lambda c, t: score(c, t, True), top)
        acc[...] = jnp.zeros((DH, BQ), jnp.float32)

        def weigh(c, total):
            keys = pl.ds(pl.multiple_of(c * BK, BK), BK)
            p = jnp.exp2((s_scr[keys, :] - top) * log2e)
            p_low = p.astype(bf16)
            p_scr[keys, :] = p_low
            acc[...] += jnp.dot(v_turned[:, keys], p_low, preferred_element_type=jnp.float32)
            return total + jnp.sum(p, axis=0, keepdims=True)

        total = lax.fori_loop(0, chunks, weigh, jnp.zeros((1, BQ), jnp.float32))
        inverse = 1.0 / total
        attended = acc[...] * inverse
        oc[rows, DH:] = attended.T.astype(bf16)
        g_turned = (gc[rows, :].astype(jnp.float32).T * inverse).astype(bf16)
        row_dot = jnp.sum(g_turned.astype(jnp.float32) * attended, axis=0, keepdims=True)
        g_part = g_turned.T
        acc[...] = jnp.zeros((DH, BQ), jnp.float32)

        def back(c, carry):
            keys = pl.ds(pl.multiple_of(c * BK, BK), BK)
            p_low = p_scr[keys, :]
            grad_probs = jnp.dot(vc[keys, :], g_turned, preferred_element_type=jnp.float32)
            ds = (p_low.astype(jnp.float32) * (grad_probs - row_dot)).astype(bf16)
            acc[...] += jnp.dot(k_turned[:, keys], ds, preferred_element_type=jnp.float32)
            dkc[keys, :] += jnp.dot(ds, qc[rows, :], preferred_element_type=jnp.float32)
            dvc[keys, :] += jnp.dot(p_low, g_part, preferred_element_type=jnp.float32)
            return carry

        lax.fori_loop(0, chunks, back, 0)
        oc[rows, :DH] = (acc[...] * score_scale).T.astype(bf16)
        return carry

    lax.fori_loop(0, blocks, block, 0)

    def unpack(s, carry):
        at_k, at_q = carry
        live = (count_ref[s] + GROUP - 1) // GROUP
        first = lax.rem(quarter + s, 4)
        at_k = pl.multiple_of(at_k, GROUP)
        at_q = pl.multiple_of(at_q, GROUP)
        dq_out[s] = oc[pl.ds(at_q, part_rows), :DH]
        o_out[s] = oc[pl.ds(at_q, part_rows), DH:]
        k_out[s, :, :DH] = (dkc[pl.ds(at_k, slots), :] * score_scale).astype(bf16)
        k_out[s, :, DH:] = dvc[pl.ds(at_k, slots), :].astype(bf16)
        return at_k + live * GROUP, at_q + (live - first + 3) // 4 * GROUP

    lax.fori_loop(0, shards, unpack, (jnp.int32(0), jnp.int32(0)))


def attend(counts, quarter, query_in, grad_in, key_in, value_in):
    shards, part_rows, _ = query_in.shape
    slots = key_in.shape[1]
    keys = shards * slots
    queries = shards * part_rows
    bf16 = jnp.bfloat16
    vmem = pl.BlockSpec(memory_space=pltpu.VMEM)
    smem = pl.BlockSpec(memory_space=pltpu.SMEM)
    hbm = pl.BlockSpec(memory_space=pl.ANY)
    return pl.pallas_call(
        attend_kernel,
        out_shape=(
            jax.ShapeDtypeStruct((shards, part_rows, DH), bf16),
            jax.ShapeDtypeStruct((shards, part_rows, DH), bf16),
            jax.ShapeDtypeStruct((shards, slots, 2 * DH), bf16),
        ),
        in_specs=[smem, smem, hbm, hbm, hbm, hbm],
        out_specs=(vmem, vmem, vmem),
        scratch_shapes=[
            pltpu.VMEM((shards, part_rows, DH), bf16),
            pltpu.VMEM((shards, part_rows, DH), bf16),
            pltpu.VMEM((shards, slots, DH), bf16),
            pltpu.VMEM((shards, slots, DH), bf16),
            pltpu.VMEM((queries + BQ, DH), bf16),
            pltpu.VMEM((queries + BQ, DH), bf16),
            pltpu.VMEM((keys + BK, 2 * DH), bf16),
            pltpu.VMEM((keys + BK, DH), bf16),
            pltpu.VMEM((DH, keys), bf16),
            pltpu.VMEM((DH, keys), bf16),
            pltpu.VMEM((2 * DH, BQ), bf16),
            pltpu.VMEM((keys, DH), jnp.float32),
            pltpu.VMEM((keys, DH), jnp.float32),
            pltpu.VMEM((queries + BQ, 2 * DH), bf16),
            pltpu.VMEM((keys, BQ), jnp.float32),
            pltpu.VMEM((keys, BQ), bf16),
            pltpu.VMEM((queries + BQ, DH), jnp.int32),
            pltpu.VMEM((DH, BQ), jnp.float32),
            pltpu.SMEM((queries // GROUP + 8,), jnp.int32),
            pltpu.SemaphoreType.DMA((4,)),
        ],
        compiler_params=pltpu.CompilerParams(vmem_limit_bytes=52 * 1024 * 1024),
        cost_estimate=pl.CostEstimate(
            flops=6 * queries * keys * DH, bytes_accessed=16 * 1024 * 1024, transcendentals=0
        ),
        name="attend",
    )(counts, quarter, query_in, grad_in, key_in, value_in)


def block_bytes_wait(ref, sem):
    pltpu.make_async_copy(ref, ref, sem).wait()


def greet(peers, peer_of, ring=0):
    barrier = pltpu.get_barrier_semaphore()

    def signal(k, carry):
        pl.semaphore_signal(
            barrier, inc=1, device_id={"seq": peer_of(k)}, device_id_type=pl.DeviceIdType.MESH
        )
        return carry

    lax.fori_loop(1, peers + 1, signal, 0)
    if ring:
        row = lax.axis_index("head")
        for k in range(1, ring):
            pl.semaphore_signal(
                barrier,
                inc=1,
                device_id={"head": lax.rem(row + k, ring)},
                device_id_type=pl.DeviceIdType.MESH,
            )
        peers = peers + ring - 1
    pl.semaphore_wait(barrier, peers)


def send(src, dst, send_sem, recv_sem, target, axis="seq"):
    copy = pltpu.make_async_remote_copy(
        src_ref=src,
        dst_ref=dst,
        send_sem=send_sem,
        recv_sem=recv_sem,
        device_id={axis: target},
        device_id_type=pl.DeviceIdType.MESH,
    )
    copy.start()
    return copy


def spread_kernel(
    grad_ref,
    q_ref,
    k_ref,
    v_ref,
    w_hbm,
    g0_out,
    g1_out,
    g2_out,
    g3_out,
    q_in,
    g_in,
    k_in,
    v_in,
    w_ref,
    acc,
    g_local,
    gblk,
    w_sem,
    copy_sem,
    y_send,
    y_recv,
    kv_send,
    kv_recv,
    pass_send,
    pass_recv,
    q_send,
    q_recv,
):
    shards, part_rows, _ = q_in.shape
    slots, cols = grad_ref.shape
    half = cols // 2
    me = lax.axis_index("seq")
    row = lax.axis_index("head")
    core = me % 2
    sibling = me + 1 - 2 * core
    chip = me // 2
    chips = shards // 2
    my_z = me // 8
    my_head = me // 4
    my_rows = pl.ds(pl.multiple_of((me % 4) * part_rows, GROUP), part_rows)

    load_w = pltpu.make_async_copy(w_hbm, w_ref, w_sem)
    load_w.start()
    greet(shards - 1, lambda k: lax.rem(me + k, shards), 4)

    def head_cols(head):
        return pl.ds(pl.multiple_of(head * DH, DH), DH)

    def slot_of(y):
        return lax.rem(y - my_z + 4, 4)

    right, left, across = lax.rem(row + 1, 4), lax.rem(row + 3, 4), lax.rem(row + 2, 4)
    to_right = send(grad_ref, gblk.at[slot_of(row)], y_send.at[0], y_recv.at[0], right, "head")
    to_left = send(grad_ref, gblk.at[slot_of(row)], y_send.at[1], y_recv.at[1], left, "head")

    def send_kv(k, carry):
        t = lax.rem(chip + k, chips)
        source = head_cols(t // 2)
        target = 2 * t + core
        send(k_ref.at[:, source], k_in.at[me], kv_send.at[0], kv_recv.at[k], target)
        send(v_ref.at[:, source], v_in.at[me], kv_send.at[1], kv_recv.at[chips + k], target)
        return carry

    lax.fori_loop(1, chips, send_kv, 0)
    own = head_cols(my_head)
    send(k_ref.at[:, own], k_in.at[me], pass_send.at[0], pass_recv.at[0], sibling)
    send(v_ref.at[:, own], v_in.at[me], pass_send.at[1], pass_recv.at[1], sibling)
    k_in[me] = k_ref[:, own]
    v_in[me] = v_ref[:, own]

    def send_q(k, carry):
        t = lax.rem(me + k, shards)
        rows = pl.ds(pl.multiple_of((t % 4) * part_rows, GROUP), part_rows)
        send(q_ref.at[rows, head_cols(t // 4)], q_in.at[me], q_send.at[0], q_recv.at[0], t)
        return carry

    lax.fori_loop(1, shards, send_q, 0)
    q_in[me] = q_ref[my_rows, own]

    width = 256
    tiles = acc.shape[1] // width
    gblk[slot_of(row)] = grad_ref[...]
    load_w.wait()

    def multiply(y, first):
        def tile(j, carry):
            at = pl.ds(pl.multiple_of(j * width, width), width)
            rows = pl.ds(pl.multiple_of(y * cols, width), cols)
            part = jnp.dot(gblk[slot_of(y)], w_ref[rows, at], preferred_element_type=jnp.float32)
            acc[:, at] = part if first else acc[:, at] + part
            return carry

        lax.fori_loop(0, tiles, tile, 0)

    multiply(row, True)
    to_right.wait_recv()
    from_left = gblk.at[slot_of(left), :, pl.ds(0, half)]
    on_right = send(from_left, from_left, y_send.at[2], y_recv.at[2], right, "head")
    to_left.wait_recv()
    from_right = gblk.at[slot_of(right), :, pl.ds(half, half)]
    on_left = send(from_right, from_right, y_send.at[3], y_recv.at[3], left, "head")
    multiply(left, False)
    multiply(right, False)

    def pass_on(k, carry):
        s = 2 * lax.rem(chip - k + chips, chips) + core
        block_bytes_wait(k_in.at[s], kv_recv.at[k])
        send(k_in.at[s], k_in.at[s], pass_send.at[0], pass_recv.at[0], sibling)
        block_bytes_wait(v_in.at[s], kv_recv.at[chips + k])
        send(v_in.at[s], v_in.at[s], pass_send.at[1], pass_recv.at[1], sibling)
        return carry

    lax.fori_loop(1, chips, pass_on, 0)
    on_right.wait_recv()
    on_left.wait_recv()

    def finish(step, carry):
        j = lax.rem(my_head // 2 + step, tiles)
        at = pl.ds(pl.multiple_of(j * width, width), width)
        rows = pl.ds(pl.multiple_of(across * cols, width), cols)
        part = jnp.dot(gblk[slot_of(across)], w_ref[rows, at], preferred_element_type=jnp.float32)
        g_local[:, at] = (acc[:, at] + part).astype(jnp.bfloat16)
        for i in range(8):
            t = j * 8 + i
            part_at = (i % 4) * part_rows

            @pl.when(t != me)
            def _():
                send(
                    g_local.at[pl.ds(part_at, part_rows), head_cols(t // 4)],
                    g_in.at[me],
                    q_send.at[1],
                    q_recv.at[1],
                    t,
                )

        return carry

    lax.fori_loop(0, tiles, finish, 0)
    g_in[me] = g_local[my_rows, own]
    copies = [
        pltpu.make_async_copy(gblk.at[k], out, copy_sem.at[k])
        for k, out in enumerate((g0_out, g1_out, g2_out, g3_out))
    ]
    for copy in copies:
        copy.start()
    for copy in copies:
        copy.wait()

    others = pl.ds(0, shards - 1)
    block_bytes_wait(q_in.at[others], q_recv.at[0])
    block_bytes_wait(q_in.at[others], q_send.at[0])
    passed = pl.ds(0, chips)
    block_bytes_wait(k_in.at[passed], pass_recv.at[0])
    block_bytes_wait(v_in.at[passed], pass_recv.at[1])
    block_bytes_wait(k_in.at[passed], pass_send.at[0])
    block_bytes_wait(v_in.at[passed], pass_send.at[1])
    sent = pl.ds(0, chips - 1)
    block_bytes_wait(k_in.at[sent], kv_send.at[0])
    block_bytes_wait(v_in.at[sent], kv_send.at[1])
    for copy in (to_right, to_left, on_right, on_left):
        copy.wait_send()
    block_bytes_wait(g_in.at[others], q_recv.at[1])
    block_bytes_wait(g_in.at[others], q_send.at[1])


def spread(grad_local, query, key, value, weight, shards):
    slots, cols = grad_local.shape
    depth, width = weight.shape
    part_rows = slots // 4
    bf16 = jnp.bfloat16
    vmem = pl.BlockSpec(memory_space=pltpu.VMEM)
    return pl.pallas_call(
        spread_kernel,
        out_shape=(
            jax.ShapeDtypeStruct((slots, cols), bf16),
            jax.ShapeDtypeStruct((slots, cols), bf16),
            jax.ShapeDtypeStruct((slots, cols), bf16),
            jax.ShapeDtypeStruct((slots, cols), bf16),
            jax.ShapeDtypeStruct((shards, part_rows, DH), bf16),
            jax.ShapeDtypeStruct((shards, part_rows, DH), bf16),
            jax.ShapeDtypeStruct((shards, slots, DH), bf16),
            jax.ShapeDtypeStruct((shards, slots, DH), bf16),
        ),
        in_specs=[vmem] * 4 + [pl.BlockSpec(memory_space=pl.ANY)],
        out_specs=(pl.BlockSpec(memory_space=pl.ANY),) * 4 + (vmem,) * 4,
        scratch_shapes=[
            pltpu.VMEM((depth, width), bf16),
            pltpu.VMEM((slots, width), jnp.float32),
            pltpu.VMEM((slots, width), bf16),
            pltpu.VMEM((4, slots, cols), bf16),
            pltpu.SemaphoreType.DMA,
            pltpu.SemaphoreType.DMA((4,)),
            pltpu.SemaphoreType.DMA((4,)),
            pltpu.SemaphoreType.DMA((4,)),
            pltpu.SemaphoreType.DMA((2,)),
            pltpu.SemaphoreType.DMA((shards,)),
            pltpu.SemaphoreType.DMA((2,)),
            pltpu.SemaphoreType.DMA((2,)),
            pltpu.SemaphoreType.DMA((2,)),
            pltpu.SemaphoreType.DMA((2,)),
        ],
        compiler_params=pltpu.CompilerParams(
            collective_id=2, has_side_effects=True, vmem_limit_bytes=48 * 1024 * 1024
        ),
        name="spread",
    )(grad_local, query, key, value, weight)


def home_kernel(
    o_ref,
    dq_ref,
    k_ref,
    g0_ref,
    g1_ref,
    g2_ref,
    g3_ref,
    dq_home,
    gk_home,
    gv_home,
    wg_out,
    g_turned,
    oz,
    kx,
    ks,
    k_row,
    k_pair,
    k_col,
    part,
    px,
    half_send,
    half_recv,
    full_send,
    full_recv,
    send_sem,
    recv_sem,
    k_send,
    k_recv,
    z_send,
    z_recv,
    p_send,
    p_recv,
    x_send,
    x_recv,
):
    shards, part_rows, _ = o_ref.shape
    slots = k_ref.shape[3]
    me = lax.axis_index("seq")
    core = me % 2
    sibling = me + 1 - 2 * core
    plane_x = me // 2 % 4
    my_z = me // 8
    out_rows, width = wg_out.shape
    my_rows = pl.ds(pl.multiple_of((me % 4) * part_rows, GROUP), part_rows)
    my_cols = pl.ds(pl.multiple_of((me // 4) * DH, DH), DH)
    f32, bf16 = jnp.float32, jnp.bfloat16

    greet(shards - 1, lambda k: lax.rem(me + k, shards))

    def send_o(k, carry):
        t = lax.rem(me + k, shards)
        send(o_ref.at[t], oz.at[0, my_rows, my_cols], send_sem.at[0], recv_sem.at[0], t)
        return carry

    lax.fori_loop(1, shards, send_o, 0)
    swap = send(k_ref.at[:, :, 1 - core], kx, send_sem.at[1], recv_sem.at[1], sibling)
    oz[0, my_rows, my_cols] = o_ref[me]
    dq_home[my_rows, my_cols] = dq_ref[me]

    tile = 256

    def turn(j, carry):
        cols = pl.ds(pl.multiple_of(j * tile, tile), tile)
        for k, g_ref in enumerate((g0_ref, g1_ref, g2_ref, g3_ref)):
            g_turned[k, cols, :] = g_ref[:, cols].T
        return carry

    lax.fori_loop(0, part.shape[0] // tile, turn, 0)
    block_bytes_wait(o_ref.at[pl.ds(0, shards - 1)], recv_sem.at[0])

    chunk = width // CHUNKS
    z_up, z_down = lax.rem(me + 8, shards), lax.rem(me + 24, shards)
    x_up = me + 2 * (lax.rem(plane_x + 1, 4) - plane_x)
    x_down = me + 2 * (lax.rem(plane_x + 3, 4) - plane_x)
    upper, lower = pl.ds(0, slots // 2), pl.ds(slots // 2, slots // 2)
    top, bottom = pl.ds(0, out_rows // 2), pl.ds(out_rows // 2, out_rows // 2)

    def cols_of(c):
        return pl.ds(c * chunk, chunk)

    def start_z(c):
        own = oz.at[0, :, cols_of(c)]
        send(own, oz.at[1, :, cols_of(c)], z_send.at[0], z_recv.at[0, c], z_up)
        send(own, oz.at[3, :, cols_of(c)], z_send.at[1], z_recv.at[1, c], z_down)

    def forward_z(c):
        cols = cols_of(c)
        block_bytes_wait(oz.at[1, :, cols], z_recv.at[0, c])
        send(
            oz.at[1, upper, cols], oz.at[2, upper, cols], z_send.at[2], z_recv.at[2, c], z_up
        )
        block_bytes_wait(oz.at[3, :, cols], z_recv.at[1, c])
        send(
            oz.at[3, lower, cols], oz.at[2, lower, cols], z_send.at[3], z_recv.at[3, c], z_down
        )
        if c + 2 < CHUNKS:
            start_z(c + 2)

    def piece(x, c):
        return pl.ds(pl.multiple_of((2 * x + c) * out_rows, 32), out_rows)

    def product(c):
        cols = cols_of(c)
        block_bytes_wait(oz.at[2, upper, cols], z_recv.at[2, c])
        block_bytes_wait(oz.at[2, lower, cols], z_recv.at[3, c])

        def rows_tile(j, carry):
            rows = pl.ds(pl.multiple_of(j * tile, tile), tile)
            total = jnp.dot(g_turned[0, rows, :], oz[0, :, cols], preferred_element_type=f32)
            for k in (1, 2, 3):
                total += jnp.dot(g_turned[k, rows, :], oz[k, :, cols], preferred_element_type=f32)
            part[rows, cols] = total.astype(bf16)
            return carry

        lax.fori_loop(0, part.shape[0] // tile, rows_tile, 0)
        for x in range(4):
            send(
                part.at[piece(x, 1 - core), cols],
                px.at[x, :, cols],
                p_send,
                p_recv.at[c],
                sibling,
            )

    def pair_sum(x, c):
        cols = cols_of(c)
        return part[piece(x, core), cols].astype(f32) + px[x, :, cols].astype(f32)

    def send_half(c):
        cols = cols_of(c)
        block_bytes_wait(px.at[:, :, cols], p_recv.at[c])
        half_send[:, cols] = pair_sum(lax.rem(plane_x + 2, 4), c).astype(bf16)
        send(
            half_send.at[top, cols], half_recv.at[top, cols], x_send.at[0], x_recv.at[0, c], x_up
        )
        send(
            half_send.at[bottom, cols],
            half_recv.at[bottom, cols],
            x_send.at[1],
            x_recv.at[1, c],
            x_down,
        )

    def send_full(c):
        cols = cols_of(c)
        split = out_rows // 2
        block_bytes_wait(half_recv.at[top, cols], x_recv.at[0, c])
        ahead = pair_sum(lax.rem(plane_x + 1, 4), c)
        full_send[0, top, cols] = (ahead[:split] + half_recv[top, cols].astype(f32)).astype(bf16)
        full_send[0, bottom, cols] = ahead[split:].astype(bf16)
        send(
            full_send.at[0, :, cols], full_recv.at[0, :, cols], x_send.at[2], x_recv.at[2, c], x_up
        )
        block_bytes_wait(half_recv.at[bottom, cols], x_recv.at[1, c])
        behind = pair_sum(lax.rem(plane_x + 3, 4), c)
        full_send[1, top, cols] = behind[:split].astype(bf16)
        full_send[1, bottom, cols] = (behind[split:] + half_recv[bottom, cols].astype(f32)).astype(
            bf16
        )
        send(
            full_send.at[1, :, cols],
            full_recv.at[1, :, cols],
            x_send.at[3],
            x_recv.at[3, c],
            x_down,
        )

    def finish(c):
        cols = cols_of(c)
        block_bytes_wait(full_recv.at[0, :, cols], x_recv.at[2, c])
        block_bytes_wait(full_recv.at[1, :, cols], x_recv.at[3, c])
        wg_out[:, cols] = (
            pair_sum(plane_x, c)
            + full_recv[0, :, cols].astype(f32)
            + full_recv[1, :, cols].astype(f32)
        )

    def k_sum(z, x):
        return (k_ref[z, x, core].astype(f32) + kx[z, x].astype(f32)).astype(bf16)

    def k_along_x():
        for k in (1, 2, 3):
            x = lax.rem(plane_x + k, 4)
            for z in range(4):
                ks[z, x] = k_sum(z, x)
            send(
                ks.at[:, x],
                k_row.at[plane_x],
                k_send.at[k - 1],
                k_recv.at[k - 1],
                me + 2 * (x - plane_x),
            )
        for z in range(4):
            k_row[plane_x, z] = k_sum(z, plane_x)

    def k_along_z():
        for k in range(3):
            block_bytes_wait(k_row.at[0], k_recv.at[k])
        for k in (1, 2, 3, 0):
            z = lax.rem(my_z + k, 4)
            for h in range(2):
                pair = k_row[2 * h, z].astype(f32) + k_row[2 * h + 1, z].astype(f32)
                k_pair[z, h] = pair.astype(bf16)
            if k:
                send(
                    k_pair.at[z],
                    k_col.at[my_z],
                    k_send.at[2 + k],
                    k_recv.at[2 + k],
                    lax.rem(me + 8 * k, shards),
                )
            else:
                k_col[my_z] = k_pair[z]

    def send_dq(k, carry):
        t = lax.rem(me + k, shards)
        send(dq_ref.at[t], dq_home.at[my_rows, my_cols], send_sem.at[3], recv_sem.at[3], t)
        return carry

    start_z(0)
    start_z(1)
    swap.wait()
    k_along_x()
    stages = (forward_z, product, send_half, send_full, finish)
    for step in range(CHUNKS + len(stages) - 1):
        if step == K_STEP:
            k_along_z()
        if step == DQ_STEP:
            lax.fori_loop(1, shards, send_dq, 0)
        for i, stage in enumerate(stages):
            if 0 <= step - i < CHUNKS:
                stage(step - i)
    for k in range(3):
        block_bytes_wait(k_col.at[0], k_recv.at[3 + k])
    for z in range(4):
        for h in range(2):
            cols = pl.ds((2 * z + h) * DH, DH)
            gk_home[:, cols] = k_col[z, h, :, :DH]
            gv_home[:, cols] = k_col[z, h, :, DH:]
    block_bytes_wait(dq_ref.at[pl.ds(0, shards - 1)], recv_sem.at[3])
    block_bytes_wait(o_ref.at[pl.ds(0, shards - 1)], send_sem.at[0])
    for k in range(3):
        block_bytes_wait(ks.at[:, 0], k_send.at[k])
        block_bytes_wait(k_pair.at[0], k_send.at[3 + k])
    block_bytes_wait(dq_ref.at[pl.ds(0, shards - 1)], send_sem.at[3])
    block_bytes_wait(oz.at[0], z_send.at[0])
    block_bytes_wait(oz.at[0], z_send.at[1])
    block_bytes_wait(oz.at[1, upper], z_send.at[2])
    block_bytes_wait(oz.at[3, lower], z_send.at[3])
    block_bytes_wait(px, p_send)
    block_bytes_wait(half_send.at[top], x_send.at[0])
    block_bytes_wait(half_send.at[bottom], x_send.at[1])
    block_bytes_wait(full_send.at[0], x_send.at[2])
    block_bytes_wait(full_send.at[1], x_send.at[3])


def bring_home(o_back, dq_back, key_back, grad_parts, out_rows):
    shards, part_rows, _ = o_back.shape
    slots = key_back.shape[1]
    width = shards // 4 * DH
    rows = grad_parts[0].shape[1]
    key_back = key_back.reshape(4, 4, 2, slots, 2 * DH)
    vmem = pl.BlockSpec(memory_space=pltpu.VMEM)
    bf16 = jnp.bfloat16
    return pl.pallas_call(
        home_kernel,
        out_shape=(
            jax.ShapeDtypeStruct((slots, width), bf16),
            jax.ShapeDtypeStruct((slots, width), bf16),
            jax.ShapeDtypeStruct((slots, width), bf16),
            jax.ShapeDtypeStruct((out_rows, width), jnp.float32),
        ),
        in_specs=[vmem] * 7,
        out_specs=(vmem,) * 4,
        scratch_shapes=[
            pltpu.VMEM((4, rows, slots), bf16),
            pltpu.VMEM((4, slots, width), bf16),
            pltpu.VMEM((4, 4, slots, 2 * DH), bf16),
            pltpu.VMEM((4, 4, slots, 2 * DH), bf16),
            pltpu.VMEM((4, 4, slots, 2 * DH), bf16),
            pltpu.VMEM((4, 2, slots, 2 * DH), bf16),
            pltpu.VMEM((4, 2, slots, 2 * DH), bf16),
            pltpu.VMEM((rows, width), bf16),
            pltpu.VMEM((4, out_rows, width), bf16),
            pltpu.VMEM((out_rows, width), bf16),
            pltpu.VMEM((out_rows, width), bf16),
            pltpu.VMEM((2, out_rows, width), bf16),
            pltpu.VMEM((2, out_rows, width), bf16),
            pltpu.SemaphoreType.DMA((4,)),
            pltpu.SemaphoreType.DMA((4,)),
            pltpu.SemaphoreType.DMA((6,)),
            pltpu.SemaphoreType.DMA((6,)),
            pltpu.SemaphoreType.DMA((4,)),
            pltpu.SemaphoreType.DMA((4, CHUNKS)),
            pltpu.SemaphoreType.DMA,
            pltpu.SemaphoreType.DMA((CHUNKS,)),
            pltpu.SemaphoreType.DMA((4,)),
            pltpu.SemaphoreType.DMA((4, CHUNKS)),
        ],
        compiler_params=pltpu.CompilerParams(
            collective_id=1, has_side_effects=True, vmem_limit_bytes=48 * 1024 * 1024
        ),
        name="home",
    )(o_back, dq_back, key_back, *grad_parts)


def on_device(
    projections,
    output_gradient,
    output_projection_weight,
    kept_token_indices,
    surviving_token_count,
):
    tok_dev = projections.shape[0]
    group_width = projections.shape[2]
    slots = kept_token_indices.shape[1]
    heads_local = group_width // DH
    seq_count = lax.axis_size("seq")
    quarters = seq_count // heads_local
    part_rows = slots // quarters
    me = lax.axis_index("seq")
    my_quarter = (me % quarters).astype(jnp.int32)[None]

    kept = kept_token_indices[0]
    dealt = kept.reshape(part_rows // GROUP, quarters, GROUP).transpose(1, 0, 2)
    dealt = lax.dynamic_slice_in_dim(
        jnp.concatenate([dealt, dealt], axis=0), me % quarters, quarters, axis=0
    ).reshape(slots)
    token = jnp.arange(tok_dev, dtype=jnp.int32)[None, :]
    selector = (kept[:, None] == token).astype(jnp.bfloat16)
    dealt_selector = (dealt[:, None] == token).astype(jnp.bfloat16)

    def pick(which, values):
        return jnp.dot(which, values, preferred_element_type=jnp.float32).astype(jnp.bfloat16)

    grad_local = pick(dealt_selector, output_gradient)
    query = pick(dealt_selector, projections[:, 0])
    key = pick(selector, projections[:, 1])
    value = pick(selector, projections[:, 2])

    *blocks, query_in, grad_in, key_in, value_in = spread(
        grad_local, query, key, value, output_projection_weight, seq_count
    )

    def along_z(k):
        if k == 0:
            return blocks[0]
        return lax.ppermute(
            blocks[k], "seq", [(i, (i + 8 * k) % seq_count) for i in range(seq_count)]
        )

    grad_parts = [along_z(k) for k in range(4)]
    dq_back, o_back, key_back = attend(
        surviving_token_count, my_quarter, query_in, grad_in, key_in, value_in
    )
    out_rows = output_projection_weight.shape[0] // seq_count
    grad_query, grad_key, grad_value, weight_grad = bring_home(
        o_back, dq_back, key_back, grad_parts, out_rows
    )
    projection_grad = jnp.stack(
        [
            contract_rows(dealt_selector, grad_query).astype(jnp.bfloat16),
            contract_rows(selector, grad_key).astype(jnp.bfloat16),
            contract_rows(selector, grad_value).astype(jnp.bfloat16),
        ],
        axis=1,
    )
    return (projection_grad, weight_grad)


def solution(mesh):
    return jax.shard_map(
        on_device,
        mesh=mesh,
        in_specs=(P("seq", None, "head"), P("seq", "head"), P(None, "head"), P("seq", None), P()),
        out_specs=(P("seq", None, "head"), P("seq", "head")),
        check_vma=False,
    )
```

```python
import math

import jax
import jax.numpy as jnp
from jax import lax
from jax.experimental import pallas as pl
from jax.experimental.pallas import tpu as pltpu
from jax.sharding import PartitionSpec as P

DH = 128
BQ = 256
BK = 1536
GROUP = 16
NEG = -1e30
CHUNKS = 4
K_STEP = 4
DQ_STEP = 4


def contract_rows(left, right):
    return lax.dot_general(
        left, right, (((0,), (0,)), ((), ())), preferred_element_type=jnp.float32
    )


def attend_kernel(
    count_ref,
    quarter_ref,
    q_hbm,
    g_hbm,
    k_hbm,
    v_hbm,
    dq_out,
    o_out,
    k_out,
    q_ref,
    g_ref,
    k_ref,
    v_ref,
    qc,
    gc,
    kc,
    vc,
    k_turned,
    v_turned,
    q_turned,
    dkc,
    dvc,
    oc,
    s_scr,
    p_scr,
    qpos,
    acc,
    group_pos,
    load_sem,
):
    shards, part_rows, _ = q_ref.shape
    slots = k_ref.shape[1]
    quarter = quarter_ref[0]
    groups = part_rows // GROUP
    score_scale = 1.0 / math.sqrt(DH)
    log2e = score_scale * math.log2(math.e)
    bf16 = jnp.bfloat16
    loads = [
        pltpu.make_async_copy(src, dst, load_sem.at[i])
        for i, (src, dst) in enumerate(
            ((q_hbm, q_ref), (g_hbm, g_ref), (k_hbm, k_ref), (v_hbm, v_ref))
        )
    ]
    for load in loads:
        load.start()

    def clear(i, carry):
        rows = pl.ds(pl.multiple_of(i * slots, slots), slots)
        dkc[rows, :] = jnp.zeros((slots, DH), jnp.float32)
        dvc[rows, :] = jnp.zeros((slots, DH), jnp.float32)
        return carry

    lax.fori_loop(0, shards, clear, 0)
    q_turned[DH:, :] = jnp.where(
        lax.broadcasted_iota(jnp.int32, (DH, BQ), 0) == 0, 1.0, 0.0
    ).astype(bf16)
    for load in loads:
        load.wait()

    def dead_marks(rows, live):
        row = lax.broadcasted_iota(jnp.int32, (rows, DH), 0)
        lane = lax.broadcasted_iota(jnp.int32, (rows, DH), 1)
        return jnp.where((row >= live) & (lane == 0), NEG, 0.0).astype(bf16)

    def pack(s, carry):
        at_k, at_q = carry
        live = (count_ref[s] + GROUP - 1) // GROUP
        first = lax.rem(quarter + s, 4)
        at_k = pl.multiple_of(at_k, GROUP)
        at_q = pl.multiple_of(at_q, GROUP)
        kc[pl.ds(at_k, slots), :DH] = k_ref[s]
        kc[pl.ds(at_k, slots), DH:] = dead_marks(slots, count_ref[s])
        vc[pl.ds(at_k, slots), :] = v_ref[s]
        qc[pl.ds(at_q, part_rows), :] = q_ref[s]
        gc[pl.ds(at_q, part_rows), :] = g_ref[s]
        rows = lax.broadcasted_iota(jnp.int32, (GROUP, DH), 0)
        for i in range(groups):
            base = at_k + (first + 4 * i) * GROUP
            qpos[pl.ds(at_q + i * GROUP, GROUP), :] = base + rows
            group_pos[at_q // GROUP + i] = base
        return at_k + live * GROUP, at_q + (live - first + 3) // 4 * GROUP

    end_k, end_q = lax.fori_loop(0, shards, pack, (jnp.int32(0), jnp.int32(0)))
    end_k = pl.multiple_of(end_k, GROUP)
    end_q = pl.multiple_of(end_q, GROUP)
    kc[pl.ds(end_k, BK), :DH] = jnp.zeros((BK, DH), bf16)
    kc[pl.ds(end_k, BK), DH:] = dead_marks(BK, 0)
    vc[pl.ds(end_k, BK), :] = jnp.zeros((BK, DH), bf16)
    qc[pl.ds(end_q, BQ), :] = jnp.zeros((BQ, DH), bf16)
    gc[pl.ds(end_q, BQ), :] = jnp.zeros((BQ, DH), bf16)
    qpos[pl.ds(end_q, BQ), :] = jnp.zeros((BQ, DH), jnp.int32)
    blocks = (end_q + BQ - 1) // BQ
    oc[pl.ds(pl.multiple_of(blocks * BQ, BQ), part_rows), :] = jnp.zeros(
        (part_rows, 2 * DH), bf16
    )

    def turn(c, carry):
        keys = pl.ds(pl.multiple_of(c * BK, BK), BK)
        k_turned[:, keys] = kc[keys, :DH].T
        v_turned[:, keys] = vc[keys, :].T
        return carry

    lax.fori_loop(0, (end_k + BK - 1) // BK, turn, 0)

    def block(b, carry):
        rows = pl.ds(pl.multiple_of(b * BQ, BQ), BQ)
        last_group = jnp.minimum((b + 1) * (BQ // GROUP), end_q // GROUP) - 1
        chunks = (group_pos[last_group] + GROUP + BK - 1) // BK
        clear_chunks = (group_pos[b * (BQ // GROUP)] + 1) // BK
        q_turned[:DH, :] = qc[rows, :].T
        last_key = qpos[rows, :].T[0:1, :]

        def score(c, top, masked):
            at = pl.multiple_of(c * BK, BK)
            keys = pl.ds(at, BK)
            s = jnp.dot(kc[keys, :], q_turned[...], preferred_element_type=jnp.float32)
            if masked:
                key = at + lax.broadcasted_iota(jnp.int32, (BK, BQ), 0)
                s = jnp.where(key <= last_key, s, NEG)
            s_scr[keys, :] = s
            return jnp.maximum(top, jnp.max(s, axis=0, keepdims=True))

        top = jnp.full((1, BQ), NEG, jnp.float32)
        top = lax.fori_loop(0, clear_chunks, lambda c, t: score(c, t, False), top)
        top = lax.fori_loop(clear_chunks, chunks, lambda c, t: score(c, t, True), top)
        acc[...] = jnp.zeros((DH, BQ), jnp.float32)

        def weigh(c, total):
            keys = pl.ds(pl.multiple_of(c * BK, BK), BK)
            p = jnp.exp2((s_scr[keys, :] - top) * log2e)
            p_low = p.astype(bf16)
            p_scr[keys, :] = p_low
            acc[...] += jnp.dot(v_turned[:, keys], p_low, preferred_element_type=jnp.float32)
            return total + jnp.sum(p, axis=0, keepdims=True)

        total = lax.fori_loop(0, chunks, weigh, jnp.zeros((1, BQ), jnp.float32))
        inverse = 1.0 / total
        attended = acc[...] * inverse
        oc[rows, DH:] = attended.T.astype(bf16)
        g_turned = (gc[rows, :].astype(jnp.float32).T * inverse).astype(bf16)
        row_dot = jnp.sum(g_turned.astype(jnp.float32) * attended, axis=0, keepdims=True)
        g_part = g_turned.T
        acc[...] = jnp.zeros((DH, BQ), jnp.float32)

        def back(c, carry):
            keys = pl.ds(pl.multiple_of(c * BK, BK), BK)
            p_low = p_scr[keys, :]
            grad_probs = jnp.dot(vc[keys, :], g_turned, preferred_element_type=jnp.float32)
            ds = (p_low.astype(jnp.float32) * (grad_probs - row_dot)).astype(bf16)
            acc[...] += jnp.dot(k_turned[:, keys], ds, preferred_element_type=jnp.float32)
            dkc[keys, :] += jnp.dot(ds, qc[rows, :], preferred_element_type=jnp.float32)
            dvc[keys, :] += jnp.dot(p_low, g_part, preferred_element_type=jnp.float32)
            return carry

        lax.fori_loop(0, chunks, back, 0)
        oc[rows, :DH] = (acc[...] * score_scale).T.astype(bf16)
        return carry

    lax.fori_loop(0, blocks, block, 0)

    def unpack(s, carry):
        at_k, at_q = carry
        live = (count_ref[s] + GROUP - 1) // GROUP
        first = lax.rem(quarter + s, 4)
        at_k = pl.multiple_of(at_k, GROUP)
        at_q = pl.multiple_of(at_q, GROUP)
        dq_out[s] = oc[pl.ds(at_q, part_rows), :DH]
        o_out[s] = oc[pl.ds(at_q, part_rows), DH:]
        k_out[s, :, :DH] = (dkc[pl.ds(at_k, slots), :] * score_scale).astype(bf16)
        k_out[s, :, DH:] = dvc[pl.ds(at_k, slots), :].astype(bf16)
        return at_k + live * GROUP, at_q + (live - first + 3) // 4 * GROUP

    lax.fori_loop(0, shards, unpack, (jnp.int32(0), jnp.int32(0)))


def attend(counts, quarter, query_in, grad_in, key_in, value_in):
    shards, part_rows, _ = query_in.shape
    slots = key_in.shape[1]
    keys = shards * slots
    queries = shards * part_rows
    bf16 = jnp.bfloat16
    vmem = pl.BlockSpec(memory_space=pltpu.VMEM)
    smem = pl.BlockSpec(memory_space=pltpu.SMEM)
    hbm = pl.BlockSpec(memory_space=pl.ANY)
    return pl.pallas_call(
        attend_kernel,
        out_shape=(
            jax.ShapeDtypeStruct((shards, part_rows, DH), bf16),
            jax.ShapeDtypeStruct((shards, part_rows, DH), bf16),
            jax.ShapeDtypeStruct((shards, slots, 2 * DH), bf16),
        ),
        in_specs=[smem, smem, hbm, hbm, hbm, hbm],
        out_specs=(vmem, vmem, vmem),
        scratch_shapes=[
            pltpu.VMEM((shards, part_rows, DH), bf16),
            pltpu.VMEM((shards, part_rows, DH), bf16),
            pltpu.VMEM((shards, slots, DH), bf16),
            pltpu.VMEM((shards, slots, DH), bf16),
            pltpu.VMEM((queries + BQ, DH), bf16),
            pltpu.VMEM((queries + BQ, DH), bf16),
            pltpu.VMEM((keys + BK, 2 * DH), bf16),
            pltpu.VMEM((keys + BK, DH), bf16),
            pltpu.VMEM((DH, keys), bf16),
            pltpu.VMEM((DH, keys), bf16),
            pltpu.VMEM((2 * DH, BQ), bf16),
            pltpu.VMEM((keys, DH), jnp.float32),
            pltpu.VMEM((keys, DH), jnp.float32),
            pltpu.VMEM((queries + BQ, 2 * DH), bf16),
            pltpu.VMEM((keys, BQ), jnp.float32),
            pltpu.VMEM((keys, BQ), bf16),
            pltpu.VMEM((queries + BQ, DH), jnp.int32),
            pltpu.VMEM((DH, BQ), jnp.float32),
            pltpu.SMEM((queries // GROUP + 8,), jnp.int32),
            pltpu.SemaphoreType.DMA((4,)),
        ],
        compiler_params=pltpu.CompilerParams(vmem_limit_bytes=52 * 1024 * 1024),
        cost_estimate=pl.CostEstimate(
            flops=6 * queries * keys * DH, bytes_accessed=16 * 1024 * 1024, transcendentals=0
        ),
        name="attend",
    )(counts, quarter, query_in, grad_in, key_in, value_in)


def block_bytes_wait(ref, sem):
    pltpu.make_async_copy(ref, ref, sem).wait()


def greet(peers, peer_of, ring=0):
    barrier = pltpu.get_barrier_semaphore()

    def signal(k, carry):
        pl.semaphore_signal(
            barrier, inc=1, device_id={"seq": peer_of(k)}, device_id_type=pl.DeviceIdType.MESH
        )
        return carry

    lax.fori_loop(1, peers + 1, signal, 0)
    if ring:
        row = lax.axis_index("head")
        for k in range(1, ring):
            pl.semaphore_signal(
                barrier,
                inc=1,
                device_id={"head": lax.rem(row + k, ring)},
                device_id_type=pl.DeviceIdType.MESH,
            )
        peers = peers + ring - 1
    pl.semaphore_wait(barrier, peers)


def send(src, dst, send_sem, recv_sem, target, axis="seq"):
    copy = pltpu.make_async_remote_copy(
        src_ref=src,
        dst_ref=dst,
        send_sem=send_sem,
        recv_sem=recv_sem,
        device_id={axis: target},
        device_id_type=pl.DeviceIdType.MESH,
    )
    copy.start()
    return copy


def spread_kernel(
    grad_ref,
    q_ref,
    k_ref,
    v_ref,
    w_hbm,
    g0_out,
    g1_out,
    g2_out,
    g3_out,
    q_in,
    g_in,
    k_in,
    v_in,
    w_ref,
    acc,
    g_local,
    gblk,
    k_col,
    v_col,
    w_sem,
    copy_sem,
    y_send,
    y_recv,
    z_send,
    z_recv,
    x_send,
    x_recv,
    own_sem,
    pass_send,
    pass_recv,
    q_send,
    q_recv,
    q_own,
):
    shards, part_rows, _ = q_in.shape
    slots, cols = grad_ref.shape
    half = cols // 2
    me = lax.axis_index("seq")
    row = lax.axis_index("head")
    core = me % 2
    sibling = me + 1 - 2 * core
    my_z = me // 8
    my_x = me // 2 % 4
    my_head = me // 4
    my_rows = pl.ds(pl.multiple_of((me % 4) * part_rows, GROUP), part_rows)

    load_w = pltpu.make_async_copy(w_hbm, w_ref, w_sem)
    load_w.start()
    greet(shards - 1, lambda k: lax.rem(me + k, shards), 4)

    def head_cols(head):
        return pl.ds(pl.multiple_of(head * DH, DH), DH)

    def pair_cols(z):
        return pl.ds(pl.multiple_of(z * 2 * DH, 2 * DH), 2 * DH)

    def slot_of(y):
        return lax.rem(y - my_z + 4, 4)

    right, left, across = lax.rem(row + 1, 4), lax.rem(row + 3, 4), lax.rem(row + 2, 4)
    to_right = send(grad_ref, gblk.at[slot_of(row)], y_send.at[0], y_recv.at[0], right, "head")
    to_left = send(grad_ref, gblk.at[slot_of(row)], y_send.at[1], y_recv.at[1], left, "head")

    sides = ((k_ref, k_col, k_in), (v_ref, v_col, v_in))
    for k in (1, 3, 2):
        target = lax.rem(me + 8 * k, shards)
        for i, (src, col, _) in enumerate(sides):
            send(
                src.at[:, pair_cols(lax.rem(my_z + k, 4))],
                col.at[my_z],
                z_send.at[i],
                z_recv.at[i, k],
                target,
            )

    def fan(k):
        z = lax.rem(my_z - k + 4, 4)
        for i, (src, col, out) in enumerate(sides):
            if k:
                block_bytes_wait(col.at[z], z_recv.at[i, k])
            else:
                col[z] = src[:, pair_cols(my_z)]
            for d in (1, 3, 2):
                x = lax.rem(my_x + d, 4)
                send(
                    col.at[z, :, head_cols(x // 2)],
                    out.at[z, my_x, core],
                    x_send.at[i],
                    x_recv.at[i, k],
                    me + 2 * (x - my_x),
                )
            pltpu.make_async_copy(
                col.at[z, :, head_cols(my_x // 2)], out.at[z, my_x, core], own_sem.at[i, k]
            ).start()

    def pass_on(k):
        z = lax.rem(my_z - k + 4, 4)
        for i, (_, _, out) in enumerate(sides):
            block_bytes_wait(out.at[z, pl.ds(0, 3), core], x_recv.at[i, k])
            block_bytes_wait(out.at[z, my_x, core], own_sem.at[i, k])
            send(out.at[z, :, core], out.at[z, :, core], pass_send.at[i], pass_recv.at[i], sibling)

    fan(0)

    def send_q(k, carry):
        t = lax.rem(me + k, shards)
        rows = pl.ds(pl.multiple_of((t % 4) * part_rows, GROUP), part_rows)
        send(q_ref.at[rows, head_cols(t // 4)], q_in.at[me], q_send.at[0], q_recv.at[0], t)
        return carry

    lax.fori_loop(1, shards, send_q, 0)
    own_q = pltpu.make_async_copy(q_ref.at[my_rows, head_cols(my_head)], q_in.at[me], q_own.at[0])
    own_q.start()

    width = 256
    tiles = acc.shape[1] // width
    gblk[slot_of(row)] = grad_ref[...]
    load_w.wait()

    def multiply(y, first):
        def tile(j, carry):
            at = pl.ds(pl.multiple_of(j * width, width), width)
            rows = pl.ds(pl.multiple_of(y * cols, width), cols)
            part = jnp.dot(gblk[slot_of(y)], w_ref[rows, at], preferred_element_type=jnp.float32)
            acc[:, at] = part if first else acc[:, at] + part
            return carry

        lax.fori_loop(0, tiles, tile, 0)

    multiply(row, True)
    for k in (1, 3, 2):
        fan(k)
    to_right.wait_recv()
    from_left = gblk.at[slot_of(left), :, pl.ds(0, half)]
    on_right = send(from_left, from_left, y_send.at[2], y_recv.at[2], right, "head")
    to_left.wait_recv()
    from_right = gblk.at[slot_of(right), :, pl.ds(half, half)]
    on_left = send(from_right, from_right, y_send.at[3], y_recv.at[3], left, "head")
    pass_on(0)
    multiply(left, False)
    pass_on(1)
    multiply(right, False)
    pass_on(3)
    on_right.wait_recv()
    on_left.wait_recv()

    def finish(step, carry):
        j = lax.rem(my_head // 2 + step, tiles)
        at = pl.ds(pl.multiple_of(j * width, width), width)
        rows = pl.ds(pl.multiple_of(across * cols, width), cols)
        part = jnp.dot(gblk[slot_of(across)], w_ref[rows, at], preferred_element_type=jnp.float32)
        g_local[:, at] = (acc[:, at] + part).astype(jnp.bfloat16)
        for i in range(8):
            t = j * 8 + i
            part_at = (i % 4) * part_rows

            @pl.when(t != me)
            def _():
                send(
                    g_local.at[pl.ds(part_at, part_rows), head_cols(t // 4)],
                    g_in.at[me],
                    q_send.at[1],
                    q_recv.at[1],
                    t,
                )

        return carry

    lax.fori_loop(0, tiles, finish, 0)
    own_g = pltpu.make_async_copy(
        g_local.at[my_rows, head_cols(my_head)], g_in.at[me], q_own.at[1]
    )
    own_g.start()
    copies = [
        pltpu.make_async_copy(gblk.at[k], out, copy_sem.at[k])
        for k, out in enumerate((g0_out, g1_out, g2_out, g3_out))
    ]
    for copy in copies:
        copy.start()
    pass_on(2)
    for copy in copies:
        copy.wait()
    own_q.wait()
    own_g.wait()

    others = pl.ds(0, shards - 1)
    block_bytes_wait(q_in.at[others], q_recv.at[0])
    block_bytes_wait(q_in.at[others], q_send.at[0])
    for i, (_, col, out) in enumerate(sides):
        block_bytes_wait(out.at[:, :, core], pass_recv.at[i])
        block_bytes_wait(out.at[:, :, core], pass_send.at[i])
        block_bytes_wait(col.at[pl.ds(0, 3)], z_send.at[i])
        block_bytes_wait(out.at[:, pl.ds(0, 3), core], x_send.at[i])
    for copy in (to_right, to_left, on_right, on_left):
        copy.wait_send()
    block_bytes_wait(g_in.at[others], q_recv.at[1])
    block_bytes_wait(g_in.at[others], q_send.at[1])


def spread(grad_local, query, key, value, weight, shards):
    slots, cols = grad_local.shape
    depth, width = weight.shape
    part_rows = slots // 4
    bf16 = jnp.bfloat16
    vmem = pl.BlockSpec(memory_space=pltpu.VMEM)
    block = jax.ShapeDtypeStruct((slots, cols), bf16)
    small = jax.ShapeDtypeStruct((shards, part_rows, DH), bf16)
    large = jax.ShapeDtypeStruct((4, 4, 2, slots, DH), bf16)
    *blocks, query_in, grad_in, key_in, value_in = pl.pallas_call(
        spread_kernel,
        out_shape=(block,) * 4 + (small,) * 2 + (large,) * 2,
        in_specs=[vmem] * 4 + [pl.BlockSpec(memory_space=pl.ANY)],
        out_specs=(pl.BlockSpec(memory_space=pl.ANY),) * 8,
        scratch_shapes=[
            pltpu.VMEM((depth, width), bf16),
            pltpu.VMEM((slots, width), jnp.float32),
            pltpu.VMEM((slots, width), bf16),
            pltpu.VMEM((4, slots, cols), bf16),
            pltpu.VMEM((4, slots, 2 * DH), bf16),
            pltpu.VMEM((4, slots, 2 * DH), bf16),
            pltpu.SemaphoreType.DMA,
            pltpu.SemaphoreType.DMA((4,)),
            pltpu.SemaphoreType.DMA((4,)),
            pltpu.SemaphoreType.DMA((4,)),
            pltpu.SemaphoreType.DMA((2,)),
            pltpu.SemaphoreType.DMA((2, 4)),
            pltpu.SemaphoreType.DMA((2,)),
            pltpu.SemaphoreType.DMA((2, 4)),
            pltpu.SemaphoreType.DMA((2, 4)),
            pltpu.SemaphoreType.DMA((2,)),
            pltpu.SemaphoreType.DMA((2,)),
            pltpu.SemaphoreType.DMA((2,)),
            pltpu.SemaphoreType.DMA((2,)),
            pltpu.SemaphoreType.DMA((2,)),
        ],
        compiler_params=pltpu.CompilerParams(
            collective_id=2, has_side_effects=True, vmem_limit_bytes=48 * 1024 * 1024
        ),
        name="spread",
    )(grad_local, query, key, value, weight)
    key_in = key_in.reshape(shards, slots, DH)
    value_in = value_in.reshape(shards, slots, DH)
    return (*blocks, query_in, grad_in, key_in, value_in)


def home_kernel(
    o_ref,
    dq_ref,
    k_ref,
    g0_ref,
    g1_ref,
    g2_ref,
    g3_ref,
    dq_home,
    gk_home,
    gv_home,
    wg_out,
    g_turned,
    oz,
    kx,
    ks,
    k_row,
    k_pair,
    k_col,
    part,
    px,
    half_send,
    half_recv,
    full_send,
    full_recv,
    send_sem,
    recv_sem,
    k_send,
    k_recv,
    z_send,
    z_recv,
    p_send,
    p_recv,
    x_send,
    x_recv,
):
    shards, part_rows, _ = o_ref.shape
    slots = k_ref.shape[3]
    me = lax.axis_index("seq")
    core = me % 2
    sibling = me + 1 - 2 * core
    plane_x = me // 2 % 4
    my_z = me // 8
    out_rows, width = wg_out.shape
    my_rows = pl.ds(pl.multiple_of((me % 4) * part_rows, GROUP), part_rows)
    my_cols = pl.ds(pl.multiple_of((me // 4) * DH, DH), DH)
    f32, bf16 = jnp.float32, jnp.bfloat16

    greet(shards - 1, lambda k: lax.rem(me + k, shards))

    def send_o(k, carry):
        t = lax.rem(me + k, shards)
        send(o_ref.at[t], oz.at[0, my_rows, my_cols], send_sem.at[0], recv_sem.at[0], t)
        return carry

    lax.fori_loop(1, shards, send_o, 0)
    swap = send(k_ref.at[:, :, 1 - core], kx, send_sem.at[1], recv_sem.at[1], sibling)
    oz[0, my_rows, my_cols] = o_ref[me]
    dq_home[my_rows, my_cols] = dq_ref[me]

    tile = 256

    def turn(j, carry):
        cols = pl.ds(pl.multiple_of(j * tile, tile), tile)
        for k, g_ref in enumerate((g0_ref, g1_ref, g2_ref, g3_ref)):
            g_turned[k, cols, :] = g_ref[:, cols].T
        return carry

    lax.fori_loop(0, part.shape[0] // tile, turn, 0)
    block_bytes_wait(o_ref.at[pl.ds(0, shards - 1)], recv_sem.at[0])

    chunk = width // CHUNKS
    z_up, z_down = lax.rem(me + 8, shards), lax.rem(me + 24, shards)
    x_up = me + 2 * (lax.rem(plane_x + 1, 4) - plane_x)
    x_down = me + 2 * (lax.rem(plane_x + 3, 4) - plane_x)
    upper, lower = pl.ds(0, slots // 2), pl.ds(slots // 2, slots // 2)
    top, bottom = pl.ds(0, out_rows // 2), pl.ds(out_rows // 2, out_rows // 2)

    def cols_of(c):
        return pl.ds(c * chunk, chunk)

    def start_z(c):
        own = oz.at[0, :, cols_of(c)]
        send(own, oz.at[1, :, cols_of(c)], z_send.at[0], z_recv.at[0, c], z_up)
        send(own, oz.at[3, :, cols_of(c)], z_send.at[1], z_recv.at[1, c], z_down)

    def forward_z(c):
        cols = cols_of(c)
        block_bytes_wait(oz.at[1, :, cols], z_recv.at[0, c])
        send(
            oz.at[1, upper, cols], oz.at[2, upper, cols], z_send.at[2], z_recv.at[2, c], z_up
        )
        block_bytes_wait(oz.at[3, :, cols], z_recv.at[1, c])
        send(
            oz.at[3, lower, cols], oz.at[2, lower, cols], z_send.at[3], z_recv.at[3, c], z_down
        )
        if c + 2 < CHUNKS:
            start_z(c + 2)

    def piece(x, c):
        return pl.ds(pl.multiple_of((2 * x + c) * out_rows, 32), out_rows)

    def product(c):
        cols = cols_of(c)
        block_bytes_wait(oz.at[2, upper, cols], z_recv.at[2, c])
        block_bytes_wait(oz.at[2, lower, cols], z_recv.at[3, c])

        def rows_tile(j, carry):
            rows = pl.ds(pl.multiple_of(j * tile, tile), tile)
            total = jnp.dot(g_turned[0, rows, :], oz[0, :, cols], preferred_element_type=f32)
            for k in (1, 2, 3):
                total += jnp.dot(g_turned[k, rows, :], oz[k, :, cols], preferred_element_type=f32)
            part[rows, cols] = total.astype(bf16)
            return carry

        lax.fori_loop(0, part.shape[0] // tile, rows_tile, 0)
        for x in range(4):
            send(
                part.at[piece(x, 1 - core), cols],
                px.at[x, :, cols],
                p_send,
                p_recv.at[c],
                sibling,
            )

    def pair_sum(x, c):
        cols = cols_of(c)
        return part[piece(x, core), cols].astype(f32) + px[x, :, cols].astype(f32)

    def send_half(c):
        cols = cols_of(c)
        block_bytes_wait(px.at[:, :, cols], p_recv.at[c])
        half_send[:, cols] = pair_sum(lax.rem(plane_x + 2, 4), c).astype(bf16)
        send(
            half_send.at[top, cols], half_recv.at[top, cols], x_send.at[0], x_recv.at[0, c], x_up
        )
        send(
            half_send.at[bottom, cols],
            half_recv.at[bottom, cols],
            x_send.at[1],
            x_recv.at[1, c],
            x_down,
        )

    def send_full(c):
        cols = cols_of(c)
        split = out_rows // 2
        block_bytes_wait(half_recv.at[top, cols], x_recv.at[0, c])
        ahead = pair_sum(lax.rem(plane_x + 1, 4), c)
        full_send[0, top, cols] = (ahead[:split] + half_recv[top, cols].astype(f32)).astype(bf16)
        full_send[0, bottom, cols] = ahead[split:].astype(bf16)
        send(
            full_send.at[0, :, cols], full_recv.at[0, :, cols], x_send.at[2], x_recv.at[2, c], x_up
        )
        block_bytes_wait(half_recv.at[bottom, cols], x_recv.at[1, c])
        behind = pair_sum(lax.rem(plane_x + 3, 4), c)
        full_send[1, top, cols] = behind[:split].astype(bf16)
        full_send[1, bottom, cols] = (behind[split:] + half_recv[bottom, cols].astype(f32)).astype(
            bf16
        )
        send(
            full_send.at[1, :, cols],
            full_recv.at[1, :, cols],
            x_send.at[3],
            x_recv.at[3, c],
            x_down,
        )

    def finish(c):
        cols = cols_of(c)
        block_bytes_wait(full_recv.at[0, :, cols], x_recv.at[2, c])
        block_bytes_wait(full_recv.at[1, :, cols], x_recv.at[3, c])
        wg_out[:, cols] = (
            pair_sum(plane_x, c)
            + full_recv[0, :, cols].astype(f32)
            + full_recv[1, :, cols].astype(f32)
        )

    def k_sum(z, x):
        return (k_ref[z, x, core].astype(f32) + kx[z, x].astype(f32)).astype(bf16)

    def k_along_x():
        for k in (1, 2, 3):
            x = lax.rem(plane_x + k, 4)
            for z in range(4):
                ks[z, x] = k_sum(z, x)
            send(
                ks.at[:, x],
                k_row.at[plane_x],
                k_send.at[k - 1],
                k_recv.at[k - 1],
                me + 2 * (x - plane_x),
            )
        for z in range(4):
            k_row[plane_x, z] = k_sum(z, plane_x)

    def k_along_z():
        for k in range(3):
            block_bytes_wait(k_row.at[0], k_recv.at[k])
        for k in (1, 2, 3, 0):
            z = lax.rem(my_z + k, 4)
            for h in range(2):
                pair = k_row[2 * h, z].astype(f32) + k_row[2 * h + 1, z].astype(f32)
                k_pair[z, h] = pair.astype(bf16)
            if k:
                send(
                    k_pair.at[z],
                    k_col.at[my_z],
                    k_send.at[2 + k],
                    k_recv.at[2 + k],
                    lax.rem(me + 8 * k, shards),
                )
            else:
                k_col[my_z] = k_pair[z]

    def send_dq(k, carry):
        t = lax.rem(me + k, shards)
        send(dq_ref.at[t], dq_home.at[my_rows, my_cols], send_sem.at[3], recv_sem.at[3], t)
        return carry

    start_z(0)
    start_z(1)
    swap.wait()
    k_along_x()
    stages = (forward_z, product, send_half, send_full, finish)
    for step in range(CHUNKS + len(stages) - 1):
        if step == K_STEP:
            k_along_z()
        if step == DQ_STEP:
            lax.fori_loop(1, shards, send_dq, 0)
        for i, stage in enumerate(stages):
            if 0 <= step - i < CHUNKS:
                stage(step - i)
    for k in range(3):
        block_bytes_wait(k_col.at[0], k_recv.at[3 + k])
    for z in range(4):
        for h in range(2):
            cols = pl.ds((2 * z + h) * DH, DH)
            gk_home[:, cols] = k_col[z, h, :, :DH]
            gv_home[:, cols] = k_col[z, h, :, DH:]
    block_bytes_wait(dq_ref.at[pl.ds(0, shards - 1)], recv_sem.at[3])
    block_bytes_wait(o_ref.at[pl.ds(0, shards - 1)], send_sem.at[0])
    for k in range(3):
        block_bytes_wait(ks.at[:, 0], k_send.at[k])
        block_bytes_wait(k_pair.at[0], k_send.at[3 + k])
    block_bytes_wait(dq_ref.at[pl.ds(0, shards - 1)], send_sem.at[3])
    block_bytes_wait(oz.at[0], z_send.at[0])
    block_bytes_wait(oz.at[0], z_send.at[1])
    block_bytes_wait(oz.at[1, upper], z_send.at[2])
    block_bytes_wait(oz.at[3, lower], z_send.at[3])
    block_bytes_wait(px, p_send)
    block_bytes_wait(half_send.at[top], x_send.at[0])
    block_bytes_wait(half_send.at[bottom], x_send.at[1])
    block_bytes_wait(full_send.at[0], x_send.at[2])
    block_bytes_wait(full_send.at[1], x_send.at[3])


def bring_home(o_back, dq_back, key_back, grad_parts, out_rows):
    shards, part_rows, _ = o_back.shape
    slots = key_back.shape[1]
    width = shards // 4 * DH
    rows = grad_parts[0].shape[1]
    key_back = key_back.reshape(4, 4, 2, slots, 2 * DH)
    vmem = pl.BlockSpec(memory_space=pltpu.VMEM)
    bf16 = jnp.bfloat16
    return pl.pallas_call(
        home_kernel,
        out_shape=(
            jax.ShapeDtypeStruct((slots, width), bf16),
            jax.ShapeDtypeStruct((slots, width), bf16),
            jax.ShapeDtypeStruct((slots, width), bf16),
            jax.ShapeDtypeStruct((out_rows, width), jnp.float32),
        ),
        in_specs=[vmem] * 7,
        out_specs=(vmem,) * 4,
        scratch_shapes=[
            pltpu.VMEM((4, rows, slots), bf16),
            pltpu.VMEM((4, slots, width), bf16),
            pltpu.VMEM((4, 4, slots, 2 * DH), bf16),
            pltpu.VMEM((4, 4, slots, 2 * DH), bf16),
            pltpu.VMEM((4, 4, slots, 2 * DH), bf16),
            pltpu.VMEM((4, 2, slots, 2 * DH), bf16),
            pltpu.VMEM((4, 2, slots, 2 * DH), bf16),
            pltpu.VMEM((rows, width), bf16),
            pltpu.VMEM((4, out_rows, width), bf16),
            pltpu.VMEM((out_rows, width), bf16),
            pltpu.VMEM((out_rows, width), bf16),
            pltpu.VMEM((2, out_rows, width), bf16),
            pltpu.VMEM((2, out_rows, width), bf16),
            pltpu.SemaphoreType.DMA((4,)),
            pltpu.SemaphoreType.DMA((4,)),
            pltpu.SemaphoreType.DMA((6,)),
            pltpu.SemaphoreType.DMA((6,)),
            pltpu.SemaphoreType.DMA((4,)),
            pltpu.SemaphoreType.DMA((4, CHUNKS)),
            pltpu.SemaphoreType.DMA,
            pltpu.SemaphoreType.DMA((CHUNKS,)),
            pltpu.SemaphoreType.DMA((4,)),
            pltpu.SemaphoreType.DMA((4, CHUNKS)),
        ],
        compiler_params=pltpu.CompilerParams(
            collective_id=1, has_side_effects=True, vmem_limit_bytes=48 * 1024 * 1024
        ),
        name="home",
    )(o_back, dq_back, key_back, *grad_parts)


def on_device(
    projections,
    output_gradient,
    output_projection_weight,
    kept_token_indices,
    surviving_token_count,
):
    tok_dev = projections.shape[0]
    group_width = projections.shape[2]
    slots = kept_token_indices.shape[1]
    heads_local = group_width // DH
    seq_count = lax.axis_size("seq")
    quarters = seq_count // heads_local
    part_rows = slots // quarters
    me = lax.axis_index("seq")
    my_quarter = (me % quarters).astype(jnp.int32)[None]

    kept = kept_token_indices[0]
    dealt = kept.reshape(part_rows // GROUP, quarters, GROUP).transpose(1, 0, 2)
    dealt = lax.dynamic_slice_in_dim(
        jnp.concatenate([dealt, dealt], axis=0), me % quarters, quarters, axis=0
    ).reshape(slots)
    token = jnp.arange(tok_dev, dtype=jnp.int32)[None, :]
    selector = (kept[:, None] == token).astype(jnp.bfloat16)
    dealt_selector = (dealt[:, None] == token).astype(jnp.bfloat16)

    def pick(which, values):
        return jnp.dot(which, values, preferred_element_type=jnp.float32).astype(jnp.bfloat16)

    grad_local = pick(dealt_selector, output_gradient)
    query = pick(dealt_selector, projections[:, 0])
    key = pick(selector, projections[:, 1])
    value = pick(selector, projections[:, 2])

    *blocks, query_in, grad_in, key_in, value_in = spread(
        grad_local, query, key, value, output_projection_weight, seq_count
    )

    def along_z(k):
        if k == 0:
            return blocks[0]
        return lax.ppermute(
            blocks[k], "seq", [(i, (i + 8 * k) % seq_count) for i in range(seq_count)]
        )

    grad_parts = [along_z(k) for k in range(4)]
    dq_back, o_back, key_back = attend(
        surviving_token_count, my_quarter, query_in, grad_in, key_in, value_in
    )
    out_rows = output_projection_weight.shape[0] // seq_count
    grad_query, grad_key, grad_value, weight_grad = bring_home(
        o_back, dq_back, key_back, grad_parts, out_rows
    )
    projection_grad = jnp.stack(
        [
            contract_rows(dealt_selector, grad_query).astype(jnp.bfloat16),
            contract_rows(selector, grad_key).astype(jnp.bfloat16),
            contract_rows(selector, grad_value).astype(jnp.bfloat16),
        ],
        axis=1,
    )
    return (projection_grad, weight_grad)


def solution(mesh):
    return jax.shard_map(
        on_device,
        mesh=mesh,
        in_specs=(P("seq", None, "head"), P("seq", "head"), P(None, "head"), P("seq", None), P()),
        out_specs=(P("seq", None, "head"), P("seq", "head")),
        check_vma=False,
    )
```

```python
import math

import jax
import jax.numpy as jnp
from jax import lax
from jax.experimental import pallas as pl
from jax.experimental.pallas import tpu as pltpu
from jax.sharding import PartitionSpec as P

DH = 128
BQ = 256
BK = 1536
GROUP = 16
NEG = -1e30
CHUNKS = 4
K_STEP = 4
DQ_STEP = 4


def contract_rows(left, right):
    return lax.dot_general(
        left, right, (((0,), (0,)), ((), ())), preferred_element_type=jnp.float32
    )


def attend_kernel(
    count_ref,
    quarter_ref,
    q_hbm,
    g_hbm,
    k_hbm,
    v_hbm,
    dq_out,
    o_out,
    k_out,
    q_ref,
    g_ref,
    k_ref,
    v_ref,
    k_stage,
    qc,
    gc,
    kc,
    vc,
    k_turned,
    v_turned,
    q_turned,
    dkc,
    dvc,
    oc,
    s_scr,
    p_scr,
    qpos,
    acc,
    group_pos,
    load_sem,
    store_sem,
):
    shards, part_rows, _ = q_ref.shape
    slots = k_ref.shape[1]
    quarter = quarter_ref[0]
    groups = part_rows // GROUP
    score_scale = 1.0 / math.sqrt(DH)
    log2e = score_scale * math.log2(math.e)
    bf16 = jnp.bfloat16
    loads = [
        pltpu.make_async_copy(src, dst, load_sem.at[i])
        for i, (src, dst) in enumerate(
            ((q_hbm, q_ref), (g_hbm, g_ref), (k_hbm, k_ref), (v_hbm, v_ref))
        )
    ]
    for load in loads:
        load.start()

    def clear(i, carry):
        rows = pl.ds(pl.multiple_of(i * slots, slots), slots)
        dkc[rows, :] = jnp.zeros((slots, DH), jnp.float32)
        dvc[rows, :] = jnp.zeros((slots, DH), jnp.float32)
        return carry

    lax.fori_loop(0, shards, clear, 0)
    q_turned[DH:, :] = jnp.where(
        lax.broadcasted_iota(jnp.int32, (DH, BQ), 0) == 0, 1.0, 0.0
    ).astype(bf16)
    for load in loads:
        load.wait()

    def dead_marks(rows, live):
        row = lax.broadcasted_iota(jnp.int32, (rows, DH), 0)
        lane = lax.broadcasted_iota(jnp.int32, (rows, DH), 1)
        return jnp.where((row >= live) & (lane == 0), NEG, 0.0).astype(bf16)

    def pack(s, carry):
        at_k, at_q = carry
        live = (count_ref[s] + GROUP - 1) // GROUP
        first = lax.rem(quarter + s, 4)
        at_k = pl.multiple_of(at_k, GROUP)
        at_q = pl.multiple_of(at_q, GROUP)
        kc[pl.ds(at_k, slots), :DH] = k_ref[s]
        kc[pl.ds(at_k, slots), DH:] = dead_marks(slots, count_ref[s])
        vc[pl.ds(at_k, slots), :] = v_ref[s]
        qc[pl.ds(at_q, part_rows), :] = q_ref[s]
        gc[pl.ds(at_q, part_rows), :] = g_ref[s]
        rows = lax.broadcasted_iota(jnp.int32, (GROUP, DH), 0)
        for i in range(groups):
            base = at_k + (first + 4 * i) * GROUP
            qpos[pl.ds(at_q + i * GROUP, GROUP), :] = base + rows
            group_pos[at_q // GROUP + i] = base
        return at_k + live * GROUP, at_q + (live - first + 3) // 4 * GROUP

    end_k, end_q = lax.fori_loop(0, shards, pack, (jnp.int32(0), jnp.int32(0)))
    end_k = pl.multiple_of(end_k, GROUP)
    end_q = pl.multiple_of(end_q, GROUP)
    kc[pl.ds(end_k, BK), :DH] = jnp.zeros((BK, DH), bf16)
    kc[pl.ds(end_k, BK), DH:] = dead_marks(BK, 0)
    vc[pl.ds(end_k, BK), :] = jnp.zeros((BK, DH), bf16)
    qc[pl.ds(end_q, BQ), :] = jnp.zeros((BQ, DH), bf16)
    gc[pl.ds(end_q, BQ), :] = jnp.zeros((BQ, DH), bf16)
    qpos[pl.ds(end_q, BQ), :] = jnp.zeros((BQ, DH), jnp.int32)
    blocks = (end_q + BQ - 1) // BQ
    oc[pl.ds(pl.multiple_of(blocks * BQ, BQ), part_rows), :] = jnp.zeros(
        (part_rows, 2 * DH), bf16
    )

    def turn(c, carry):
        keys = pl.ds(pl.multiple_of(c * BK, BK), BK)
        k_turned[:, keys] = kc[keys, :DH].T
        v_turned[:, keys] = vc[keys, :].T
        return carry

    lax.fori_loop(0, (end_k + BK - 1) // BK, turn, 0)

    def block(b, carry):
        rows = pl.ds(pl.multiple_of(b * BQ, BQ), BQ)
        last_group = jnp.minimum((b + 1) * (BQ // GROUP), end_q // GROUP) - 1
        chunks = (group_pos[last_group] + GROUP + BK - 1) // BK
        clear_chunks = (group_pos[b * (BQ // GROUP)] + 1) // BK
        q_turned[:DH, :] = qc[rows, :].T
        last_key = qpos[rows, :].T[0:1, :]

        def score(c, top, masked):
            at = pl.multiple_of(c * BK, BK)
            keys = pl.ds(at, BK)
            s = jnp.dot(kc[keys, :], q_turned[...], preferred_element_type=jnp.float32)
            if masked:
                key = at + lax.broadcasted_iota(jnp.int32, (BK, BQ), 0)
                s = jnp.where(key <= last_key, s, NEG)
            s_scr[keys, :] = s
            return jnp.maximum(top, jnp.max(s, axis=0, keepdims=True))

        top = jnp.full((1, BQ), NEG, jnp.float32)
        top = lax.fori_loop(0, clear_chunks, lambda c, t: score(c, t, False), top)
        top = lax.fori_loop(clear_chunks, chunks, lambda c, t: score(c, t, True), top)
        acc[...] = jnp.zeros((DH, BQ), jnp.float32)

        def weigh(c, total):
            keys = pl.ds(pl.multiple_of(c * BK, BK), BK)
            p = jnp.exp2((s_scr[keys, :] - top) * log2e)
            p_low = p.astype(bf16)
            p_scr[keys, :] = p_low
            acc[...] += jnp.dot(v_turned[:, keys], p_low, preferred_element_type=jnp.float32)
            return total + jnp.sum(p, axis=0, keepdims=True)

        total = lax.fori_loop(0, chunks, weigh, jnp.zeros((1, BQ), jnp.float32))
        inverse = 1.0 / total
        attended = acc[...] * inverse
        oc[rows, DH:] = attended.T.astype(bf16)
        g_turned = (gc[rows, :].astype(jnp.float32).T * inverse).astype(bf16)
        row_dot = jnp.sum(g_turned.astype(jnp.float32) * attended, axis=0, keepdims=True)
        g_part = g_turned.T
        acc[...] = jnp.zeros((DH, BQ), jnp.float32)

        def back(c, carry):
            keys = pl.ds(pl.multiple_of(c * BK, BK), BK)
            p_low = p_scr[keys, :]
            grad_probs = jnp.dot(vc[keys, :], g_turned, preferred_element_type=jnp.float32)
            ds = (p_low.astype(jnp.float32) * (grad_probs - row_dot)).astype(bf16)
            acc[...] += jnp.dot(k_turned[:, keys], ds, preferred_element_type=jnp.float32)
            dkc[keys, :] += jnp.dot(ds, qc[rows, :], preferred_element_type=jnp.float32)
            dvc[keys, :] += jnp.dot(p_low, g_part, preferred_element_type=jnp.float32)
            return carry

        lax.fori_loop(0, chunks, back, 0)
        oc[rows, :DH] = (acc[...] * score_scale).T.astype(bf16)
        return carry

    lax.fori_loop(0, blocks, block, 0)

    def unpack(s, carry):
        at_k, at_q = carry
        live = (count_ref[s] + GROUP - 1) // GROUP
        first = lax.rem(quarter + s, 4)
        at_k = pl.multiple_of(at_k, GROUP)
        at_q = pl.multiple_of(at_q, GROUP)
        q_ref[s] = oc[pl.ds(at_q, part_rows), :DH]
        g_ref[s] = oc[pl.ds(at_q, part_rows), DH:]
        k_stage[s, :, :DH] = (dkc[pl.ds(at_k, slots), :] * score_scale).astype(bf16)
        k_stage[s, :, DH:] = dvc[pl.ds(at_k, slots), :].astype(bf16)
        pltpu.make_async_copy(k_stage.at[s], k_out.at[s], store_sem.at[0]).start()
        return at_k + live * GROUP, at_q + (live - first + 3) // 4 * GROUP

    lax.fori_loop(0, shards, unpack, (jnp.int32(0), jnp.int32(0)))
    stores = [
        pltpu.make_async_copy(q_ref, dq_out, store_sem.at[1]),
        pltpu.make_async_copy(g_ref, o_out, store_sem.at[2]),
    ]
    for store in stores:
        store.start()
    pltpu.make_async_copy(k_stage, k_out, store_sem.at[0]).wait()
    for store in stores:
        store.wait()


def attend(counts, quarter, query_in, grad_in, key_in, value_in):
    shards, part_rows, _ = query_in.shape
    slots = key_in.shape[1]
    keys = shards * slots
    queries = shards * part_rows
    bf16 = jnp.bfloat16
    smem = pl.BlockSpec(memory_space=pltpu.SMEM)
    hbm = pl.BlockSpec(memory_space=pltpu.HBM)
    return pl.pallas_call(
        attend_kernel,
        out_shape=(
            jax.ShapeDtypeStruct((shards, part_rows, DH), bf16),
            jax.ShapeDtypeStruct((shards, part_rows, DH), bf16),
            jax.ShapeDtypeStruct((shards, slots, 2 * DH), bf16),
        ),
        in_specs=[smem, smem, hbm, hbm, hbm, hbm],
        out_specs=(hbm, hbm, hbm),
        scratch_shapes=[
            pltpu.VMEM((shards, part_rows, DH), bf16),
            pltpu.VMEM((shards, part_rows, DH), bf16),
            pltpu.VMEM((shards, slots, DH), bf16),
            pltpu.VMEM((shards, slots, DH), bf16),
            pltpu.VMEM((shards, slots, 2 * DH), bf16),
            pltpu.VMEM((queries + BQ, DH), bf16),
            pltpu.VMEM((queries + BQ, DH), bf16),
            pltpu.VMEM((keys + BK, 2 * DH), bf16),
            pltpu.VMEM((keys + BK, DH), bf16),
            pltpu.VMEM((DH, keys), bf16),
            pltpu.VMEM((DH, keys), bf16),
            pltpu.VMEM((2 * DH, BQ), bf16),
            pltpu.VMEM((keys, DH), jnp.float32),
            pltpu.VMEM((keys, DH), jnp.float32),
            pltpu.VMEM((queries + BQ, 2 * DH), bf16),
            pltpu.VMEM((keys, BQ), jnp.float32),
            pltpu.VMEM((keys, BQ), bf16),
            pltpu.VMEM((queries + BQ, DH), jnp.int32),
            pltpu.VMEM((DH, BQ), jnp.float32),
            pltpu.SMEM((queries // GROUP + 8,), jnp.int32),
            pltpu.SemaphoreType.DMA((4,)),
            pltpu.SemaphoreType.DMA((3,)),
        ],
        compiler_params=pltpu.CompilerParams(vmem_limit_bytes=52 * 1024 * 1024),
        cost_estimate=pl.CostEstimate(
            flops=6 * queries * keys * DH, bytes_accessed=16 * 1024 * 1024, transcendentals=0
        ),
        name="attend",
    )(counts, quarter, query_in, grad_in, key_in, value_in)


def block_bytes_wait(ref, sem):
    pltpu.make_async_copy(ref, ref, sem).wait()


def greet(peers, peer_of, ring=0):
    barrier = pltpu.get_barrier_semaphore()

    def signal(k, carry):
        pl.semaphore_signal(
            barrier, inc=1, device_id={"seq": peer_of(k)}, device_id_type=pl.DeviceIdType.MESH
        )
        return carry

    lax.fori_loop(1, peers + 1, signal, 0)
    if ring:
        row = lax.axis_index("head")
        for k in range(1, ring):
            pl.semaphore_signal(
                barrier,
                inc=1,
                device_id={"head": lax.rem(row + k, ring)},
                device_id_type=pl.DeviceIdType.MESH,
            )
        peers = peers + ring - 1
    pl.semaphore_wait(barrier, peers)


def send(src, dst, send_sem, recv_sem, target, axis="seq"):
    copy = pltpu.make_async_remote_copy(
        src_ref=src,
        dst_ref=dst,
        send_sem=send_sem,
        recv_sem=recv_sem,
        device_id={axis: target},
        device_id_type=pl.DeviceIdType.MESH,
    )
    copy.start()
    return copy


def spread_kernel(
    grad_ref,
    q_ref,
    k_ref,
    v_ref,
    w_hbm,
    g0_out,
    g1_out,
    g2_out,
    g3_out,
    q_in,
    g_in,
    k_in,
    v_in,
    w_ref,
    acc,
    g_local,
    gblk,
    k_col,
    v_col,
    w_sem,
    copy_sem,
    y_send,
    y_recv,
    z_send,
    z_recv,
    x_send,
    x_recv,
    own_sem,
    pass_send,
    pass_recv,
    q_send,
    q_recv,
    q_own,
):
    shards, part_rows, _ = q_in.shape
    slots, cols = grad_ref.shape
    half = cols // 2
    me = lax.axis_index("seq")
    row = lax.axis_index("head")
    core = me % 2
    sibling = me + 1 - 2 * core
    my_z = me // 8
    my_x = me // 2 % 4
    my_head = me // 4
    my_rows = pl.ds(pl.multiple_of((me % 4) * part_rows, GROUP), part_rows)

    load_w = pltpu.make_async_copy(w_hbm, w_ref, w_sem)
    load_w.start()
    greet(shards - 1, lambda k: lax.rem(me + k, shards), 4)

    def head_cols(head):
        return pl.ds(pl.multiple_of(head * DH, DH), DH)

    def pair_cols(z):
        return pl.ds(pl.multiple_of(z * 2 * DH, 2 * DH), 2 * DH)

    def slot_of(y):
        return lax.rem(y - my_z + 4, 4)

    right, left, across = lax.rem(row + 1, 4), lax.rem(row + 3, 4), lax.rem(row + 2, 4)
    to_right = send(grad_ref, gblk.at[slot_of(row)], y_send.at[0], y_recv.at[0], right, "head")
    to_left = send(grad_ref, gblk.at[slot_of(row)], y_send.at[1], y_recv.at[1], left, "head")

    sides = ((k_ref, k_col, k_in), (v_ref, v_col, v_in))
    for k in (1, 3, 2):
        target = lax.rem(me + 8 * k, shards)
        for i, (src, col, _) in enumerate(sides):
            send(
                src.at[:, pair_cols(lax.rem(my_z + k, 4))],
                col.at[my_z],
                z_send.at[i],
                z_recv.at[i, k],
                target,
            )

    def fan(k):
        z = lax.rem(my_z - k + 4, 4)
        for i, (src, col, out) in enumerate(sides):
            if k:
                block_bytes_wait(col.at[z], z_recv.at[i, k])
            else:
                col[z] = src[:, pair_cols(my_z)]
            for d in (1, 3, 2):
                x = lax.rem(my_x + d, 4)
                send(
                    col.at[z, :, head_cols(x // 2)],
                    out.at[z, my_x, core],
                    x_send.at[i],
                    x_recv.at[i, k],
                    me + 2 * (x - my_x),
                )
            pltpu.make_async_copy(
                col.at[z, :, head_cols(my_x // 2)], out.at[z, my_x, core], own_sem.at[i, k]
            ).start()

    def pass_on(k):
        z = lax.rem(my_z - k + 4, 4)
        for i, (_, _, out) in enumerate(sides):
            block_bytes_wait(out.at[z, pl.ds(0, 3), core], x_recv.at[i, k])
            block_bytes_wait(out.at[z, my_x, core], own_sem.at[i, k])
            send(out.at[z, :, core], out.at[z, :, core], pass_send.at[i], pass_recv.at[i], sibling)

    fan(0)

    def send_q(k, carry):
        t = lax.rem(me + k, shards)
        rows = pl.ds(pl.multiple_of((t % 4) * part_rows, GROUP), part_rows)
        send(q_ref.at[rows, head_cols(t // 4)], q_in.at[me], q_send.at[0], q_recv.at[0], t)
        return carry

    lax.fori_loop(1, shards, send_q, 0)
    own_q = pltpu.make_async_copy(q_ref.at[my_rows, head_cols(my_head)], q_in.at[me], q_own.at[0])
    own_q.start()

    width = 256
    tiles = acc.shape[1] // width
    gblk[slot_of(row)] = grad_ref[...]
    load_w.wait()

    def multiply(y, first):
        def tile(j, carry):
            at = pl.ds(pl.multiple_of(j * width, width), width)
            rows = pl.ds(pl.multiple_of(y * cols, width), cols)
            part = jnp.dot(gblk[slot_of(y)], w_ref[rows, at], preferred_element_type=jnp.float32)
            acc[:, at] = part if first else acc[:, at] + part
            return carry

        lax.fori_loop(0, tiles, tile, 0)

    multiply(row, True)
    for k in (1, 3, 2):
        fan(k)
    to_right.wait_recv()
    from_left = gblk.at[slot_of(left), :, pl.ds(0, half)]
    on_right = send(from_left, from_left, y_send.at[2], y_recv.at[2], right, "head")
    to_left.wait_recv()
    from_right = gblk.at[slot_of(right), :, pl.ds(half, half)]
    on_left = send(from_right, from_right, y_send.at[3], y_recv.at[3], left, "head")
    pass_on(0)
    multiply(left, False)
    pass_on(1)
    multiply(right, False)
    pass_on(3)
    on_right.wait_recv()
    on_left.wait_recv()

    def finish(step, carry):
        j = lax.rem(my_head // 2 + step, tiles)
        at = pl.ds(pl.multiple_of(j * width, width), width)
        rows = pl.ds(pl.multiple_of(across * cols, width), cols)
        part = jnp.dot(gblk[slot_of(across)], w_ref[rows, at], preferred_element_type=jnp.float32)
        g_local[:, at] = (acc[:, at] + part).astype(jnp.bfloat16)
        for i in range(8):
            t = j * 8 + i
            part_at = (i % 4) * part_rows

            @pl.when(t != me)
            def _():
                send(
                    g_local.at[pl.ds(part_at, part_rows), head_cols(t // 4)],
                    g_in.at[me],
                    q_send.at[1],
                    q_recv.at[1],
                    t,
                )

        return carry

    lax.fori_loop(0, tiles, finish, 0)
    own_g = pltpu.make_async_copy(
        g_local.at[my_rows, head_cols(my_head)], g_in.at[me], q_own.at[1]
    )
    own_g.start()
    copies = [
        pltpu.make_async_copy(gblk.at[k], out, copy_sem.at[k])
        for k, out in enumerate((g0_out, g1_out, g2_out, g3_out))
    ]
    for copy in copies:
        copy.start()
    pass_on(2)
    for copy in copies:
        copy.wait()
    own_q.wait()
    own_g.wait()

    others = pl.ds(0, shards - 1)
    block_bytes_wait(q_in.at[others], q_recv.at[0])
    block_bytes_wait(q_in.at[others], q_send.at[0])
    for i, (_, col, out) in enumerate(sides):
        block_bytes_wait(out.at[:, :, core], pass_recv.at[i])
        block_bytes_wait(out.at[:, :, core], pass_send.at[i])
        block_bytes_wait(col.at[pl.ds(0, 3)], z_send.at[i])
        block_bytes_wait(out.at[:, pl.ds(0, 3), core], x_send.at[i])
    for copy in (to_right, to_left, on_right, on_left):
        copy.wait_send()
    block_bytes_wait(g_in.at[others], q_recv.at[1])
    block_bytes_wait(g_in.at[others], q_send.at[1])


def spread(grad_local, query, key, value, weight, shards):
    slots, cols = grad_local.shape
    depth, width = weight.shape
    part_rows = slots // 4
    bf16 = jnp.bfloat16
    vmem = pl.BlockSpec(memory_space=pltpu.VMEM)
    block = jax.ShapeDtypeStruct((slots, cols), bf16)
    small = jax.ShapeDtypeStruct((shards, part_rows, DH), bf16)
    large = jax.ShapeDtypeStruct((4, 4, 2, slots, DH), bf16)
    *blocks, query_in, grad_in, key_in, value_in = pl.pallas_call(
        spread_kernel,
        out_shape=(block,) * 4 + (small,) * 2 + (large,) * 2,
        in_specs=[vmem] * 4 + [pl.BlockSpec(memory_space=pl.ANY)],
        out_specs=(pl.BlockSpec(memory_space=pltpu.HBM),) * 8,
        scratch_shapes=[
            pltpu.VMEM((depth, width), bf16),
            pltpu.VMEM((slots, width), jnp.float32),
            pltpu.VMEM((slots, width), bf16),
            pltpu.VMEM((4, slots, cols), bf16),
            pltpu.VMEM((4, slots, 2 * DH), bf16),
            pltpu.VMEM((4, slots, 2 * DH), bf16),
            pltpu.SemaphoreType.DMA,
            pltpu.SemaphoreType.DMA((4,)),
            pltpu.SemaphoreType.DMA((4,)),
            pltpu.SemaphoreType.DMA((4,)),
            pltpu.SemaphoreType.DMA((2,)),
            pltpu.SemaphoreType.DMA((2, 4)),
            pltpu.SemaphoreType.DMA((2,)),
            pltpu.SemaphoreType.DMA((2, 4)),
            pltpu.SemaphoreType.DMA((2, 4)),
            pltpu.SemaphoreType.DMA((2,)),
            pltpu.SemaphoreType.DMA((2,)),
            pltpu.SemaphoreType.DMA((2,)),
            pltpu.SemaphoreType.DMA((2,)),
            pltpu.SemaphoreType.DMA((2,)),
        ],
        compiler_params=pltpu.CompilerParams(
            collective_id=2, has_side_effects=True, vmem_limit_bytes=48 * 1024 * 1024
        ),
        name="spread",
    )(grad_local, query, key, value, weight)
    key_in = key_in.reshape(shards, slots, DH)
    value_in = value_in.reshape(shards, slots, DH)
    return (*blocks, query_in, grad_in, key_in, value_in)


def home_kernel(
    o_ref,
    dq_ref,
    k_ref,
    g0_ref,
    g1_ref,
    g2_ref,
    g3_ref,
    dq_home,
    gk_home,
    gv_home,
    wg_out,
    g_vmem,
    k_own,
    g_turned,
    oz,
    kx,
    ks,
    k_row,
    k_pair,
    k_col,
    part,
    px,
    half_send,
    half_recv,
    full_send,
    full_recv,
    send_sem,
    recv_sem,
    load_sem,
    k_send,
    k_recv,
    z_send,
    z_recv,
    p_send,
    p_recv,
    x_send,
    x_recv,
):
    shards, part_rows, _ = o_ref.shape
    slots = k_ref.shape[3]
    me = lax.axis_index("seq")
    core = me % 2
    sibling = me + 1 - 2 * core
    plane_x = me // 2 % 4
    my_z = me // 8
    out_rows, width = wg_out.shape
    my_rows = pl.ds(pl.multiple_of((me % 4) * part_rows, GROUP), part_rows)
    my_cols = pl.ds(pl.multiple_of((me // 4) * DH, DH), DH)
    f32, bf16 = jnp.float32, jnp.bfloat16

    loads = [
        pltpu.make_async_copy(src, dst, load_sem.at[i])
        for i, (src, dst) in enumerate(
            (
                (o_ref.at[me], oz.at[0, my_rows, my_cols]),
                (g0_ref, g_vmem.at[0]),
                (g1_ref, g_vmem.at[1]),
                (g2_ref, g_vmem.at[2]),
                (g3_ref, g_vmem.at[3]),
                (k_ref.at[:, :, core], k_own),
                (dq_ref.at[me], dq_home.at[my_rows, my_cols]),
            )
        )
    ]
    for load in loads:
        load.start()
    greet(shards - 1, lambda k: lax.rem(me + k, shards))

    def send_o(k, carry):
        t = lax.rem(me + k, shards)
        send(o_ref.at[t], oz.at[0, my_rows, my_cols], send_sem.at[0], recv_sem.at[0], t)
        return carry

    lax.fori_loop(1, shards, send_o, 0)
    swap = send(k_ref.at[:, :, 1 - core], kx, send_sem.at[1], recv_sem.at[1], sibling)
    for load in loads:
        load.wait()

    tile = 256

    def turn(j, carry):
        cols = pl.ds(pl.multiple_of(j * tile, tile), tile)
        for k in range(4):
            g_turned[k, cols, :] = g_vmem[k, :, cols].T
        return carry

    lax.fori_loop(0, part.shape[0] // tile, turn, 0)
    block_bytes_wait(o_ref.at[pl.ds(0, shards - 1)], recv_sem.at[0])

    chunk = width // CHUNKS
    z_up, z_down = lax.rem(me + 8, shards), lax.rem(me + 24, shards)
    x_up = me + 2 * (lax.rem(plane_x + 1, 4) - plane_x)
    x_down = me + 2 * (lax.rem(plane_x + 3, 4) - plane_x)
    upper, lower = pl.ds(0, slots // 2), pl.ds(slots // 2, slots // 2)
    top, bottom = pl.ds(0, out_rows // 2), pl.ds(out_rows // 2, out_rows // 2)

    def cols_of(c):
        return pl.ds(c * chunk, chunk)

    def start_z(c):
        own = oz.at[0, :, cols_of(c)]
        send(own, oz.at[1, :, cols_of(c)], z_send.at[0], z_recv.at[0, c], z_up)
        send(own, oz.at[3, :, cols_of(c)], z_send.at[1], z_recv.at[1, c], z_down)

    def forward_z(c):
        cols = cols_of(c)
        block_bytes_wait(oz.at[1, :, cols], z_recv.at[0, c])
        send(
            oz.at[1, upper, cols], oz.at[2, upper, cols], z_send.at[2], z_recv.at[2, c], z_up
        )
        block_bytes_wait(oz.at[3, :, cols], z_recv.at[1, c])
        send(
            oz.at[3, lower, cols], oz.at[2, lower, cols], z_send.at[3], z_recv.at[3, c], z_down
        )
        if c + 2 < CHUNKS:
            start_z(c + 2)

    def piece(x, c):
        return pl.ds(pl.multiple_of((2 * x + c) * out_rows, 32), out_rows)

    def product(c):
        cols = cols_of(c)
        block_bytes_wait(oz.at[2, upper, cols], z_recv.at[2, c])
        block_bytes_wait(oz.at[2, lower, cols], z_recv.at[3, c])

        def rows_tile(j, carry):
            rows = pl.ds(pl.multiple_of(j * tile, tile), tile)
            total = jnp.dot(g_turned[0, rows, :], oz[0, :, cols], preferred_element_type=f32)
            for k in (1, 2, 3):
                total += jnp.dot(g_turned[k, rows, :], oz[k, :, cols], preferred_element_type=f32)
            part[rows, cols] = total.astype(bf16)
            return carry

        lax.fori_loop(0, part.shape[0] // tile, rows_tile, 0)
        for x in range(4):
            send(
                part.at[piece(x, 1 - core), cols],
                px.at[x, :, cols],
                p_send,
                p_recv.at[c],
                sibling,
            )

    def pair_sum(x, c):
        cols = cols_of(c)
        return part[piece(x, core), cols].astype(f32) + px[x, :, cols].astype(f32)

    def send_half(c):
        cols = cols_of(c)
        block_bytes_wait(px.at[:, :, cols], p_recv.at[c])
        half_send[:, cols] = pair_sum(lax.rem(plane_x + 2, 4), c).astype(bf16)
        send(
            half_send.at[top, cols], half_recv.at[top, cols], x_send.at[0], x_recv.at[0, c], x_up
        )
        send(
            half_send.at[bottom, cols],
            half_recv.at[bottom, cols],
            x_send.at[1],
            x_recv.at[1, c],
            x_down,
        )

    def send_full(c):
        cols = cols_of(c)
        split = out_rows // 2
        block_bytes_wait(half_recv.at[top, cols], x_recv.at[0, c])
        ahead = pair_sum(lax.rem(plane_x + 1, 4), c)
        full_send[0, top, cols] = (ahead[:split] + half_recv[top, cols].astype(f32)).astype(bf16)
        full_send[0, bottom, cols] = ahead[split:].astype(bf16)
        send(
            full_send.at[0, :, cols], full_recv.at[0, :, cols], x_send.at[2], x_recv.at[2, c], x_up
        )
        block_bytes_wait(half_recv.at[bottom, cols], x_recv.at[1, c])
        behind = pair_sum(lax.rem(plane_x + 3, 4), c)
        full_send[1, top, cols] = behind[:split].astype(bf16)
        full_send[1, bottom, cols] = (behind[split:] + half_recv[bottom, cols].astype(f32)).astype(
            bf16
        )
        send(
            full_send.at[1, :, cols],
            full_recv.at[1, :, cols],
            x_send.at[3],
            x_recv.at[3, c],
            x_down,
        )

    def finish(c):
        cols = cols_of(c)
        block_bytes_wait(full_recv.at[0, :, cols], x_recv.at[2, c])
        block_bytes_wait(full_recv.at[1, :, cols], x_recv.at[3, c])
        wg_out[:, cols] = (
            pair_sum(plane_x, c)
            + full_recv[0, :, cols].astype(f32)
            + full_recv[1, :, cols].astype(f32)
        )

    def k_sum(z, x):
        return (k_own[z, x].astype(f32) + kx[z, x].astype(f32)).astype(bf16)

    def k_along_x():
        for k in (1, 2, 3):
            x = lax.rem(plane_x + k, 4)
            for z in range(4):
                ks[z, x] = k_sum(z, x)
            send(
                ks.at[:, x],
                k_row.at[plane_x],
                k_send.at[k - 1],
                k_recv.at[k - 1],
                me + 2 * (x - plane_x),
            )
        for z in range(4):
            k_row[plane_x, z] = k_sum(z, plane_x)

    def k_along_z():
        for k in range(3):
            block_bytes_wait(k_row.at[0], k_recv.at[k])
        for k in (1, 2, 3, 0):
            z = lax.rem(my_z + k, 4)
            for h in range(2):
                pair = k_row[2 * h, z].astype(f32) + k_row[2 * h + 1, z].astype(f32)
                k_pair[z, h] = pair.astype(bf16)
            if k:
                send(
                    k_pair.at[z],
                    k_col.at[my_z],
                    k_send.at[2 + k],
                    k_recv.at[2 + k],
                    lax.rem(me + 8 * k, shards),
                )
            else:
                k_col[my_z] = k_pair[z]

    def send_dq(k, carry):
        t = lax.rem(me + k, shards)
        send(dq_ref.at[t], dq_home.at[my_rows, my_cols], send_sem.at[3], recv_sem.at[3], t)
        return carry

    start_z(0)
    start_z(1)
    swap.wait()
    k_along_x()
    stages = (forward_z, product, send_half, send_full, finish)
    for step in range(CHUNKS + len(stages) - 1):
        if step == K_STEP:
            k_along_z()
        if step == DQ_STEP:
            lax.fori_loop(1, shards, send_dq, 0)
        for i, stage in enumerate(stages):
            if 0 <= step - i < CHUNKS:
                stage(step - i)
    for k in range(3):
        block_bytes_wait(k_col.at[0], k_recv.at[3 + k])
    for z in range(4):
        for h in range(2):
            cols = pl.ds((2 * z + h) * DH, DH)
            gk_home[:, cols] = k_col[z, h, :, :DH]
            gv_home[:, cols] = k_col[z, h, :, DH:]
    block_bytes_wait(dq_ref.at[pl.ds(0, shards - 1)], recv_sem.at[3])
    block_bytes_wait(o_ref.at[pl.ds(0, shards - 1)], send_sem.at[0])
    for k in range(3):
        block_bytes_wait(ks.at[:, 0], k_send.at[k])
        block_bytes_wait(k_pair.at[0], k_send.at[3 + k])
    block_bytes_wait(dq_ref.at[pl.ds(0, shards - 1)], send_sem.at[3])
    block_bytes_wait(oz.at[0], z_send.at[0])
    block_bytes_wait(oz.at[0], z_send.at[1])
    block_bytes_wait(oz.at[1, upper], z_send.at[2])
    block_bytes_wait(oz.at[3, lower], z_send.at[3])
    block_bytes_wait(px, p_send)
    block_bytes_wait(half_send.at[top], x_send.at[0])
    block_bytes_wait(half_send.at[bottom], x_send.at[1])
    block_bytes_wait(full_send.at[0], x_send.at[2])
    block_bytes_wait(full_send.at[1], x_send.at[3])


def bring_home(o_back, dq_back, key_back, grad_parts, out_rows):
    shards, part_rows, _ = o_back.shape
    slots = key_back.shape[1]
    width = shards // 4 * DH
    rows = grad_parts[0].shape[1]
    key_back = key_back.reshape(4, 4, 2, slots, 2 * DH)
    vmem = pl.BlockSpec(memory_space=pltpu.VMEM)
    bf16 = jnp.bfloat16
    return pl.pallas_call(
        home_kernel,
        out_shape=(
            jax.ShapeDtypeStruct((slots, width), bf16),
            jax.ShapeDtypeStruct((slots, width), bf16),
            jax.ShapeDtypeStruct((slots, width), bf16),
            jax.ShapeDtypeStruct((out_rows, width), jnp.float32),
        ),
        in_specs=[pl.BlockSpec(memory_space=pltpu.HBM)] * 7,
        out_specs=(vmem,) * 4,
        scratch_shapes=[
            pltpu.VMEM((4, slots, rows), bf16),
            pltpu.VMEM((4, 4, slots, 2 * DH), bf16),
            pltpu.VMEM((4, rows, slots), bf16),
            pltpu.VMEM((4, slots, width), bf16),
            pltpu.VMEM((4, 4, slots, 2 * DH), bf16),
            pltpu.VMEM((4, 4, slots, 2 * DH), bf16),
            pltpu.VMEM((4, 4, slots, 2 * DH), bf16),
            pltpu.VMEM((4, 2, slots, 2 * DH), bf16),
            pltpu.VMEM((4, 2, slots, 2 * DH), bf16),
            pltpu.VMEM((rows, width), bf16),
            pltpu.VMEM((4, out_rows, width), bf16),
            pltpu.VMEM((out_rows, width), bf16),
            pltpu.VMEM((out_rows, width), bf16),
            pltpu.VMEM((2, out_rows, width), bf16),
            pltpu.VMEM((2, out_rows, width), bf16),
            pltpu.SemaphoreType.DMA((4,)),
            pltpu.SemaphoreType.DMA((4,)),
            pltpu.SemaphoreType.DMA((7,)),
            pltpu.SemaphoreType.DMA((6,)),
            pltpu.SemaphoreType.DMA((6,)),
            pltpu.SemaphoreType.DMA((4,)),
            pltpu.SemaphoreType.DMA((4, CHUNKS)),
            pltpu.SemaphoreType.DMA,
            pltpu.SemaphoreType.DMA((CHUNKS,)),
            pltpu.SemaphoreType.DMA((4,)),
            pltpu.SemaphoreType.DMA((4, CHUNKS)),
        ],
        compiler_params=pltpu.CompilerParams(
            collective_id=1, has_side_effects=True, vmem_limit_bytes=48 * 1024 * 1024
        ),
        name="home",
    )(o_back, dq_back, key_back, *grad_parts)


def on_device(
    projections,
    output_gradient,
    output_projection_weight,
    kept_token_indices,
    surviving_token_count,
):
    tok_dev = projections.shape[0]
    group_width = projections.shape[2]
    slots = kept_token_indices.shape[1]
    heads_local = group_width // DH
    seq_count = lax.axis_size("seq")
    quarters = seq_count // heads_local
    part_rows = slots // quarters
    me = lax.axis_index("seq")
    my_quarter = (me % quarters).astype(jnp.int32)[None]

    kept = kept_token_indices[0]
    dealt = kept.reshape(part_rows // GROUP, quarters, GROUP).transpose(1, 0, 2)
    dealt = lax.dynamic_slice_in_dim(
        jnp.concatenate([dealt, dealt], axis=0), me % quarters, quarters, axis=0
    ).reshape(slots)
    token = jnp.arange(tok_dev, dtype=jnp.int32)[None, :]
    selector = (kept[:, None] == token).astype(jnp.bfloat16)
    dealt_selector = (dealt[:, None] == token).astype(jnp.bfloat16)

    def pick(which, values):
        return jnp.dot(which, values, preferred_element_type=jnp.float32).astype(jnp.bfloat16)

    grad_local = pick(dealt_selector, output_gradient)
    query = pick(dealt_selector, projections[:, 0])
    key = pick(selector, projections[:, 1])
    value = pick(selector, projections[:, 2])

    *blocks, query_in, grad_in, key_in, value_in = spread(
        grad_local, query, key, value, output_projection_weight, seq_count
    )

    def along_z(k):
        if k == 0:
            return blocks[0]
        return lax.ppermute(
            blocks[k], "seq", [(i, (i + 8 * k) % seq_count) for i in range(seq_count)]
        )

    grad_parts = [along_z(k) for k in range(4)]
    dq_back, o_back, key_back = attend(
        surviving_token_count, my_quarter, query_in, grad_in, key_in, value_in
    )
    out_rows = output_projection_weight.shape[0] // seq_count
    grad_query, grad_key, grad_value, weight_grad = bring_home(
        o_back, dq_back, key_back, grad_parts, out_rows
    )
    projection_grad = jnp.stack(
        [
            contract_rows(dealt_selector, grad_query).astype(jnp.bfloat16),
            contract_rows(selector, grad_key).astype(jnp.bfloat16),
            contract_rows(selector, grad_value).astype(jnp.bfloat16),
        ],
        axis=1,
    )
    return (projection_grad, weight_grad)


def solution(mesh):
    return jax.shard_map(
        on_device,
        mesh=mesh,
        in_specs=(P("seq", None, "head"), P("seq", "head"), P(None, "head"), P("seq", None), P()),
        out_specs=(P("seq", None, "head"), P("seq", "head")),
        check_vma=False,
    )
```

```python
import math

import jax
import jax.numpy as jnp
from jax import lax
from jax.experimental import pallas as pl
from jax.experimental.pallas import tpu as pltpu
from jax.sharding import PartitionSpec as P

DH = 128
BQ = 256
BK = 1536
GROUP = 16
NEG = -1e30
CHUNKS = 4
VMEM_BYTES = 60 * 1024 * 1024
K_STEP = 4
DQ_STEP = 4


def contract_rows(left, right):
    return lax.dot_general(
        left, right, (((0,), (0,)), ((), ())), preferred_element_type=jnp.float32
    )


def attend_kernel(
    count_ref,
    quarter_ref,
    q_hbm,
    g_hbm,
    k_hbm,
    v_hbm,
    dq_out,
    o_out,
    k_out,
    q_ref,
    g_ref,
    k_ref,
    v_ref,
    k_stage,
    qc,
    gc,
    kc,
    vc,
    k_turned,
    v_turned,
    q_turned,
    dkc,
    dvc,
    oc,
    s_scr,
    p_scr,
    qpos,
    acc,
    group_pos,
    load_sem,
    store_sem,
):
    shards, part_rows, _ = q_ref.shape
    slots = k_ref.shape[1]
    quarter = quarter_ref[0]
    groups = part_rows // GROUP
    score_scale = 1.0 / math.sqrt(DH)
    log2e = score_scale * math.log2(math.e)
    bf16 = jnp.bfloat16
    loads = [
        pltpu.make_async_copy(src, dst, load_sem.at[i])
        for i, (src, dst) in enumerate(
            ((q_hbm, q_ref), (g_hbm, g_ref), (k_hbm, k_ref), (v_hbm, v_ref))
        )
    ]
    for load in loads:
        load.start()

    def clear(i, carry):
        rows = pl.ds(pl.multiple_of(i * slots, slots), slots)
        dkc[rows, :] = jnp.zeros((slots, DH), jnp.float32)
        dvc[rows, :] = jnp.zeros((slots, DH), jnp.float32)
        return carry

    lax.fori_loop(0, shards, clear, 0)
    q_turned[DH:, :] = jnp.where(
        lax.broadcasted_iota(jnp.int32, (DH, BQ), 0) == 0, 1.0, 0.0
    ).astype(bf16)
    for load in loads:
        load.wait()

    def dead_marks(rows, live):
        row = lax.broadcasted_iota(jnp.int32, (rows, DH), 0)
        lane = lax.broadcasted_iota(jnp.int32, (rows, DH), 1)
        return jnp.where((row >= live) & (lane == 0), NEG, 0.0).astype(bf16)

    def pack(s, carry):
        at_k, at_q = carry
        live = (count_ref[s] + GROUP - 1) // GROUP
        first = lax.rem(quarter + s, 4)
        at_k = pl.multiple_of(at_k, GROUP)
        at_q = pl.multiple_of(at_q, GROUP)
        kc[pl.ds(at_k, slots), :DH] = k_ref[s]
        kc[pl.ds(at_k, slots), DH:] = dead_marks(slots, count_ref[s])
        vc[pl.ds(at_k, slots), :] = v_ref[s]
        qc[pl.ds(at_q, part_rows), :] = q_ref[s]
        gc[pl.ds(at_q, part_rows), :] = g_ref[s]
        rows = lax.broadcasted_iota(jnp.int32, (GROUP, DH), 0)
        for i in range(groups):
            base = at_k + (first + 4 * i) * GROUP
            qpos[pl.ds(at_q + i * GROUP, GROUP), :] = base + rows
            group_pos[at_q // GROUP + i] = base
        return at_k + live * GROUP, at_q + (live - first + 3) // 4 * GROUP

    end_k, end_q = lax.fori_loop(0, shards, pack, (jnp.int32(0), jnp.int32(0)))
    end_k = pl.multiple_of(end_k, GROUP)
    end_q = pl.multiple_of(end_q, GROUP)
    kc[pl.ds(end_k, BK), :DH] = jnp.zeros((BK, DH), bf16)
    kc[pl.ds(end_k, BK), DH:] = dead_marks(BK, 0)
    vc[pl.ds(end_k, BK), :] = jnp.zeros((BK, DH), bf16)
    qc[pl.ds(end_q, BQ), :] = jnp.zeros((BQ, DH), bf16)
    gc[pl.ds(end_q, BQ), :] = jnp.zeros((BQ, DH), bf16)
    qpos[pl.ds(end_q, BQ), :] = jnp.zeros((BQ, DH), jnp.int32)
    blocks = (end_q + BQ - 1) // BQ
    oc[pl.ds(pl.multiple_of(blocks * BQ, BQ), part_rows), :] = jnp.zeros(
        (part_rows, 2 * DH), bf16
    )

    def turn(c, carry):
        keys = pl.ds(pl.multiple_of(c * BK, BK), BK)
        k_turned[:, keys] = kc[keys, :DH].T
        v_turned[:, keys] = vc[keys, :].T
        return carry

    lax.fori_loop(0, (end_k + BK - 1) // BK, turn, 0)

    def block(b, carry):
        rows = pl.ds(pl.multiple_of(b * BQ, BQ), BQ)
        last_group = jnp.minimum((b + 1) * (BQ // GROUP), end_q // GROUP) - 1
        chunks = (group_pos[last_group] + GROUP + BK - 1) // BK
        clear_chunks = (group_pos[b * (BQ // GROUP)] + 1) // BK
        q_turned[:DH, :] = qc[rows, :].T
        last_key = qpos[rows, :].T[0:1, :]

        def score(c, top, masked):
            at = pl.multiple_of(c * BK, BK)
            keys = pl.ds(at, BK)
            s = jnp.dot(kc[keys, :], q_turned[...], preferred_element_type=jnp.float32)
            if masked:
                key = at + lax.broadcasted_iota(jnp.int32, (BK, BQ), 0)
                s = jnp.where(key <= last_key, s, NEG)
            s_scr[keys, :] = s
            return jnp.maximum(top, jnp.max(s, axis=0, keepdims=True))

        top = jnp.full((1, BQ), NEG, jnp.float32)
        top = lax.fori_loop(0, clear_chunks, lambda c, t: score(c, t, False), top)
        top = lax.fori_loop(clear_chunks, chunks, lambda c, t: score(c, t, True), top)
        acc[...] = jnp.zeros((DH, BQ), jnp.float32)

        def weigh(c, total):
            keys = pl.ds(pl.multiple_of(c * BK, BK), BK)
            p = jnp.exp2((s_scr[keys, :] - top) * log2e)
            p_low = p.astype(bf16)
            p_scr[keys, :] = p_low
            acc[...] += jnp.dot(v_turned[:, keys], p_low, preferred_element_type=jnp.float32)
            return total + jnp.sum(p, axis=0, keepdims=True)

        total = lax.fori_loop(0, chunks, weigh, jnp.zeros((1, BQ), jnp.float32))
        inverse = 1.0 / total
        attended = acc[...] * inverse
        oc[rows, DH:] = attended.T.astype(bf16)
        g_turned = (gc[rows, :].astype(jnp.float32).T * inverse).astype(bf16)
        row_dot = jnp.sum(g_turned.astype(jnp.float32) * attended, axis=0, keepdims=True)
        g_part = g_turned.T
        acc[...] = jnp.zeros((DH, BQ), jnp.float32)

        def back(c, carry):
            keys = pl.ds(pl.multiple_of(c * BK, BK), BK)
            p_low = p_scr[keys, :]
            grad_probs = jnp.dot(vc[keys, :], g_turned, preferred_element_type=jnp.float32)
            ds = (p_low.astype(jnp.float32) * (grad_probs - row_dot)).astype(bf16)
            acc[...] += jnp.dot(k_turned[:, keys], ds, preferred_element_type=jnp.float32)
            dkc[keys, :] += jnp.dot(ds, qc[rows, :], preferred_element_type=jnp.float32)
            dvc[keys, :] += jnp.dot(p_low, g_part, preferred_element_type=jnp.float32)
            return carry

        lax.fori_loop(0, chunks, back, 0)
        oc[rows, :DH] = (acc[...] * score_scale).T.astype(bf16)
        return carry

    lax.fori_loop(0, blocks, block, 0)

    def unpack(s, carry):
        at_k, at_q = carry
        live = (count_ref[s] + GROUP - 1) // GROUP
        first = lax.rem(quarter + s, 4)
        at_k = pl.multiple_of(at_k, GROUP)
        at_q = pl.multiple_of(at_q, GROUP)
        q_ref[s] = oc[pl.ds(at_q, part_rows), :DH]
        g_ref[s] = oc[pl.ds(at_q, part_rows), DH:]
        k_stage[s, :, :DH] = (dkc[pl.ds(at_k, slots), :] * score_scale).astype(bf16)
        k_stage[s, :, DH:] = dvc[pl.ds(at_k, slots), :].astype(bf16)
        pltpu.make_async_copy(k_stage.at[s], k_out.at[s], store_sem.at[0]).start()
        return at_k + live * GROUP, at_q + (live - first + 3) // 4 * GROUP

    lax.fori_loop(0, shards, unpack, (jnp.int32(0), jnp.int32(0)))
    stores = [
        pltpu.make_async_copy(q_ref, dq_out, store_sem.at[1]),
        pltpu.make_async_copy(g_ref, o_out, store_sem.at[2]),
    ]
    for store in stores:
        store.start()
    pltpu.make_async_copy(k_stage, k_out, store_sem.at[0]).wait()
    for store in stores:
        store.wait()


def attend(counts, quarter, query_in, grad_in, key_in, value_in):
    shards, part_rows, _ = query_in.shape
    slots = key_in.shape[1]
    keys = shards * slots
    queries = shards * part_rows
    bf16 = jnp.bfloat16
    smem = pl.BlockSpec(memory_space=pltpu.SMEM)
    hbm = pl.BlockSpec(memory_space=pltpu.HBM)
    return pl.pallas_call(
        attend_kernel,
        out_shape=(
            jax.ShapeDtypeStruct((shards, part_rows, DH), bf16),
            jax.ShapeDtypeStruct((shards, part_rows, DH), bf16),
            jax.ShapeDtypeStruct((shards, slots, 2 * DH), bf16),
        ),
        in_specs=[smem, smem, hbm, hbm, hbm, hbm],
        out_specs=(hbm, hbm, hbm),
        scratch_shapes=[
            pltpu.VMEM((shards, part_rows, DH), bf16),
            pltpu.VMEM((shards, part_rows, DH), bf16),
            pltpu.VMEM((shards, slots, DH), bf16),
            pltpu.VMEM((shards, slots, DH), bf16),
            pltpu.VMEM((shards, slots, 2 * DH), bf16),
            pltpu.VMEM((queries + BQ, DH), bf16),
            pltpu.VMEM((queries + BQ, DH), bf16),
            pltpu.VMEM((keys + BK, 2 * DH), bf16),
            pltpu.VMEM((keys + BK, DH), bf16),
            pltpu.VMEM((DH, keys), bf16),
            pltpu.VMEM((DH, keys), bf16),
            pltpu.VMEM((2 * DH, BQ), bf16),
            pltpu.VMEM((keys, DH), jnp.float32),
            pltpu.VMEM((keys, DH), jnp.float32),
            pltpu.VMEM((queries + BQ, 2 * DH), bf16),
            pltpu.VMEM((keys, BQ), jnp.float32),
            pltpu.VMEM((keys, BQ), bf16),
            pltpu.VMEM((queries + BQ, DH), jnp.int32),
            pltpu.VMEM((DH, BQ), jnp.float32),
            pltpu.SMEM((queries // GROUP + 8,), jnp.int32),
            pltpu.SemaphoreType.DMA((4,)),
            pltpu.SemaphoreType.DMA((3,)),
        ],
        compiler_params=pltpu.CompilerParams(vmem_limit_bytes=VMEM_BYTES),
        cost_estimate=pl.CostEstimate(
            flops=6 * queries * keys * DH, bytes_accessed=16 * 1024 * 1024, transcendentals=0
        ),
        name="attend",
    )(counts, quarter, query_in, grad_in, key_in, value_in)


def block_bytes_wait(ref, sem):
    pltpu.make_async_copy(ref, ref, sem).wait()


def greet(peers, peer_of, ring=0, meanwhile=None):
    barrier = pltpu.get_barrier_semaphore()

    def signal(k, carry):
        pl.semaphore_signal(
            barrier, inc=1, device_id={"seq": peer_of(k)}, device_id_type=pl.DeviceIdType.MESH
        )
        return carry

    lax.fori_loop(1, peers + 1, signal, 0)
    if ring:
        row = lax.axis_index("head")
        for k in range(1, ring):
            pl.semaphore_signal(
                barrier,
                inc=1,
                device_id={"head": lax.rem(row + k, ring)},
                device_id_type=pl.DeviceIdType.MESH,
            )
        peers = peers + ring - 1
    if meanwhile is not None:
        meanwhile()
    pl.semaphore_wait(barrier, peers)


def send(src, dst, send_sem, recv_sem, target, axis="seq"):
    copy = pltpu.make_async_remote_copy(
        src_ref=src,
        dst_ref=dst,
        send_sem=send_sem,
        recv_sem=recv_sem,
        device_id={axis: target},
        device_id_type=pl.DeviceIdType.MESH,
    )
    copy.start()
    return copy


def spread_kernel(
    grad_ref,
    dealt_ref,
    select_ref,
    p_hbm,
    w_hbm,
    g0_out,
    g1_out,
    g2_out,
    g3_out,
    q_in,
    g_in,
    k_in,
    v_in,
    w_ref,
    p_ref,
    q_ref,
    k_ref,
    v_ref,
    acc,
    g_local,
    gblk,
    k_col,
    v_col,
    w_sem,
    p_sem,
    copy_sem,
    y_send,
    y_recv,
    z_send,
    z_recv,
    x_send,
    x_recv,
    own_sem,
    pass_send,
    pass_recv,
    q_send,
    q_recv,
    q_own,
):
    shards, part_rows, _ = q_in.shape
    slots, cols = grad_ref.shape
    half = cols // 2
    me = lax.axis_index("seq")
    row = lax.axis_index("head")
    core = me % 2
    sibling = me + 1 - 2 * core
    my_z = me // 8
    my_x = me // 2 % 4
    my_head = me // 4
    my_rows = pl.ds(pl.multiple_of((me % 4) * part_rows, GROUP), part_rows)

    load_w = pltpu.make_async_copy(w_hbm, w_ref, w_sem)
    load_p = pltpu.make_async_copy(p_hbm, p_ref, p_sem)
    load_p.start()
    load_w.start()
    width = 256
    tiles = acc.shape[1] // width

    def pick():
        load_p.wait()

        def tile(j, carry):
            at = pl.ds(pl.multiple_of(j * width, width), width)
            for i, (which, out) in enumerate(
                ((dealt_ref, q_ref), (select_ref, k_ref), (select_ref, v_ref))
            ):
                out[:, at] = jnp.dot(
                    which[...], p_ref[i, :, at], preferred_element_type=jnp.float32
                ).astype(jnp.bfloat16)
            return carry

        lax.fori_loop(0, tiles, tile, 0)

    greet(shards - 1, lambda k: lax.rem(me + k, shards), 4, pick)

    def head_cols(head):
        return pl.ds(pl.multiple_of(head * DH, DH), DH)

    def pair_cols(z):
        return pl.ds(pl.multiple_of(z * 2 * DH, 2 * DH), 2 * DH)

    def slot_of(y):
        return lax.rem(y - my_z + 4, 4)

    right, left, across = lax.rem(row + 1, 4), lax.rem(row + 3, 4), lax.rem(row + 2, 4)
    to_right = send(grad_ref, gblk.at[slot_of(row)], y_send.at[0], y_recv.at[0], right, "head")
    to_left = send(grad_ref, gblk.at[slot_of(row)], y_send.at[1], y_recv.at[1], left, "head")

    sides = ((k_ref, k_col, k_in), (v_ref, v_col, v_in))
    for k in (1, 3, 2):
        target = lax.rem(me + 8 * k, shards)
        for i, (src, col, _) in enumerate(sides):
            send(
                src.at[:, pair_cols(lax.rem(my_z + k, 4))],
                col.at[my_z],
                z_send.at[i],
                z_recv.at[i, k],
                target,
            )

    def fan(k):
        z = lax.rem(my_z - k + 4, 4)
        for i, (src, col, out) in enumerate(sides):
            if k:
                block_bytes_wait(col.at[z], z_recv.at[i, k])
            else:
                col[z] = src[:, pair_cols(my_z)]
            for d in (1, 3, 2):
                x = lax.rem(my_x + d, 4)
                send(
                    col.at[z, :, head_cols(x // 2)],
                    out.at[z, my_x, core],
                    x_send.at[i],
                    x_recv.at[i, k],
                    me + 2 * (x - my_x),
                )
            pltpu.make_async_copy(
                col.at[z, :, head_cols(my_x // 2)], out.at[z, my_x, core], own_sem.at[i, k]
            ).start()

    def pass_on(k):
        z = lax.rem(my_z - k + 4, 4)
        for i, (_, _, out) in enumerate(sides):
            block_bytes_wait(out.at[z, pl.ds(0, 3), core], x_recv.at[i, k])
            block_bytes_wait(out.at[z, my_x, core], own_sem.at[i, k])
            send(out.at[z, :, core], out.at[z, :, core], pass_send.at[i], pass_recv.at[i], sibling)

    fan(0)

    def send_q(k, carry):
        t = lax.rem(me + k, shards)
        rows = pl.ds(pl.multiple_of((t % 4) * part_rows, GROUP), part_rows)
        send(q_ref.at[rows, head_cols(t // 4)], q_in.at[me], q_send.at[0], q_recv.at[0], t)
        return carry

    lax.fori_loop(1, shards, send_q, 0)
    own_q = pltpu.make_async_copy(q_ref.at[my_rows, head_cols(my_head)], q_in.at[me], q_own.at[0])
    own_q.start()

    gblk[slot_of(row)] = grad_ref[...]
    load_w.wait()

    def multiply(y, first):
        def tile(j, carry):
            at = pl.ds(pl.multiple_of(j * width, width), width)
            rows = pl.ds(pl.multiple_of(y * cols, width), cols)
            part = jnp.dot(gblk[slot_of(y)], w_ref[rows, at], preferred_element_type=jnp.float32)
            acc[:, at] = part if first else acc[:, at] + part
            return carry

        lax.fori_loop(0, tiles, tile, 0)

    multiply(row, True)
    for k in (1, 3, 2):
        fan(k)
    to_right.wait_recv()
    from_left = gblk.at[slot_of(left), :, pl.ds(0, half)]
    on_right = send(from_left, from_left, y_send.at[2], y_recv.at[2], right, "head")
    to_left.wait_recv()
    from_right = gblk.at[slot_of(right), :, pl.ds(half, half)]
    on_left = send(from_right, from_right, y_send.at[3], y_recv.at[3], left, "head")
    pass_on(0)
    multiply(left, False)
    pass_on(1)
    multiply(right, False)
    pass_on(3)
    on_right.wait_recv()
    on_left.wait_recv()

    def finish(step, carry):
        j = lax.rem(my_head // 2 + step, tiles)
        at = pl.ds(pl.multiple_of(j * width, width), width)
        rows = pl.ds(pl.multiple_of(across * cols, width), cols)
        part = jnp.dot(gblk[slot_of(across)], w_ref[rows, at], preferred_element_type=jnp.float32)
        g_local[:, at] = (acc[:, at] + part).astype(jnp.bfloat16)
        for i in range(8):
            t = j * 8 + i
            part_at = (i % 4) * part_rows

            @pl.when(t != me)
            def _():
                send(
                    g_local.at[pl.ds(part_at, part_rows), head_cols(t // 4)],
                    g_in.at[me],
                    q_send.at[1],
                    q_recv.at[1],
                    t,
                )

        return carry

    lax.fori_loop(0, tiles, finish, 0)
    own_g = pltpu.make_async_copy(
        g_local.at[my_rows, head_cols(my_head)], g_in.at[me], q_own.at[1]
    )
    own_g.start()
    copies = [
        pltpu.make_async_copy(gblk.at[k], out, copy_sem.at[k])
        for k, out in enumerate((g0_out, g1_out, g2_out, g3_out))
    ]
    for copy in copies:
        copy.start()
    pass_on(2)
    for copy in copies:
        copy.wait()
    own_q.wait()
    own_g.wait()

    others = pl.ds(0, shards - 1)
    block_bytes_wait(q_in.at[others], q_recv.at[0])
    block_bytes_wait(q_in.at[others], q_send.at[0])
    for i, (_, col, out) in enumerate(sides):
        block_bytes_wait(out.at[:, :, core], pass_recv.at[i])
        block_bytes_wait(out.at[:, :, core], pass_send.at[i])
        block_bytes_wait(col.at[pl.ds(0, 3)], z_send.at[i])
        block_bytes_wait(out.at[:, pl.ds(0, 3), core], x_send.at[i])
    for copy in (to_right, to_left, on_right, on_left):
        copy.wait_send()
    block_bytes_wait(g_in.at[others], q_recv.at[1])
    block_bytes_wait(g_in.at[others], q_send.at[1])


def spread(grad_local, dealt_selector, selector, projections, weight, shards):
    slots, cols = grad_local.shape
    depth, width = weight.shape
    part_rows = slots // 4
    bf16 = jnp.bfloat16
    vmem = pl.BlockSpec(memory_space=pltpu.VMEM)
    block = jax.ShapeDtypeStruct((slots, cols), bf16)
    small = jax.ShapeDtypeStruct((shards, part_rows, DH), bf16)
    large = jax.ShapeDtypeStruct((4, 4, 2, slots, DH), bf16)
    *blocks, query_in, grad_in, key_in, value_in = pl.pallas_call(
        spread_kernel,
        out_shape=(block,) * 4 + (small,) * 2 + (large,) * 2,
        in_specs=[vmem] * 3 + [pl.BlockSpec(memory_space=pltpu.HBM)] * 2,
        out_specs=(pl.BlockSpec(memory_space=pltpu.HBM),) * 8,
        scratch_shapes=[
            pltpu.VMEM((depth, width), bf16),
            pltpu.VMEM(projections.shape, bf16),
            pltpu.VMEM((slots, width), bf16),
            pltpu.VMEM((slots, width), bf16),
            pltpu.VMEM((slots, width), bf16),
            pltpu.VMEM((slots, width), jnp.float32),
            pltpu.VMEM((slots, width), bf16),
            pltpu.VMEM((4, slots, cols), bf16),
            pltpu.VMEM((4, slots, 2 * DH), bf16),
            pltpu.VMEM((4, slots, 2 * DH), bf16),
            pltpu.SemaphoreType.DMA,
            pltpu.SemaphoreType.DMA,
            pltpu.SemaphoreType.DMA((4,)),
            pltpu.SemaphoreType.DMA((4,)),
            pltpu.SemaphoreType.DMA((4,)),
            pltpu.SemaphoreType.DMA((2,)),
            pltpu.SemaphoreType.DMA((2, 4)),
            pltpu.SemaphoreType.DMA((2,)),
            pltpu.SemaphoreType.DMA((2, 4)),
            pltpu.SemaphoreType.DMA((2, 4)),
            pltpu.SemaphoreType.DMA((2,)),
            pltpu.SemaphoreType.DMA((2,)),
            pltpu.SemaphoreType.DMA((2,)),
            pltpu.SemaphoreType.DMA((2,)),
            pltpu.SemaphoreType.DMA((2,)),
        ],
        compiler_params=pltpu.CompilerParams(
            collective_id=2, has_side_effects=True, vmem_limit_bytes=VMEM_BYTES
        ),
        name="spread",
    )(grad_local, dealt_selector, selector, projections, weight)
    key_in = key_in.reshape(shards, slots, DH)
    value_in = value_in.reshape(shards, slots, DH)
    return (*blocks, query_in, grad_in, key_in, value_in)


def home_kernel(
    o_ref,
    dq_ref,
    k_ref,
    g0_ref,
    g1_ref,
    g2_ref,
    g3_ref,
    home,
    wg_out,
    g_vmem,
    k_own,
    g_turned,
    oz,
    kx,
    ks,
    k_row,
    k_pair,
    k_col,
    part,
    px,
    half_send,
    half_recv,
    full_send,
    full_recv,
    send_sem,
    recv_sem,
    load_sem,
    k_send,
    k_recv,
    z_send,
    z_recv,
    p_send,
    p_recv,
    x_send,
    x_recv,
):
    shards, part_rows, _ = o_ref.shape
    slots = k_ref.shape[3]
    me = lax.axis_index("seq")
    core = me % 2
    sibling = me + 1 - 2 * core
    plane_x = me // 2 % 4
    my_z = me // 8
    out_rows, width = wg_out.shape
    my_rows = pl.ds(pl.multiple_of((me % 4) * part_rows, GROUP), part_rows)
    my_cols = pl.ds(pl.multiple_of((me // 4) * DH, DH), DH)
    f32, bf16 = jnp.float32, jnp.bfloat16

    loads = [
        pltpu.make_async_copy(src, dst, load_sem.at[i])
        for i, (src, dst) in enumerate(
            (
                (o_ref.at[me], oz.at[0, my_rows, my_cols]),
                (g0_ref, g_vmem.at[0]),
                (g1_ref, g_vmem.at[1]),
                (g2_ref, g_vmem.at[2]),
                (g3_ref, g_vmem.at[3]),
                (k_ref.at[:, :, core], k_own),
                (dq_ref.at[me], home.at[0, my_rows, my_cols]),
            )
        )
    ]
    for load in loads:
        load.start()
    greet(shards - 1, lambda k: lax.rem(me + k, shards))

    def send_o(k, carry):
        t = lax.rem(me + k, shards)
        send(o_ref.at[t], oz.at[0, my_rows, my_cols], send_sem.at[0], recv_sem.at[0], t)
        return carry

    lax.fori_loop(1, shards, send_o, 0)
    swap = send(k_ref.at[:, :, 1 - core], kx, send_sem.at[1], recv_sem.at[1], sibling)
    for load in loads:
        load.wait()

    tile = 256

    def turn(j, carry):
        cols = pl.ds(pl.multiple_of(j * tile, tile), tile)
        for k in range(4):
            g_turned[k, cols, :] = g_vmem[k, :, cols].T
        return carry

    lax.fori_loop(0, part.shape[0] // tile, turn, 0)
    block_bytes_wait(o_ref.at[pl.ds(0, shards - 1)], recv_sem.at[0])

    chunk = width // CHUNKS
    z_up, z_down = lax.rem(me + 8, shards), lax.rem(me + 24, shards)
    x_up = me + 2 * (lax.rem(plane_x + 1, 4) - plane_x)
    x_down = me + 2 * (lax.rem(plane_x + 3, 4) - plane_x)
    upper, lower = pl.ds(0, slots // 2), pl.ds(slots // 2, slots // 2)
    top, bottom = pl.ds(0, out_rows // 2), pl.ds(out_rows // 2, out_rows // 2)

    def cols_of(c):
        return pl.ds(c * chunk, chunk)

    def start_z(c):
        own = oz.at[0, :, cols_of(c)]
        send(own, oz.at[1, :, cols_of(c)], z_send.at[0], z_recv.at[0, c], z_up)
        send(own, oz.at[3, :, cols_of(c)], z_send.at[1], z_recv.at[1, c], z_down)

    def forward_z(c):
        cols = cols_of(c)
        block_bytes_wait(oz.at[1, :, cols], z_recv.at[0, c])
        send(
            oz.at[1, upper, cols], oz.at[2, upper, cols], z_send.at[2], z_recv.at[2, c], z_up
        )
        block_bytes_wait(oz.at[3, :, cols], z_recv.at[1, c])
        send(
            oz.at[3, lower, cols], oz.at[2, lower, cols], z_send.at[3], z_recv.at[3, c], z_down
        )
        if c + 2 < CHUNKS:
            start_z(c + 2)

    def piece(x, c):
        return pl.ds(pl.multiple_of((2 * x + c) * out_rows, 32), out_rows)

    def product(c):
        cols = cols_of(c)
        block_bytes_wait(oz.at[2, upper, cols], z_recv.at[2, c])
        block_bytes_wait(oz.at[2, lower, cols], z_recv.at[3, c])

        def rows_tile(j, carry):
            rows = pl.ds(pl.multiple_of(j * tile, tile), tile)
            total = jnp.dot(g_turned[0, rows, :], oz[0, :, cols], preferred_element_type=f32)
            for k in (1, 2, 3):
                total += jnp.dot(g_turned[k, rows, :], oz[k, :, cols], preferred_element_type=f32)
            part[rows, cols] = total.astype(bf16)
            return carry

        lax.fori_loop(0, part.shape[0] // tile, rows_tile, 0)
        for x in range(4):
            send(
                part.at[piece(x, 1 - core), cols],
                px.at[x, :, cols],
                p_send,
                p_recv.at[c],
                sibling,
            )

    def pair_sum(x, c):
        cols = cols_of(c)
        return part[piece(x, core), cols].astype(f32) + px[x, :, cols].astype(f32)

    def send_half(c):
        cols = cols_of(c)
        block_bytes_wait(px.at[:, :, cols], p_recv.at[c])
        half_send[:, cols] = pair_sum(lax.rem(plane_x + 2, 4), c).astype(bf16)
        send(
            half_send.at[top, cols], half_recv.at[top, cols], x_send.at[0], x_recv.at[0, c], x_up
        )
        send(
            half_send.at[bottom, cols],
            half_recv.at[bottom, cols],
            x_send.at[1],
            x_recv.at[1, c],
            x_down,
        )

    def send_full(c):
        cols = cols_of(c)
        split = out_rows // 2
        block_bytes_wait(half_recv.at[top, cols], x_recv.at[0, c])
        ahead = pair_sum(lax.rem(plane_x + 1, 4), c)
        full_send[0, top, cols] = (ahead[:split] + half_recv[top, cols].astype(f32)).astype(bf16)
        full_send[0, bottom, cols] = ahead[split:].astype(bf16)
        send(
            full_send.at[0, :, cols], full_recv.at[0, :, cols], x_send.at[2], x_recv.at[2, c], x_up
        )
        block_bytes_wait(half_recv.at[bottom, cols], x_recv.at[1, c])
        behind = pair_sum(lax.rem(plane_x + 3, 4), c)
        full_send[1, top, cols] = behind[:split].astype(bf16)
        full_send[1, bottom, cols] = (behind[split:] + half_recv[bottom, cols].astype(f32)).astype(
            bf16
        )
        send(
            full_send.at[1, :, cols],
            full_recv.at[1, :, cols],
            x_send.at[3],
            x_recv.at[3, c],
            x_down,
        )

    def finish(c):
        cols = cols_of(c)
        block_bytes_wait(full_recv.at[0, :, cols], x_recv.at[2, c])
        block_bytes_wait(full_recv.at[1, :, cols], x_recv.at[3, c])
        wg_out[:, cols] = (
            pair_sum(plane_x, c)
            + full_recv[0, :, cols].astype(f32)
            + full_recv[1, :, cols].astype(f32)
        )

    def k_sum(z, x):
        return (k_own[z, x].astype(f32) + kx[z, x].astype(f32)).astype(bf16)

    def k_along_x():
        for k in (1, 2, 3):
            x = lax.rem(plane_x + k, 4)
            for z in range(4):
                ks[z, x] = k_sum(z, x)
            send(
                ks.at[:, x],
                k_row.at[plane_x],
                k_send.at[k - 1],
                k_recv.at[k - 1],
                me + 2 * (x - plane_x),
            )
        for z in range(4):
            k_row[plane_x, z] = k_sum(z, plane_x)

    def k_along_z():
        for k in range(3):
            block_bytes_wait(k_row.at[0], k_recv.at[k])
        for k in (1, 2, 3, 0):
            z = lax.rem(my_z + k, 4)
            for h in range(2):
                pair = k_row[2 * h, z].astype(f32) + k_row[2 * h + 1, z].astype(f32)
                k_pair[z, h] = pair.astype(bf16)
            if k:
                send(
                    k_pair.at[z],
                    k_col.at[my_z],
                    k_send.at[2 + k],
                    k_recv.at[2 + k],
                    lax.rem(me + 8 * k, shards),
                )
            else:
                k_col[my_z] = k_pair[z]

    def send_dq(k, carry):
        t = lax.rem(me + k, shards)
        send(dq_ref.at[t], home.at[0, my_rows, my_cols], send_sem.at[3], recv_sem.at[3], t)
        return carry

    start_z(0)
    start_z(1)
    swap.wait()
    k_along_x()
    stages = (forward_z, product, send_half, send_full, finish)
    for step in range(CHUNKS + len(stages) - 1):
        if step == K_STEP:
            k_along_z()
        if step == DQ_STEP:
            lax.fori_loop(1, shards, send_dq, 0)
        for i, stage in enumerate(stages):
            if 0 <= step - i < CHUNKS:
                stage(step - i)
    for k in range(3):
        block_bytes_wait(k_col.at[0], k_recv.at[3 + k])
    for z in range(4):
        for h in range(2):
            cols = pl.ds((2 * z + h) * DH, DH)
            home[1, :, cols] = k_col[z, h, :, :DH]
            home[2, :, cols] = k_col[z, h, :, DH:]
    block_bytes_wait(dq_ref.at[pl.ds(0, shards - 1)], recv_sem.at[3])
    block_bytes_wait(o_ref.at[pl.ds(0, shards - 1)], send_sem.at[0])
    for k in range(3):
        block_bytes_wait(ks.at[:, 0], k_send.at[k])
        block_bytes_wait(k_pair.at[0], k_send.at[3 + k])
    block_bytes_wait(dq_ref.at[pl.ds(0, shards - 1)], send_sem.at[3])
    block_bytes_wait(oz.at[0], z_send.at[0])
    block_bytes_wait(oz.at[0], z_send.at[1])
    block_bytes_wait(oz.at[1, upper], z_send.at[2])
    block_bytes_wait(oz.at[3, lower], z_send.at[3])
    block_bytes_wait(px, p_send)
    block_bytes_wait(half_send.at[top], x_send.at[0])
    block_bytes_wait(half_send.at[bottom], x_send.at[1])
    block_bytes_wait(full_send.at[0], x_send.at[2])
    block_bytes_wait(full_send.at[1], x_send.at[3])


def bring_home(o_back, dq_back, key_back, grad_parts, out_rows):
    shards, part_rows, _ = o_back.shape
    slots = key_back.shape[1]
    width = shards // 4 * DH
    rows = grad_parts[0].shape[1]
    key_back = key_back.reshape(4, 4, 2, slots, 2 * DH)
    vmem = pl.BlockSpec(memory_space=pltpu.VMEM)
    bf16 = jnp.bfloat16
    return pl.pallas_call(
        home_kernel,
        out_shape=(
            jax.ShapeDtypeStruct((3, slots, width), bf16),
            jax.ShapeDtypeStruct((out_rows, width), jnp.float32),
        ),
        in_specs=[pl.BlockSpec(memory_space=pltpu.HBM)] * 3
        + [pl.BlockSpec(memory_space=pl.ANY)] * 4,
        out_specs=(vmem,) * 2,
        scratch_shapes=[
            pltpu.VMEM((4, slots, rows), bf16),
            pltpu.VMEM((4, 4, slots, 2 * DH), bf16),
            pltpu.VMEM((4, rows, slots), bf16),
            pltpu.VMEM((4, slots, width), bf16),
            pltpu.VMEM((4, 4, slots, 2 * DH), bf16),
            pltpu.VMEM((4, 4, slots, 2 * DH), bf16),
            pltpu.VMEM((4, 4, slots, 2 * DH), bf16),
            pltpu.VMEM((4, 2, slots, 2 * DH), bf16),
            pltpu.VMEM((4, 2, slots, 2 * DH), bf16),
            pltpu.VMEM((rows, width), bf16),
            pltpu.VMEM((4, out_rows, width), bf16),
            pltpu.VMEM((out_rows, width), bf16),
            pltpu.VMEM((out_rows, width), bf16),
            pltpu.VMEM((2, out_rows, width), bf16),
            pltpu.VMEM((2, out_rows, width), bf16),
            pltpu.SemaphoreType.DMA((4,)),
            pltpu.SemaphoreType.DMA((4,)),
            pltpu.SemaphoreType.DMA((7,)),
            pltpu.SemaphoreType.DMA((6,)),
            pltpu.SemaphoreType.DMA((6,)),
            pltpu.SemaphoreType.DMA((4,)),
            pltpu.SemaphoreType.DMA((4, CHUNKS)),
            pltpu.SemaphoreType.DMA,
            pltpu.SemaphoreType.DMA((CHUNKS,)),
            pltpu.SemaphoreType.DMA((4,)),
            pltpu.SemaphoreType.DMA((4, CHUNKS)),
        ],
        compiler_params=pltpu.CompilerParams(
            collective_id=1, has_side_effects=True, vmem_limit_bytes=VMEM_BYTES
        ),
        name="home",
    )(o_back, dq_back, key_back, *grad_parts)


def on_device(
    projections,
    output_gradient,
    output_projection_weight,
    kept_token_indices,
    surviving_token_count,
):
    tok_dev = projections.shape[0]
    group_width = projections.shape[2]
    slots = kept_token_indices.shape[1]
    heads_local = group_width // DH
    seq_count = lax.axis_size("seq")
    quarters = seq_count // heads_local
    part_rows = slots // quarters
    me = lax.axis_index("seq")
    my_quarter = (me % quarters).astype(jnp.int32)[None]

    kept = kept_token_indices[0]
    dealt = kept.reshape(part_rows // GROUP, quarters, GROUP).transpose(1, 0, 2)
    dealt = lax.dynamic_slice_in_dim(
        jnp.concatenate([dealt, dealt], axis=0), me % quarters, quarters, axis=0
    ).reshape(slots)
    token = jnp.arange(tok_dev, dtype=jnp.int32)[None, :]
    selector = (kept[:, None] == token).astype(jnp.bfloat16)
    dealt_selector = (dealt[:, None] == token).astype(jnp.bfloat16)

    def pick(which, values):
        return jnp.dot(which, values, preferred_element_type=jnp.float32).astype(jnp.bfloat16)

    grad_local = pick(dealt_selector, output_gradient)

    *blocks, query_in, grad_in, key_in, value_in = spread(
        grad_local,
        dealt_selector,
        selector,
        projections.transpose(1, 0, 2),
        output_projection_weight,
        seq_count,
    )

    def along_z(k):
        if k == 0:
            return blocks[0]
        return lax.ppermute(
            blocks[k], "seq", [(i, (i + 8 * k) % seq_count) for i in range(seq_count)]
        )

    grad_parts = [along_z(k) for k in range(4)]
    dq_back, o_back, key_back = attend(
        surviving_token_count, my_quarter, query_in, grad_in, key_in, value_in
    )
    out_rows = output_projection_weight.shape[0] // seq_count
    grad_packed, weight_grad = bring_home(o_back, dq_back, key_back, grad_parts, out_rows)
    projection_grad = lax.dot_general(
        jnp.stack([dealt_selector, selector, selector]),
        grad_packed,
        (((1,), (1,)), ((0,), (0,))),
        preferred_element_type=jnp.float32,
    )
    projection_grad = projection_grad.astype(jnp.bfloat16).transpose(1, 0, 2)
    return (projection_grad, weight_grad)


def solution(mesh):
    return jax.shard_map(
        on_device,
        mesh=mesh,
        in_specs=(P("seq", None, "head"), P("seq", "head"), P(None, "head"), P("seq", None), P()),
        out_specs=(P("seq", None, "head"), P("seq", "head")),
        check_vma=False,
    )
```

```python
import math

import jax
import jax.numpy as jnp
from jax import lax
from jax.experimental import pallas as pl
from jax.experimental.pallas import tpu as pltpu
from jax.sharding import PartitionSpec as P

DH = 128
BQ = 256
BK = 1536
TAIL = 512
GROUP = 16
NEG = -1e30
CHUNKS = 4
VMEM_BYTES = 60 * 1024 * 1024
K_STEP = 4
DQ_STEP = 4


def contract_rows(left, right):
    return lax.dot_general(
        left, right, (((0,), (0,)), ((), ())), preferred_element_type=jnp.float32
    )


def attend_kernel(
    count_ref,
    quarter_ref,
    q_hbm,
    g_hbm,
    k_hbm,
    v_hbm,
    dq_out,
    o_out,
    k_out,
    q_ref,
    g_ref,
    k_ref,
    v_ref,
    k_stage,
    qc,
    gc,
    kc,
    vc,
    k_turned,
    v_turned,
    q_turned,
    dkc,
    dvc,
    oc,
    s_scr,
    p_scr,
    qpos,
    acc,
    group_pos,
    load_sem,
    store_sem,
):
    shards, part_rows, _ = q_ref.shape
    slots = k_ref.shape[1]
    quarter = quarter_ref[0]
    groups = part_rows // GROUP
    score_scale = 1.0 / math.sqrt(DH)
    log2e = score_scale * math.log2(math.e)
    bf16 = jnp.bfloat16
    loads = [
        pltpu.make_async_copy(src, dst, load_sem.at[i])
        for i, (src, dst) in enumerate(
            ((q_hbm, q_ref), (g_hbm, g_ref), (k_hbm, k_ref), (v_hbm, v_ref))
        )
    ]
    for load in loads:
        load.start()

    def clear(i, carry):
        rows = pl.ds(pl.multiple_of(i * slots, slots), slots)
        dkc[rows, :] = jnp.zeros((slots, DH), jnp.float32)
        dvc[rows, :] = jnp.zeros((slots, DH), jnp.float32)
        return carry

    lax.fori_loop(0, shards, clear, 0)
    q_turned[DH:, :] = jnp.where(
        lax.broadcasted_iota(jnp.int32, (DH, BQ), 0) == 0, 1.0, 0.0
    ).astype(bf16)
    for load in loads:
        load.wait()

    def dead_marks(rows, live):
        row = lax.broadcasted_iota(jnp.int32, (rows, DH), 0)
        lane = lax.broadcasted_iota(jnp.int32, (rows, DH), 1)
        return jnp.where((row >= live) & (lane == 0), NEG, 0.0).astype(bf16)

    def live_groups(s):
        live = (count_ref[s] + GROUP - 1) // GROUP
        first = lax.rem(quarter + s, 4)
        return live, first, (live - first + 3) // 4

    rows_live = GROUP * lax.fori_loop(0, shards, lambda s, n: n + live_groups(s)[2], jnp.int32(0))
    blocks = (rows_live + BQ - 1) // BQ
    end_q = blocks * BQ
    start_q = pl.multiple_of(end_q - rows_live, GROUP)
    qc[pl.ds(0, BQ), :] = jnp.zeros((BQ, DH), bf16)
    gc[pl.ds(0, BQ), :] = jnp.zeros((BQ, DH), bf16)
    qpos[pl.ds(0, BQ), :] = jnp.zeros((BQ, DH), jnp.int32)
    group_pos[0] = 0

    def pack(s, carry):
        at_k, at_q = carry
        live, first, mine = live_groups(s)
        at_k = pl.multiple_of(at_k, GROUP)
        at_q = pl.multiple_of(at_q, GROUP)
        kc[pl.ds(at_k, slots), :DH] = k_ref[s]
        kc[pl.ds(at_k, slots), DH:] = dead_marks(slots, count_ref[s])
        vc[pl.ds(at_k, slots), :] = v_ref[s]
        qc[pl.ds(at_q, part_rows), :] = q_ref[s]
        gc[pl.ds(at_q, part_rows), :] = g_ref[s]
        rows = lax.broadcasted_iota(jnp.int32, (GROUP, DH), 0)
        for i in range(groups):
            base = at_k + (first + 4 * i) * GROUP
            qpos[pl.ds(at_q + i * GROUP, GROUP), :] = base + rows
            group_pos[at_q // GROUP + i] = base
        return at_k + live * GROUP, at_q + mine * GROUP

    end_k, _ = lax.fori_loop(0, shards, pack, (jnp.int32(0), start_q))
    end_k = pl.multiple_of(end_k, GROUP)
    kc[pl.ds(end_k, BK), :DH] = jnp.zeros((BK, DH), bf16)
    kc[pl.ds(end_k, BK), DH:] = dead_marks(BK, 0)
    vc[pl.ds(end_k, BK), :] = jnp.zeros((BK, DH), bf16)
    oc[pl.ds(pl.multiple_of(end_q, BQ), part_rows), :] = jnp.zeros(
        (part_rows, 2 * DH), bf16
    )

    def turn(c, carry):
        keys = pl.ds(pl.multiple_of(c * BK, BK), BK)
        k_turned[:, keys] = kc[keys, :DH].T
        v_turned[:, keys] = vc[keys, :].T
        return carry

    lax.fori_loop(0, (end_k + BK - 1) // BK, turn, 0)

    def block(b, carry):
        rows = pl.ds(pl.multiple_of(b * BQ, BQ), BQ)
        key_end = group_pos[(b + 1) * (BQ // GROUP) - 1] + GROUP
        chunks = (key_end + TAIL - 1) // BK
        tails = (jnp.maximum(key_end - chunks * BK, 0) + TAIL - 1) // TAIL
        first_end = jnp.where(b == 0, 0, group_pos[b * (BQ // GROUP)] + 1)
        clear_chunks = jnp.minimum(first_end // BK, chunks)

        def over(body, carry):
            carry = lax.fori_loop(0, chunks, lambda c, x: body(c * BK, BK, x), carry)
            return lax.fori_loop(
                0, tails, lambda c, x: body(chunks * BK + c * TAIL, TAIL, x), carry
            )

        q_turned[:DH, :] = qc[rows, :].T
        last_key = qpos[rows, :].T[0:1, :]

        def score(at, size, top, masked):
            at = pl.multiple_of(at, TAIL)
            keys = pl.ds(at, size)
            s = jnp.dot(kc[keys, :], q_turned[...], preferred_element_type=jnp.float32)
            if masked:
                key = at + lax.broadcasted_iota(jnp.int32, (size, BQ), 0)
                s = jnp.where(key <= last_key, s, NEG)
            s_scr[keys, :] = s
            return jnp.maximum(top, jnp.max(s, axis=0, keepdims=True))

        top = jnp.full((1, BQ), NEG, jnp.float32)
        top = lax.fori_loop(0, clear_chunks, lambda c, t: score(c * BK, BK, t, False), top)
        top = lax.fori_loop(clear_chunks, chunks, lambda c, t: score(c * BK, BK, t, True), top)
        top = lax.fori_loop(
            0, tails, lambda c, t: score(chunks * BK + c * TAIL, TAIL, t, True), top
        )
        acc[...] = jnp.zeros((DH, BQ), jnp.float32)

        def weigh(at, size, total):
            keys = pl.ds(pl.multiple_of(at, TAIL), size)
            p = jnp.exp2((s_scr[keys, :] - top) * log2e)
            p_low = p.astype(bf16)
            p_scr[keys, :] = p_low
            acc[...] += jnp.dot(v_turned[:, keys], p_low, preferred_element_type=jnp.float32)
            return total + jnp.sum(p, axis=0, keepdims=True)

        total = over(weigh, jnp.zeros((1, BQ), jnp.float32))
        inverse = 1.0 / total
        attended = acc[...] * inverse
        oc[rows, DH:] = attended.T.astype(bf16)
        g_turned = (gc[rows, :].astype(jnp.float32).T * inverse).astype(bf16)
        row_dot = jnp.sum(g_turned.astype(jnp.float32) * attended, axis=0, keepdims=True)
        g_part = g_turned.T
        acc[...] = jnp.zeros((DH, BQ), jnp.float32)

        def back(at, size, carry):
            keys = pl.ds(pl.multiple_of(at, TAIL), size)
            p_low = p_scr[keys, :]
            grad_probs = jnp.dot(vc[keys, :], g_turned, preferred_element_type=jnp.float32)
            ds = (p_low.astype(jnp.float32) * (grad_probs - row_dot)).astype(bf16)
            acc[...] += jnp.dot(k_turned[:, keys], ds, preferred_element_type=jnp.float32)
            dkc[keys, :] += jnp.dot(ds, qc[rows, :], preferred_element_type=jnp.float32)
            dvc[keys, :] += jnp.dot(p_low, g_part, preferred_element_type=jnp.float32)
            return carry

        over(back, 0)
        oc[rows, :DH] = (acc[...] * score_scale).T.astype(bf16)
        return carry

    lax.fori_loop(0, blocks, block, 0)

    def unpack(s, carry):
        at_k, at_q = carry
        live, first, mine = live_groups(s)
        at_k = pl.multiple_of(at_k, GROUP)
        at_q = pl.multiple_of(at_q, GROUP)
        q_ref[s] = oc[pl.ds(at_q, part_rows), :DH]
        g_ref[s] = oc[pl.ds(at_q, part_rows), DH:]
        k_stage[s, :, :DH] = (dkc[pl.ds(at_k, slots), :] * score_scale).astype(bf16)
        k_stage[s, :, DH:] = dvc[pl.ds(at_k, slots), :].astype(bf16)
        pltpu.make_async_copy(k_stage.at[s], k_out.at[s], store_sem.at[0]).start()
        return at_k + live * GROUP, at_q + mine * GROUP

    lax.fori_loop(0, shards, unpack, (jnp.int32(0), start_q))
    stores = [
        pltpu.make_async_copy(q_ref, dq_out, store_sem.at[1]),
        pltpu.make_async_copy(g_ref, o_out, store_sem.at[2]),
    ]
    for store in stores:
        store.start()
    pltpu.make_async_copy(k_stage, k_out, store_sem.at[0]).wait()
    for store in stores:
        store.wait()


def attend(counts, quarter, query_in, grad_in, key_in, value_in):
    shards, part_rows, _ = query_in.shape
    slots = key_in.shape[1]
    keys = shards * slots
    queries = shards * part_rows
    bf16 = jnp.bfloat16
    smem = pl.BlockSpec(memory_space=pltpu.SMEM)
    hbm = pl.BlockSpec(memory_space=pltpu.HBM)
    return pl.pallas_call(
        attend_kernel,
        out_shape=(
            jax.ShapeDtypeStruct((shards, part_rows, DH), bf16),
            jax.ShapeDtypeStruct((shards, part_rows, DH), bf16),
            jax.ShapeDtypeStruct((shards, slots, 2 * DH), bf16),
        ),
        in_specs=[smem, smem, hbm, hbm, hbm, hbm],
        out_specs=(hbm, hbm, hbm),
        scratch_shapes=[
            pltpu.VMEM((shards, part_rows, DH), bf16),
            pltpu.VMEM((shards, part_rows, DH), bf16),
            pltpu.VMEM((shards, slots, DH), bf16),
            pltpu.VMEM((shards, slots, DH), bf16),
            pltpu.VMEM((shards, slots, 2 * DH), bf16),
            pltpu.VMEM((queries + BQ, DH), bf16),
            pltpu.VMEM((queries + BQ, DH), bf16),
            pltpu.VMEM((keys + BK, 2 * DH), bf16),
            pltpu.VMEM((keys + BK, DH), bf16),
            pltpu.VMEM((DH, keys), bf16),
            pltpu.VMEM((DH, keys), bf16),
            pltpu.VMEM((2 * DH, BQ), bf16),
            pltpu.VMEM((keys, DH), jnp.float32),
            pltpu.VMEM((keys, DH), jnp.float32),
            pltpu.VMEM((queries + BQ, 2 * DH), bf16),
            pltpu.VMEM((keys, BQ), jnp.float32),
            pltpu.VMEM((keys, BQ), bf16),
            pltpu.VMEM((queries + BQ, DH), jnp.int32),
            pltpu.VMEM((DH, BQ), jnp.float32),
            pltpu.SMEM((queries // GROUP + 8,), jnp.int32),
            pltpu.SemaphoreType.DMA((4,)),
            pltpu.SemaphoreType.DMA((3,)),
        ],
        compiler_params=pltpu.CompilerParams(vmem_limit_bytes=VMEM_BYTES),
        cost_estimate=pl.CostEstimate(
            flops=6 * queries * keys * DH, bytes_accessed=16 * 1024 * 1024, transcendentals=0
        ),
        name="attend",
    )(counts, quarter, query_in, grad_in, key_in, value_in)


def block_bytes_wait(ref, sem):
    pltpu.make_async_copy(ref, ref, sem).wait()


def greet(peers, peer_of, ring=0, meanwhile=None):
    barrier = pltpu.get_barrier_semaphore()

    def signal(k, carry):
        pl.semaphore_signal(
            barrier, inc=1, device_id={"seq": peer_of(k)}, device_id_type=pl.DeviceIdType.MESH
        )
        return carry

    lax.fori_loop(1, peers + 1, signal, 0)
    if ring:
        row = lax.axis_index("head")
        for k in range(1, ring):
            pl.semaphore_signal(
                barrier,
                inc=1,
                device_id={"head": lax.rem(row + k, ring)},
                device_id_type=pl.DeviceIdType.MESH,
            )
        peers = peers + ring - 1
    if meanwhile is not None:
        meanwhile()
    pl.semaphore_wait(barrier, peers)


def send(src, dst, send_sem, recv_sem, target, axis="seq"):
    copy = pltpu.make_async_remote_copy(
        src_ref=src,
        dst_ref=dst,
        send_sem=send_sem,
        recv_sem=recv_sem,
        device_id={axis: target},
        device_id_type=pl.DeviceIdType.MESH,
    )
    copy.start()
    return copy


def dealt_rows(group, first, part_rows):
    at = lax.rem(group + 4 - first, 4) * part_rows + group // 4 * GROUP
    return pl.ds(pl.multiple_of(at, GROUP), GROUP)


def spread_kernel(
    all_grad_ref,
    kept_ref,
    p_hbm,
    w_hbm,
    g0_out,
    g1_out,
    g2_out,
    g3_out,
    q_in,
    g_in,
    k_in,
    v_in,
    w_ref,
    p_ref,
    select,
    grad_ref,
    q_ref,
    k_ref,
    v_ref,
    acc,
    g_local,
    gblk,
    k_col,
    v_col,
    w_sem,
    p_sem,
    copy_sem,
    y_send,
    y_recv,
    z_send,
    z_recv,
    x_send,
    x_recv,
    own_sem,
    pass_send,
    pass_recv,
    q_send,
    q_recv,
    q_own,
):
    shards, part_rows, _ = q_in.shape
    slots, cols = grad_ref.shape
    half = cols // 2
    me = lax.axis_index("seq")
    row = lax.axis_index("head")
    core = me % 2
    sibling = me + 1 - 2 * core
    my_z = me // 8
    my_x = me // 2 % 4
    my_head = me // 4
    my_rows = pl.ds(pl.multiple_of((me % 4) * part_rows, GROUP), part_rows)

    load_w = pltpu.make_async_copy(w_hbm, w_ref, w_sem)
    load_p = pltpu.make_async_copy(p_hbm, p_ref, p_sem)
    load_p.start()
    load_w.start()
    width = 256
    tiles = acc.shape[1] // width

    def pick():
        token = lax.broadcasted_iota(jnp.int32, select.shape, 0)
        select[...] = jnp.where(token == kept_ref[...], 1.0, 0.0).astype(jnp.bfloat16)

        def deal(out, at, values):
            for g in range(slots // GROUP):
                out[dealt_rows(g, me % 4, part_rows), at] = values[g * GROUP : (g + 1) * GROUP]

        def grad_tile(j, carry):
            at = pl.ds(pl.multiple_of(j * width, width), width)
            picked = contract_rows(select[...], all_grad_ref[:, at])
            deal(grad_ref, at, picked.astype(jnp.bfloat16))
            return carry

        lax.fori_loop(0, cols // width, grad_tile, 0)
        load_p.wait()

        def tile(j, carry):
            at = pl.ds(pl.multiple_of(j * width, width), width)
            picked = [
                contract_rows(select[...], p_ref[i, :, at]).astype(jnp.bfloat16) for i in range(3)
            ]
            deal(q_ref, at, picked[0])
            k_ref[:, at] = picked[1]
            v_ref[:, at] = picked[2]
            return carry

        lax.fori_loop(0, tiles, tile, 0)

    greet(shards - 1, lambda k: lax.rem(me + k, shards), 4, pick)

    def head_cols(head):
        return pl.ds(pl.multiple_of(head * DH, DH), DH)

    def pair_cols(z):
        return pl.ds(pl.multiple_of(z * 2 * DH, 2 * DH), 2 * DH)

    def slot_of(y):
        return lax.rem(y - my_z + 4, 4)

    right, left, across = lax.rem(row + 1, 4), lax.rem(row + 3, 4), lax.rem(row + 2, 4)
    to_right = send(grad_ref, gblk.at[slot_of(row)], y_send.at[0], y_recv.at[0], right, "head")
    to_left = send(grad_ref, gblk.at[slot_of(row)], y_send.at[1], y_recv.at[1], left, "head")

    sides = ((k_ref, k_col, k_in), (v_ref, v_col, v_in))
    for k in (1, 3, 2):
        target = lax.rem(me + 8 * k, shards)
        for i, (src, col, _) in enumerate(sides):
            send(
                src.at[:, pair_cols(lax.rem(my_z + k, 4))],
                col.at[my_z],
                z_send.at[i],
                z_recv.at[i, k],
                target,
            )

    def fan(k):
        z = lax.rem(my_z - k + 4, 4)
        for i, (src, col, out) in enumerate(sides):
            if k:
                block_bytes_wait(col.at[z], z_recv.at[i, k])
            else:
                col[z] = src[:, pair_cols(my_z)]
            for d in (1, 3, 2):
                x = lax.rem(my_x + d, 4)
                send(
                    col.at[z, :, head_cols(x // 2)],
                    out.at[z, my_x, core],
                    x_send.at[i],
                    x_recv.at[i, k],
                    me + 2 * (x - my_x),
                )
            pltpu.make_async_copy(
                col.at[z, :, head_cols(my_x // 2)], out.at[z, my_x, core], own_sem.at[i, k]
            ).start()

    def pass_on(k):
        z = lax.rem(my_z - k + 4, 4)
        for i, (_, _, out) in enumerate(sides):
            block_bytes_wait(out.at[z, pl.ds(0, 3), core], x_recv.at[i, k])
            block_bytes_wait(out.at[z, my_x, core], own_sem.at[i, k])
            send(out.at[z, :, core], out.at[z, :, core], pass_send.at[i], pass_recv.at[i], sibling)

    fan(0)

    def send_q(k, carry):
        t = lax.rem(me + k, shards)
        rows = pl.ds(pl.multiple_of((t % 4) * part_rows, GROUP), part_rows)
        send(q_ref.at[rows, head_cols(t // 4)], q_in.at[me], q_send.at[0], q_recv.at[0], t)
        return carry

    lax.fori_loop(1, shards, send_q, 0)
    own_q = pltpu.make_async_copy(q_ref.at[my_rows, head_cols(my_head)], q_in.at[me], q_own.at[0])
    own_q.start()

    gblk[slot_of(row)] = grad_ref[...]
    load_w.wait()

    def multiply(y, first):
        def tile(j, carry):
            at = pl.ds(pl.multiple_of(j * width, width), width)
            rows = pl.ds(pl.multiple_of(y * cols, width), cols)
            part = jnp.dot(gblk[slot_of(y)], w_ref[rows, at], preferred_element_type=jnp.float32)
            acc[:, at] = part if first else acc[:, at] + part
            return carry

        lax.fori_loop(0, tiles, tile, 0)

    multiply(row, True)
    for k in (1, 3, 2):
        fan(k)
    to_right.wait_recv()
    from_left = gblk.at[slot_of(left), :, pl.ds(0, half)]
    on_right = send(from_left, from_left, y_send.at[2], y_recv.at[2], right, "head")
    to_left.wait_recv()
    from_right = gblk.at[slot_of(right), :, pl.ds(half, half)]
    on_left = send(from_right, from_right, y_send.at[3], y_recv.at[3], left, "head")
    pass_on(0)
    multiply(left, False)
    pass_on(1)
    multiply(right, False)
    pass_on(3)
    on_right.wait_recv()
    on_left.wait_recv()

    def finish(step, carry):
        j = lax.rem(my_head // 2 + step, tiles)
        at = pl.ds(pl.multiple_of(j * width, width), width)
        rows = pl.ds(pl.multiple_of(across * cols, width), cols)
        part = jnp.dot(gblk[slot_of(across)], w_ref[rows, at], preferred_element_type=jnp.float32)
        g_local[:, at] = (acc[:, at] + part).astype(jnp.bfloat16)
        for i in range(8):
            t = j * 8 + i
            part_at = (i % 4) * part_rows

            @pl.when(t != me)
            def _():
                send(
                    g_local.at[pl.ds(part_at, part_rows), head_cols(t // 4)],
                    g_in.at[me],
                    q_send.at[1],
                    q_recv.at[1],
                    t,
                )

        return carry

    lax.fori_loop(0, tiles, finish, 0)
    own_g = pltpu.make_async_copy(
        g_local.at[my_rows, head_cols(my_head)], g_in.at[me], q_own.at[1]
    )
    own_g.start()
    copies = [
        pltpu.make_async_copy(gblk.at[k], out, copy_sem.at[k])
        for k, out in enumerate((g0_out, g1_out, g2_out, g3_out))
    ]
    for copy in copies:
        copy.start()
    pass_on(2)
    for copy in copies:
        copy.wait()
    own_q.wait()
    own_g.wait()

    others = pl.ds(0, shards - 1)
    block_bytes_wait(q_in.at[others], q_recv.at[0])
    block_bytes_wait(q_in.at[others], q_send.at[0])
    for i, (_, col, out) in enumerate(sides):
        block_bytes_wait(out.at[:, :, core], pass_recv.at[i])
        block_bytes_wait(out.at[:, :, core], pass_send.at[i])
        block_bytes_wait(col.at[pl.ds(0, 3)], z_send.at[i])
        block_bytes_wait(out.at[:, pl.ds(0, 3), core], x_send.at[i])
    for copy in (to_right, to_left, on_right, on_left):
        copy.wait_send()
    block_bytes_wait(g_in.at[others], q_recv.at[1])
    block_bytes_wait(g_in.at[others], q_send.at[1])


def spread(output_gradient, kept, projections, weight, shards):
    tokens, cols = output_gradient.shape
    slots = kept.shape[1]
    depth, width = weight.shape
    part_rows = slots // 4
    bf16 = jnp.bfloat16
    vmem = pl.BlockSpec(memory_space=pltpu.VMEM)
    block = jax.ShapeDtypeStruct((slots, cols), bf16)
    small = jax.ShapeDtypeStruct((shards, part_rows, DH), bf16)
    large = jax.ShapeDtypeStruct((4, 4, 2, slots, DH), bf16)
    *blocks, query_in, grad_in, key_in, value_in = pl.pallas_call(
        spread_kernel,
        out_shape=(block,) * 4 + (small,) * 2 + (large,) * 2,
        in_specs=[vmem] * 2 + [pl.BlockSpec(memory_space=pltpu.HBM)] * 2,
        out_specs=(pl.BlockSpec(memory_space=pltpu.HBM),) * 8,
        scratch_shapes=[
            pltpu.VMEM((depth, width), bf16),
            pltpu.VMEM(projections.shape, bf16),
            pltpu.VMEM((tokens, slots), bf16),
            pltpu.VMEM((slots, cols), bf16),
            pltpu.VMEM((slots, width), bf16),
            pltpu.VMEM((slots, width), bf16),
            pltpu.VMEM((slots, width), bf16),
            pltpu.VMEM((slots, width), jnp.float32),
            pltpu.VMEM((slots, width), bf16),
            pltpu.VMEM((4, slots, cols), bf16),
            pltpu.VMEM((4, slots, 2 * DH), bf16),
            pltpu.VMEM((4, slots, 2 * DH), bf16),
            pltpu.SemaphoreType.DMA,
            pltpu.SemaphoreType.DMA,
            pltpu.SemaphoreType.DMA((4,)),
            pltpu.SemaphoreType.DMA((4,)),
            pltpu.SemaphoreType.DMA((4,)),
            pltpu.SemaphoreType.DMA((2,)),
            pltpu.SemaphoreType.DMA((2, 4)),
            pltpu.SemaphoreType.DMA((2,)),
            pltpu.SemaphoreType.DMA((2, 4)),
            pltpu.SemaphoreType.DMA((2, 4)),
            pltpu.SemaphoreType.DMA((2,)),
            pltpu.SemaphoreType.DMA((2,)),
            pltpu.SemaphoreType.DMA((2,)),
            pltpu.SemaphoreType.DMA((2,)),
            pltpu.SemaphoreType.DMA((2,)),
        ],
        compiler_params=pltpu.CompilerParams(
            collective_id=2, has_side_effects=True, vmem_limit_bytes=VMEM_BYTES
        ),
        name="spread",
    )(output_gradient, kept, projections, weight)
    key_in = key_in.reshape(shards, slots, DH)
    value_in = value_in.reshape(shards, slots, DH)
    return (*blocks, query_in, grad_in, key_in, value_in)


def home_kernel(
    o_ref,
    dq_ref,
    k_ref,
    g0_ref,
    g1_ref,
    g2_ref,
    g3_ref,
    home,
    wg_out,
    g_vmem,
    k_own,
    g_turned,
    oz,
    kx,
    ks,
    k_row,
    k_pair,
    k_col,
    part,
    px,
    half_send,
    half_recv,
    full_send,
    full_recv,
    send_sem,
    recv_sem,
    load_sem,
    k_send,
    k_recv,
    z_send,
    z_recv,
    p_send,
    p_recv,
    x_send,
    x_recv,
):
    shards, part_rows, _ = o_ref.shape
    slots = k_ref.shape[3]
    me = lax.axis_index("seq")
    core = me % 2
    sibling = me + 1 - 2 * core
    plane_x = me // 2 % 4
    my_z = me // 8
    out_rows, width = wg_out.shape
    my_rows = pl.ds(pl.multiple_of((me % 4) * part_rows, GROUP), part_rows)
    my_cols = pl.ds(pl.multiple_of((me // 4) * DH, DH), DH)
    f32, bf16 = jnp.float32, jnp.bfloat16

    loads = [
        pltpu.make_async_copy(src, dst, load_sem.at[i])
        for i, (src, dst) in enumerate(
            (
                (o_ref.at[me], oz.at[0, my_rows, my_cols]),
                (g0_ref, g_vmem.at[0]),
                (g1_ref, g_vmem.at[1]),
                (g2_ref, g_vmem.at[2]),
                (g3_ref, g_vmem.at[3]),
                (k_ref.at[:, :, core], k_own),
                (dq_ref.at[me], home.at[0, my_rows, my_cols]),
            )
        )
    ]
    for load in loads:
        load.start()
    greet(shards - 1, lambda k: lax.rem(me + k, shards))

    def send_o(k, carry):
        t = lax.rem(me + k, shards)
        send(o_ref.at[t], oz.at[0, my_rows, my_cols], send_sem.at[0], recv_sem.at[0], t)
        return carry

    lax.fori_loop(1, shards, send_o, 0)
    swap = send(k_ref.at[:, :, 1 - core], kx, send_sem.at[1], recv_sem.at[1], sibling)
    for load in loads:
        load.wait()

    tile = 256

    def turn(j, carry):
        cols = pl.ds(pl.multiple_of(j * tile, tile), tile)
        for k in range(4):
            g_turned[k, cols, :] = g_vmem[k, :, cols].T
        return carry

    lax.fori_loop(0, part.shape[0] // tile, turn, 0)
    block_bytes_wait(o_ref.at[pl.ds(0, shards - 1)], recv_sem.at[0])

    chunk = width // CHUNKS
    z_up, z_down = lax.rem(me + 8, shards), lax.rem(me + 24, shards)
    x_up = me + 2 * (lax.rem(plane_x + 1, 4) - plane_x)
    x_down = me + 2 * (lax.rem(plane_x + 3, 4) - plane_x)
    upper, lower = pl.ds(0, slots // 2), pl.ds(slots // 2, slots // 2)
    top, bottom = pl.ds(0, out_rows // 2), pl.ds(out_rows // 2, out_rows // 2)

    def cols_of(c):
        return pl.ds(c * chunk, chunk)

    def start_z(c):
        own = oz.at[0, :, cols_of(c)]
        send(own, oz.at[1, :, cols_of(c)], z_send.at[0], z_recv.at[0, c], z_up)
        send(own, oz.at[3, :, cols_of(c)], z_send.at[1], z_recv.at[1, c], z_down)

    def forward_z(c):
        cols = cols_of(c)
        block_bytes_wait(oz.at[1, :, cols], z_recv.at[0, c])
        send(
            oz.at[1, upper, cols], oz.at[2, upper, cols], z_send.at[2], z_recv.at[2, c], z_up
        )
        block_bytes_wait(oz.at[3, :, cols], z_recv.at[1, c])
        send(
            oz.at[3, lower, cols], oz.at[2, lower, cols], z_send.at[3], z_recv.at[3, c], z_down
        )
        if c + 2 < CHUNKS:
            start_z(c + 2)

    def piece(x, c):
        return pl.ds(pl.multiple_of((2 * x + c) * out_rows, 32), out_rows)

    def product(c):
        cols = cols_of(c)
        block_bytes_wait(oz.at[2, upper, cols], z_recv.at[2, c])
        block_bytes_wait(oz.at[2, lower, cols], z_recv.at[3, c])

        def rows_tile(j, carry):
            rows = pl.ds(pl.multiple_of(j * tile, tile), tile)
            total = jnp.dot(g_turned[0, rows, :], oz[0, :, cols], preferred_element_type=f32)
            for k in (1, 2, 3):
                total += jnp.dot(g_turned[k, rows, :], oz[k, :, cols], preferred_element_type=f32)
            part[rows, cols] = total.astype(bf16)
            return carry

        lax.fori_loop(0, part.shape[0] // tile, rows_tile, 0)
        for x in range(4):
            send(
                part.at[piece(x, 1 - core), cols],
                px.at[x, :, cols],
                p_send,
                p_recv.at[c],
                sibling,
            )

    def pair_sum(x, c):
        cols = cols_of(c)
        return part[piece(x, core), cols].astype(f32) + px[x, :, cols].astype(f32)

    def send_half(c):
        cols = cols_of(c)
        block_bytes_wait(px.at[:, :, cols], p_recv.at[c])
        half_send[:, cols] = pair_sum(lax.rem(plane_x + 2, 4), c).astype(bf16)
        send(
            half_send.at[top, cols], half_recv.at[top, cols], x_send.at[0], x_recv.at[0, c], x_up
        )
        send(
            half_send.at[bottom, cols],
            half_recv.at[bottom, cols],
            x_send.at[1],
            x_recv.at[1, c],
            x_down,
        )

    def send_full(c):
        cols = cols_of(c)
        split = out_rows // 2
        block_bytes_wait(half_recv.at[top, cols], x_recv.at[0, c])
        ahead = pair_sum(lax.rem(plane_x + 1, 4), c)
        full_send[0, top, cols] = (ahead[:split] + half_recv[top, cols].astype(f32)).astype(bf16)
        full_send[0, bottom, cols] = ahead[split:].astype(bf16)
        send(
            full_send.at[0, :, cols], full_recv.at[0, :, cols], x_send.at[2], x_recv.at[2, c], x_up
        )
        block_bytes_wait(half_recv.at[bottom, cols], x_recv.at[1, c])
        behind = pair_sum(lax.rem(plane_x + 3, 4), c)
        full_send[1, top, cols] = behind[:split].astype(bf16)
        full_send[1, bottom, cols] = (behind[split:] + half_recv[bottom, cols].astype(f32)).astype(
            bf16
        )
        send(
            full_send.at[1, :, cols],
            full_recv.at[1, :, cols],
            x_send.at[3],
            x_recv.at[3, c],
            x_down,
        )

    def finish(c):
        cols = cols_of(c)
        block_bytes_wait(full_recv.at[0, :, cols], x_recv.at[2, c])
        block_bytes_wait(full_recv.at[1, :, cols], x_recv.at[3, c])
        wg_out[:, cols] = (
            pair_sum(plane_x, c)
            + full_recv[0, :, cols].astype(f32)
            + full_recv[1, :, cols].astype(f32)
        )

    def k_sum(z, x):
        return (k_own[z, x].astype(f32) + kx[z, x].astype(f32)).astype(bf16)

    def k_along_x():
        for k in (1, 2, 3):
            x = lax.rem(plane_x + k, 4)
            for z in range(4):
                ks[z, x] = k_sum(z, x)
            send(
                ks.at[:, x],
                k_row.at[plane_x],
                k_send.at[k - 1],
                k_recv.at[k - 1],
                me + 2 * (x - plane_x),
            )
        for z in range(4):
            k_row[plane_x, z] = k_sum(z, plane_x)

    def k_along_z():
        for k in range(3):
            block_bytes_wait(k_row.at[0], k_recv.at[k])
        for k in (1, 2, 3, 0):
            z = lax.rem(my_z + k, 4)
            for h in range(2):
                pair = k_row[2 * h, z].astype(f32) + k_row[2 * h + 1, z].astype(f32)
                k_pair[z, h] = pair.astype(bf16)
            if k:
                send(
                    k_pair.at[z],
                    k_col.at[my_z],
                    k_send.at[2 + k],
                    k_recv.at[2 + k],
                    lax.rem(me + 8 * k, shards),
                )
            else:
                k_col[my_z] = k_pair[z]

    def send_dq(k, carry):
        t = lax.rem(me + k, shards)
        send(dq_ref.at[t], home.at[0, my_rows, my_cols], send_sem.at[3], recv_sem.at[3], t)
        return carry

    start_z(0)
    start_z(1)
    swap.wait()
    k_along_x()
    stages = (forward_z, product, send_half, send_full, finish)
    for step in range(CHUNKS + len(stages) - 1):
        if step == K_STEP:
            k_along_z()
        if step == DQ_STEP:
            lax.fori_loop(1, shards, send_dq, 0)
        for i, stage in enumerate(stages):
            if 0 <= step - i < CHUNKS:
                stage(step - i)
    for k in range(3):
        block_bytes_wait(k_col.at[0], k_recv.at[3 + k])
    for z in range(4):
        for h in range(2):
            cols = pl.ds((2 * z + h) * DH, DH)
            home[1, :, cols] = k_col[z, h, :, :DH]
            home[2, :, cols] = k_col[z, h, :, DH:]
    block_bytes_wait(dq_ref.at[pl.ds(0, shards - 1)], recv_sem.at[3])
    block_bytes_wait(o_ref.at[pl.ds(0, shards - 1)], send_sem.at[0])
    for k in range(3):
        block_bytes_wait(ks.at[:, 0], k_send.at[k])
        block_bytes_wait(k_pair.at[0], k_send.at[3 + k])
    block_bytes_wait(dq_ref.at[pl.ds(0, shards - 1)], send_sem.at[3])
    block_bytes_wait(oz.at[0], z_send.at[0])
    block_bytes_wait(oz.at[0], z_send.at[1])
    block_bytes_wait(oz.at[1, upper], z_send.at[2])
    block_bytes_wait(oz.at[3, lower], z_send.at[3])
    block_bytes_wait(px, p_send)
    block_bytes_wait(half_send.at[top], x_send.at[0])
    block_bytes_wait(half_send.at[bottom], x_send.at[1])
    block_bytes_wait(full_send.at[0], x_send.at[2])
    block_bytes_wait(full_send.at[1], x_send.at[3])


def bring_home(o_back, dq_back, key_back, grad_parts, out_rows):
    shards, part_rows, _ = o_back.shape
    slots = key_back.shape[1]
    width = shards // 4 * DH
    rows = grad_parts[0].shape[1]
    key_back = key_back.reshape(4, 4, 2, slots, 2 * DH)
    vmem = pl.BlockSpec(memory_space=pltpu.VMEM)
    bf16 = jnp.bfloat16
    return pl.pallas_call(
        home_kernel,
        out_shape=(
            jax.ShapeDtypeStruct((3, slots, width), bf16),
            jax.ShapeDtypeStruct((out_rows, width), jnp.float32),
        ),
        in_specs=[pl.BlockSpec(memory_space=pltpu.HBM)] * 3
        + [pl.BlockSpec(memory_space=pl.ANY)] * 4,
        out_specs=(vmem,) * 2,
        scratch_shapes=[
            pltpu.VMEM((4, slots, rows), bf16),
            pltpu.VMEM((4, 4, slots, 2 * DH), bf16),
            pltpu.VMEM((4, rows, slots), bf16),
            pltpu.VMEM((4, slots, width), bf16),
            pltpu.VMEM((4, 4, slots, 2 * DH), bf16),
            pltpu.VMEM((4, 4, slots, 2 * DH), bf16),
            pltpu.VMEM((4, 4, slots, 2 * DH), bf16),
            pltpu.VMEM((4, 2, slots, 2 * DH), bf16),
            pltpu.VMEM((4, 2, slots, 2 * DH), bf16),
            pltpu.VMEM((rows, width), bf16),
            pltpu.VMEM((4, out_rows, width), bf16),
            pltpu.VMEM((out_rows, width), bf16),
            pltpu.VMEM((out_rows, width), bf16),
            pltpu.VMEM((2, out_rows, width), bf16),
            pltpu.VMEM((2, out_rows, width), bf16),
            pltpu.SemaphoreType.DMA((4,)),
            pltpu.SemaphoreType.DMA((4,)),
            pltpu.SemaphoreType.DMA((7,)),
            pltpu.SemaphoreType.DMA((6,)),
            pltpu.SemaphoreType.DMA((6,)),
            pltpu.SemaphoreType.DMA((4,)),
            pltpu.SemaphoreType.DMA((4, CHUNKS)),
            pltpu.SemaphoreType.DMA,
            pltpu.SemaphoreType.DMA((CHUNKS,)),
            pltpu.SemaphoreType.DMA((4,)),
            pltpu.SemaphoreType.DMA((4, CHUNKS)),
        ],
        compiler_params=pltpu.CompilerParams(
            collective_id=1, has_side_effects=True, vmem_limit_bytes=48 * 1024 * 1024
        ),
        name="home",
    )(o_back, dq_back, key_back, *grad_parts)


def scatter_kernel(first_ref, kept_ref, packed_ref, out_ref, rows_ref):
    slots = rows_ref.shape[0]

    @pl.when(pl.program_id(0) == 0)
    def _():
        for g in range(slots // GROUP):
            dealt = dealt_rows(g, first_ref[0], slots // 4)
            rows_ref[g * GROUP : (g + 1) * GROUP, :] = packed_ref[0, dealt, :]

    @pl.when(pl.program_id(0) > 0)
    def _():
        rows_ref[...] = packed_ref[0]

    token = lax.broadcasted_iota(jnp.int32, (out_ref.shape[1], slots), 0)
    select = jnp.where(token == kept_ref[...], 1.0, 0.0).astype(jnp.bfloat16)
    out_ref[0] = jnp.dot(
        select, rows_ref[...], preferred_element_type=jnp.float32
    ).astype(jnp.bfloat16)


def scatter(first, kept, packed, tokens):
    parts, slots, width = packed.shape
    return pl.pallas_call(
        scatter_kernel,
        grid=(parts,),
        out_shape=jax.ShapeDtypeStruct((parts, tokens, width), jnp.bfloat16),
        in_specs=[
            pl.BlockSpec(memory_space=pltpu.SMEM),
            pl.BlockSpec((1, slots), lambda i: (0, 0)),
            pl.BlockSpec((1, slots, width), lambda i: (i, 0, 0)),
        ],
        out_specs=pl.BlockSpec((1, tokens, width), lambda i: (i, 0, 0)),
        scratch_shapes=[pltpu.VMEM((slots, width), jnp.bfloat16)],
        compiler_params=pltpu.CompilerParams(vmem_limit_bytes=32 * 1024 * 1024),
        name="scatter",
    )(first, kept, packed)


def on_device(
    projections,
    output_gradient,
    output_projection_weight,
    kept_token_indices,
    surviving_token_count,
):
    tok_dev = projections.shape[0]
    group_width = projections.shape[2]
    slots = kept_token_indices.shape[1]
    heads_local = group_width // DH
    seq_count = lax.axis_size("seq")
    quarters = seq_count // heads_local
    part_rows = slots // quarters
    me = lax.axis_index("seq")
    my_quarter = (me % quarters).astype(jnp.int32)[None]

    *blocks, query_in, grad_in, key_in, value_in = spread(
        output_gradient,
        kept_token_indices,
        projections.transpose(1, 0, 2),
        output_projection_weight,
        seq_count,
    )

    def along_z(k):
        if k == 0:
            return blocks[0]
        return lax.ppermute(
            blocks[k], "seq", [(i, (i + 8 * k) % seq_count) for i in range(seq_count)]
        )

    grad_parts = [along_z(k) for k in range(4)]
    dq_back, o_back, key_back = attend(
        surviving_token_count, my_quarter, query_in, grad_in, key_in, value_in
    )
    out_rows = output_projection_weight.shape[0] // seq_count
    grad_packed, weight_grad = bring_home(o_back, dq_back, key_back, grad_parts, out_rows)
    projection_grad = scatter(my_quarter, kept_token_indices, grad_packed, tok_dev)
    projection_grad = projection_grad.transpose(1, 0, 2)
    return (projection_grad, weight_grad)


def solution(mesh):
    return jax.shard_map(
        on_device,
        mesh=mesh,
        in_specs=(P("seq", None, "head"), P("seq", "head"), P(None, "head"), P("seq", None), P()),
        out_specs=(P("seq", None, "head"), P("seq", "head")),
        check_vma=False,
    )
```

```python
import math

import jax
import jax.numpy as jnp
from jax import lax
from jax.experimental import pallas as pl
from jax.experimental.pallas import tpu as pltpu
from jax.sharding import PartitionSpec as P

DH = 128
BQ = 256
BK = 1536
TAIL = 512
GROUP = 16
NEG = -1e30
CHUNKS = 4
VMEM_BYTES = 63 * 1024 * 1024 + 640 * 1024
K_STEP = 4
DQ_STEP = 4


def contract_rows(left, right):
    return lax.dot_general(
        left, right, (((0,), (0,)), ((), ())), preferred_element_type=jnp.float32
    )


def attend_kernel(
    count_ref,
    quarter_ref,
    q_hbm,
    g_hbm,
    k_hbm,
    v_hbm,
    dq_out,
    o_out,
    k_out,
    q_ref,
    g_ref,
    k_ref,
    v_ref,
    k_stage,
    qc,
    gc,
    kc,
    vc,
    k_turned,
    v_turned,
    q_turned,
    dkc,
    dvc,
    oc,
    s_scr,
    p_scr,
    qpos,
    acc,
    group_pos,
    load_sem,
    store_sem,
):
    shards, part_rows, _ = q_ref.shape
    slots = k_ref.shape[1]
    quarter = quarter_ref[0]
    groups = part_rows // GROUP
    score_scale = 1.0 / math.sqrt(DH)
    log2e = score_scale * math.log2(math.e)
    bf16 = jnp.bfloat16
    loads = [
        pltpu.make_async_copy(src, dst, load_sem.at[i])
        for i, (src, dst) in enumerate(
            ((q_hbm, q_ref), (g_hbm, g_ref), (k_hbm, k_ref), (v_hbm, v_ref))
        )
    ]
    for load in loads:
        load.start()

    def clear(i, carry):
        rows = pl.ds(pl.multiple_of(i * slots, slots), slots)
        dkc[rows, :] = jnp.zeros((slots, DH), jnp.float32)
        dvc[rows, :] = jnp.zeros((slots, DH), jnp.float32)
        return carry

    lax.fori_loop(0, shards, clear, 0)
    q_turned[DH:, :] = jnp.where(
        lax.broadcasted_iota(jnp.int32, (DH, BQ), 0) == 0, 1.0, 0.0
    ).astype(bf16)
    for load in loads:
        load.wait()

    def dead_marks(rows, live):
        row = lax.broadcasted_iota(jnp.int32, (rows, DH), 0)
        lane = lax.broadcasted_iota(jnp.int32, (rows, DH), 1)
        return jnp.where((row >= live) & (lane == 0), NEG, 0.0).astype(bf16)

    def live_groups(s):
        live = (count_ref[s] + GROUP - 1) // GROUP
        first = lax.rem(quarter + s, 4)
        return live, first, (live - first + 3) // 4

    rows_live = GROUP * lax.fori_loop(0, shards, lambda s, n: n + live_groups(s)[2], jnp.int32(0))
    blocks = (rows_live + BQ - 1) // BQ
    end_q = blocks * BQ
    start_q = pl.multiple_of(end_q - rows_live, GROUP)
    qc[pl.ds(0, BQ), :] = jnp.zeros((BQ, DH), bf16)
    gc[pl.ds(0, BQ), :] = jnp.zeros((BQ, DH), bf16)
    qpos[pl.ds(0, BQ), :] = jnp.zeros((BQ, DH), jnp.int32)
    group_pos[0] = 0

    def pack(s, carry):
        at_k, at_q = carry
        live, first, mine = live_groups(s)
        at_k = pl.multiple_of(at_k, GROUP)
        at_q = pl.multiple_of(at_q, GROUP)
        kc[pl.ds(at_k, slots), :DH] = k_ref[s]
        kc[pl.ds(at_k, slots), DH:] = dead_marks(slots, count_ref[s])
        vc[pl.ds(at_k, slots), :] = v_ref[s]
        qc[pl.ds(at_q, part_rows), :] = q_ref[s]
        gc[pl.ds(at_q, part_rows), :] = g_ref[s]
        rows = lax.broadcasted_iota(jnp.int32, (GROUP, DH), 0)
        for i in range(groups):
            base = at_k + (first + 4 * i) * GROUP
            qpos[pl.ds(at_q + i * GROUP, GROUP), :] = base + rows
            group_pos[at_q // GROUP + i] = base
        return at_k + live * GROUP, at_q + mine * GROUP

    end_k, _ = lax.fori_loop(0, shards, pack, (jnp.int32(0), start_q))
    end_k = pl.multiple_of(end_k, GROUP)
    kc[pl.ds(end_k, BK), :DH] = jnp.zeros((BK, DH), bf16)
    kc[pl.ds(end_k, BK), DH:] = dead_marks(BK, 0)
    vc[pl.ds(end_k, BK), :] = jnp.zeros((BK, DH), bf16)
    oc[pl.ds(pl.multiple_of(end_q, BQ), part_rows), :] = jnp.zeros(
        (part_rows, 2 * DH), bf16
    )

    def turn(c, carry):
        keys = pl.ds(pl.multiple_of(c * BK, BK), BK)
        k_turned[:, keys] = kc[keys, :DH].T
        v_turned[:, keys] = vc[keys, :].T
        return carry

    lax.fori_loop(0, (end_k + BK - 1) // BK, turn, 0)

    def block(b, carry):
        rows = pl.ds(pl.multiple_of(b * BQ, BQ), BQ)
        key_end = group_pos[(b + 1) * (BQ // GROUP) - 1] + GROUP
        chunks = (key_end + TAIL - 1) // BK
        tails = (jnp.maximum(key_end - chunks * BK, 0) + TAIL - 1) // TAIL
        first_end = jnp.where(b == 0, 0, group_pos[b * (BQ // GROUP)] + 1)
        clear_chunks = jnp.minimum(first_end // BK, chunks)

        def over(body, carry):
            carry = lax.fori_loop(0, chunks, lambda c, x: body(c * BK, BK, x), carry)
            return lax.fori_loop(
                0, tails, lambda c, x: body(chunks * BK + c * TAIL, TAIL, x), carry
            )

        q_turned[:DH, :] = qc[rows, :].T
        last_key = qpos[rows, :].T[0:1, :]

        def score(at, size, top, masked):
            at = pl.multiple_of(at, TAIL)
            keys = pl.ds(at, size)
            s = jnp.dot(kc[keys, :], q_turned[...], preferred_element_type=jnp.float32)
            if masked:
                key = at + lax.broadcasted_iota(jnp.int32, (size, BQ), 0)
                s = jnp.where(key <= last_key, s, NEG)
            s_scr[keys, :] = s
            return jnp.maximum(top, jnp.max(s, axis=0, keepdims=True))

        top = jnp.full((1, BQ), NEG, jnp.float32)
        top = lax.fori_loop(0, clear_chunks, lambda c, t: score(c * BK, BK, t, False), top)
        top = lax.fori_loop(clear_chunks, chunks, lambda c, t: score(c * BK, BK, t, True), top)
        top = lax.fori_loop(
            0, tails, lambda c, t: score(chunks * BK + c * TAIL, TAIL, t, True), top
        )
        acc[...] = jnp.zeros((DH, BQ), jnp.float32)

        def weigh(at, size, total):
            keys = pl.ds(pl.multiple_of(at, TAIL), size)
            p = jnp.exp2((s_scr[keys, :] - top) * log2e)
            p_low = p.astype(bf16)
            p_scr[keys, :] = p_low
            acc[...] += jnp.dot(v_turned[:, keys], p_low, preferred_element_type=jnp.float32)
            return total + jnp.sum(p, axis=0, keepdims=True)

        total = over(weigh, jnp.zeros((1, BQ), jnp.float32))
        inverse = 1.0 / total
        attended = acc[...] * inverse
        oc[rows, DH:] = attended.T.astype(bf16)
        g_turned = (gc[rows, :].astype(jnp.float32).T * inverse).astype(bf16)
        row_dot = jnp.sum(g_turned.astype(jnp.float32) * attended, axis=0, keepdims=True)
        g_part = g_turned.T
        acc[...] = jnp.zeros((DH, BQ), jnp.float32)

        def back(at, size, carry):
            keys = pl.ds(pl.multiple_of(at, TAIL), size)
            p_low = p_scr[keys, :]
            grad_probs = jnp.dot(vc[keys, :], g_turned, preferred_element_type=jnp.float32)
            ds = (p_low.astype(jnp.float32) * (grad_probs - row_dot)).astype(bf16)
            acc[...] += jnp.dot(k_turned[:, keys], ds, preferred_element_type=jnp.float32)
            dkc[keys, :] += jnp.dot(ds, qc[rows, :], preferred_element_type=jnp.float32)
            dvc[keys, :] += jnp.dot(p_low, g_part, preferred_element_type=jnp.float32)
            return carry

        over(back, 0)
        oc[rows, :DH] = (acc[...] * score_scale).T.astype(bf16)
        return carry

    lax.fori_loop(0, blocks, block, 0)

    def unpack(s, carry):
        at_k, at_q = carry
        live, first, mine = live_groups(s)
        at_k = pl.multiple_of(at_k, GROUP)
        at_q = pl.multiple_of(at_q, GROUP)
        q_ref[s] = oc[pl.ds(at_q, part_rows), :DH]
        g_ref[s] = oc[pl.ds(at_q, part_rows), DH:]
        k_stage[s, :, :DH] = (dkc[pl.ds(at_k, slots), :] * score_scale).astype(bf16)
        k_stage[s, :, DH:] = dvc[pl.ds(at_k, slots), :].astype(bf16)
        pltpu.make_async_copy(k_stage.at[s], k_out.at[s], store_sem.at[0]).start()
        return at_k + live * GROUP, at_q + mine * GROUP

    lax.fori_loop(0, shards, unpack, (jnp.int32(0), start_q))
    stores = [
        pltpu.make_async_copy(q_ref, dq_out, store_sem.at[1]),
        pltpu.make_async_copy(g_ref, o_out, store_sem.at[2]),
    ]
    for store in stores:
        store.start()
    pltpu.make_async_copy(k_stage, k_out, store_sem.at[0]).wait()
    for store in stores:
        store.wait()


def attend(counts, quarter, query_in, grad_in, key_in, value_in):
    shards, part_rows, _ = query_in.shape
    slots = key_in.shape[1]
    keys = shards * slots
    queries = shards * part_rows
    bf16 = jnp.bfloat16
    smem = pl.BlockSpec(memory_space=pltpu.SMEM)
    hbm = pl.BlockSpec(memory_space=pltpu.HBM)
    return pl.pallas_call(
        attend_kernel,
        out_shape=(
            jax.ShapeDtypeStruct((shards, part_rows, DH), bf16),
            jax.ShapeDtypeStruct((shards, part_rows, DH), bf16),
            jax.ShapeDtypeStruct((shards, slots, 2 * DH), bf16),
        ),
        in_specs=[smem, smem, hbm, hbm, hbm, hbm],
        out_specs=(hbm, hbm, hbm),
        scratch_shapes=[
            pltpu.VMEM((shards, part_rows, DH), bf16),
            pltpu.VMEM((shards, part_rows, DH), bf16),
            pltpu.VMEM((shards, slots, DH), bf16),
            pltpu.VMEM((shards, slots, DH), bf16),
            pltpu.VMEM((shards, slots, 2 * DH), bf16),
            pltpu.VMEM((queries + BQ, DH), bf16),
            pltpu.VMEM((queries + BQ, DH), bf16),
            pltpu.VMEM((keys + BK, 2 * DH), bf16),
            pltpu.VMEM((keys + BK, DH), bf16),
            pltpu.VMEM((DH, keys), bf16),
            pltpu.VMEM((DH, keys), bf16),
            pltpu.VMEM((2 * DH, BQ), bf16),
            pltpu.VMEM((keys, DH), jnp.float32),
            pltpu.VMEM((keys, DH), jnp.float32),
            pltpu.VMEM((queries + BQ, 2 * DH), bf16),
            pltpu.VMEM((keys, BQ), jnp.float32),
            pltpu.VMEM((keys, BQ), bf16),
            pltpu.VMEM((queries + BQ, DH), jnp.int32),
            pltpu.VMEM((DH, BQ), jnp.float32),
            pltpu.SMEM((queries // GROUP + 8,), jnp.int32),
            pltpu.SemaphoreType.DMA((4,)),
            pltpu.SemaphoreType.DMA((3,)),
        ],
        compiler_params=pltpu.CompilerParams(vmem_limit_bytes=VMEM_BYTES),
        cost_estimate=pl.CostEstimate(
            flops=6 * queries * keys * DH, bytes_accessed=16 * 1024 * 1024, transcendentals=0
        ),
        name="attend",
    )(counts, quarter, query_in, grad_in, key_in, value_in)


def block_bytes_wait(ref, sem):
    pltpu.make_async_copy(ref, ref, sem).wait()


def greet(peers, peer_of, ring=0, meanwhile=None):
    barrier = pltpu.get_barrier_semaphore()

    def signal(k, carry):
        pl.semaphore_signal(
            barrier, inc=1, device_id={"seq": peer_of(k)}, device_id_type=pl.DeviceIdType.MESH
        )
        return carry

    lax.fori_loop(1, peers + 1, signal, 0)
    if ring:
        row = lax.axis_index("head")
        for k in range(1, ring):
            pl.semaphore_signal(
                barrier,
                inc=1,
                device_id={"head": lax.rem(row + k, ring)},
                device_id_type=pl.DeviceIdType.MESH,
            )
        peers = peers + ring - 1
    if meanwhile is not None:
        meanwhile()
    pl.semaphore_wait(barrier, peers)


def send(src, dst, send_sem, recv_sem, target, axis="seq"):
    copy = pltpu.make_async_remote_copy(
        src_ref=src,
        dst_ref=dst,
        send_sem=send_sem,
        recv_sem=recv_sem,
        device_id={axis: target},
        device_id_type=pl.DeviceIdType.MESH,
    )
    copy.start()
    return copy


def dealt_rows(group, first, part_rows):
    at = lax.rem(group + 4 - first, 4) * part_rows + group // 4 * GROUP
    return pl.ds(pl.multiple_of(at, GROUP), GROUP)


def spread_kernel(
    all_grad_ref,
    kept_ref,
    p_hbm,
    w_hbm,
    g0_out,
    g1_out,
    g2_out,
    g3_out,
    q_in,
    g_in,
    k_in,
    v_in,
    w_ref,
    p_ref,
    select,
    grad_ref,
    q_ref,
    k_ref,
    v_ref,
    acc,
    g_local,
    gblk,
    k_col,
    v_col,
    w_sem,
    p_sem,
    copy_sem,
    y_send,
    y_recv,
    z_send,
    z_recv,
    x_send,
    x_recv,
    own_sem,
    pass_send,
    pass_recv,
    q_send,
    q_recv,
    q_own,
):
    shards, part_rows, _ = q_in.shape
    slots, cols = grad_ref.shape
    half = cols // 2
    me = lax.axis_index("seq")
    row = lax.axis_index("head")
    core = me % 2
    sibling = me + 1 - 2 * core
    my_z = me // 8
    my_x = me // 2 % 4
    my_head = me // 4
    my_rows = pl.ds(pl.multiple_of((me % 4) * part_rows, GROUP), part_rows)

    load_w = pltpu.make_async_copy(w_hbm, w_ref, w_sem)
    load_p = pltpu.make_async_copy(p_hbm, p_ref, p_sem)
    load_p.start()
    load_w.start()
    width = 256
    tiles = acc.shape[1] // width

    def pick():
        token = lax.broadcasted_iota(jnp.int32, select.shape, 0)
        select[...] = jnp.where(token == kept_ref[...], 1.0, 0.0).astype(jnp.bfloat16)

        def deal(out, at, values):
            for g in range(slots // GROUP):
                out[dealt_rows(g, me % 4, part_rows), at] = values[g * GROUP : (g + 1) * GROUP]

        def grad_tile(j, carry):
            at = pl.ds(pl.multiple_of(j * width, width), width)
            picked = contract_rows(select[...], all_grad_ref[:, at])
            deal(grad_ref, at, picked.astype(jnp.bfloat16))
            return carry

        lax.fori_loop(0, cols // width, grad_tile, 0)
        load_p.wait()

        def tile(j, carry):
            at = pl.ds(pl.multiple_of(j * width, width), width)
            picked = [
                contract_rows(select[...], p_ref[i, :, at]).astype(jnp.bfloat16) for i in range(3)
            ]
            deal(q_ref, at, picked[0])
            k_ref[:, at] = picked[1]
            v_ref[:, at] = picked[2]
            return carry

        lax.fori_loop(0, tiles, tile, 0)

    greet(shards - 1, lambda k: lax.rem(me + k, shards), 4, pick)

    def head_cols(head):
        return pl.ds(pl.multiple_of(head * DH, DH), DH)

    def pair_cols(z):
        return pl.ds(pl.multiple_of(z * 2 * DH, 2 * DH), 2 * DH)

    def slot_of(y):
        return lax.rem(y - my_z + 4, 4)

    right, left, across = lax.rem(row + 1, 4), lax.rem(row + 3, 4), lax.rem(row + 2, 4)
    to_right = send(grad_ref, gblk.at[slot_of(row)], y_send.at[0], y_recv.at[0], right, "head")
    to_left = send(grad_ref, gblk.at[slot_of(row)], y_send.at[1], y_recv.at[1], left, "head")

    sides = ((k_ref, k_col, k_in), (v_ref, v_col, v_in))
    for k in (1, 3, 2):
        target = lax.rem(me + 8 * k, shards)
        for i, (src, col, _) in enumerate(sides):
            send(
                src.at[:, pair_cols(lax.rem(my_z + k, 4))],
                col.at[my_z],
                z_send.at[i],
                z_recv.at[i, k],
                target,
            )

    def fan(k):
        z = lax.rem(my_z - k + 4, 4)
        for i, (src, col, out) in enumerate(sides):
            if k:
                block_bytes_wait(col.at[z], z_recv.at[i, k])
            else:
                col[z] = src[:, pair_cols(my_z)]
            for d in (1, 3, 2):
                x = lax.rem(my_x + d, 4)
                send(
                    col.at[z, :, head_cols(x // 2)],
                    out.at[z, my_x, core],
                    x_send.at[i],
                    x_recv.at[i, k],
                    me + 2 * (x - my_x),
                )
            pltpu.make_async_copy(
                col.at[z, :, head_cols(my_x // 2)], out.at[z, my_x, core], own_sem.at[i, k]
            ).start()

    def pass_on(k):
        z = lax.rem(my_z - k + 4, 4)
        for i, (_, _, out) in enumerate(sides):
            block_bytes_wait(out.at[z, pl.ds(0, 3), core], x_recv.at[i, k])
            block_bytes_wait(out.at[z, my_x, core], own_sem.at[i, k])
            send(out.at[z, :, core], out.at[z, :, core], pass_send.at[i], pass_recv.at[i], sibling)

    fan(0)

    def send_q(k, carry):
        t = lax.rem(me + k, shards)
        rows = pl.ds(pl.multiple_of((t % 4) * part_rows, GROUP), part_rows)
        send(q_ref.at[rows, head_cols(t // 4)], q_in.at[me], q_send.at[0], q_recv.at[0], t)
        return carry

    lax.fori_loop(1, shards, send_q, 0)
    own_q = pltpu.make_async_copy(q_ref.at[my_rows, head_cols(my_head)], q_in.at[me], q_own.at[0])
    own_q.start()

    gblk[slot_of(row)] = grad_ref[...]
    load_w.wait()

    def multiply(y, first):
        def tile(j, carry):
            at = pl.ds(pl.multiple_of(j * width, width), width)
            rows = pl.ds(pl.multiple_of(y * cols, width), cols)
            part = jnp.dot(gblk[slot_of(y)], w_ref[rows, at], preferred_element_type=jnp.float32)
            acc[:, at] = part if first else acc[:, at] + part
            return carry

        lax.fori_loop(0, tiles, tile, 0)

    multiply(row, True)
    for k in (1, 3, 2):
        fan(k)
    to_right.wait_recv()
    from_left = gblk.at[slot_of(left), :, pl.ds(0, half)]
    on_right = send(from_left, from_left, y_send.at[2], y_recv.at[2], right, "head")
    to_left.wait_recv()
    from_right = gblk.at[slot_of(right), :, pl.ds(half, half)]
    on_left = send(from_right, from_right, y_send.at[3], y_recv.at[3], left, "head")
    pass_on(0)
    multiply(left, False)
    pass_on(1)
    multiply(right, False)
    pass_on(3)
    on_right.wait_recv()
    on_left.wait_recv()

    def finish(step, carry):
        j = lax.rem(my_head // 2 + step, tiles)
        at = pl.ds(pl.multiple_of(j * width, width), width)
        rows = pl.ds(pl.multiple_of(across * cols, width), cols)
        part = jnp.dot(gblk[slot_of(across)], w_ref[rows, at], preferred_element_type=jnp.float32)
        g_local[:, at] = (acc[:, at] + part).astype(jnp.bfloat16)
        for i in range(8):
            t = j * 8 + i
            part_at = (i % 4) * part_rows

            @pl.when(t != me)
            def _():
                send(
                    g_local.at[pl.ds(part_at, part_rows), head_cols(t // 4)],
                    g_in.at[me],
                    q_send.at[1],
                    q_recv.at[1],
                    t,
                )

        return carry

    lax.fori_loop(0, tiles, finish, 0)
    own_g = pltpu.make_async_copy(
        g_local.at[my_rows, head_cols(my_head)], g_in.at[me], q_own.at[1]
    )
    own_g.start()
    copies = [
        pltpu.make_async_copy(gblk.at[k], out, copy_sem.at[k])
        for k, out in enumerate((g0_out, g1_out, g2_out, g3_out))
    ]
    for copy in copies:
        copy.start()
    pass_on(2)
    for copy in copies:
        copy.wait()
    own_q.wait()
    own_g.wait()

    others = pl.ds(0, shards - 1)
    block_bytes_wait(q_in.at[others], q_recv.at[0])
    block_bytes_wait(q_in.at[others], q_send.at[0])
    for i, (_, col, out) in enumerate(sides):
        block_bytes_wait(out.at[:, :, core], pass_recv.at[i])
        block_bytes_wait(out.at[:, :, core], pass_send.at[i])
        block_bytes_wait(col.at[pl.ds(0, 3)], z_send.at[i])
        block_bytes_wait(out.at[:, pl.ds(0, 3), core], x_send.at[i])
    for copy in (to_right, to_left, on_right, on_left):
        copy.wait_send()
    block_bytes_wait(g_in.at[others], q_recv.at[1])
    block_bytes_wait(g_in.at[others], q_send.at[1])


def spread(output_gradient, kept, projections, weight, shards):
    tokens, cols = output_gradient.shape
    slots = kept.shape[1]
    depth, width = weight.shape
    part_rows = slots // 4
    bf16 = jnp.bfloat16
    vmem = pl.BlockSpec(memory_space=pltpu.VMEM)
    block = jax.ShapeDtypeStruct((slots, cols), bf16)
    small = jax.ShapeDtypeStruct((shards, part_rows, DH), bf16)
    large = jax.ShapeDtypeStruct((4, 4, 2, slots, DH), bf16)
    *blocks, query_in, grad_in, key_in, value_in = pl.pallas_call(
        spread_kernel,
        out_shape=(block,) * 4 + (small,) * 2 + (large,) * 2,
        in_specs=[vmem] * 2 + [pl.BlockSpec(memory_space=pltpu.HBM)] * 2,
        out_specs=(pl.BlockSpec(memory_space=pltpu.HBM),) * 8,
        scratch_shapes=[
            pltpu.VMEM((depth, width), bf16),
            pltpu.VMEM(projections.shape, bf16),
            pltpu.VMEM((tokens, slots), bf16),
            pltpu.VMEM((slots, cols), bf16),
            pltpu.VMEM((slots, width), bf16),
            pltpu.VMEM((slots, width), bf16),
            pltpu.VMEM((slots, width), bf16),
            pltpu.VMEM((slots, width), jnp.float32),
            pltpu.VMEM((slots, width), bf16),
            pltpu.VMEM((4, slots, cols), bf16),
            pltpu.VMEM((4, slots, 2 * DH), bf16),
            pltpu.VMEM((4, slots, 2 * DH), bf16),
            pltpu.SemaphoreType.DMA,
            pltpu.SemaphoreType.DMA,
            pltpu.SemaphoreType.DMA((4,)),
            pltpu.SemaphoreType.DMA((4,)),
            pltpu.SemaphoreType.DMA((4,)),
            pltpu.SemaphoreType.DMA((2,)),
            pltpu.SemaphoreType.DMA((2, 4)),
            pltpu.SemaphoreType.DMA((2,)),
            pltpu.SemaphoreType.DMA((2, 4)),
            pltpu.SemaphoreType.DMA((2, 4)),
            pltpu.SemaphoreType.DMA((2,)),
            pltpu.SemaphoreType.DMA((2,)),
            pltpu.SemaphoreType.DMA((2,)),
            pltpu.SemaphoreType.DMA((2,)),
            pltpu.SemaphoreType.DMA((2,)),
        ],
        compiler_params=pltpu.CompilerParams(
            collective_id=2, has_side_effects=True, vmem_limit_bytes=VMEM_BYTES
        ),
        name="spread",
    )(output_gradient, kept, projections, weight)
    key_in = key_in.reshape(shards, slots, DH)
    value_in = value_in.reshape(shards, slots, DH)
    return (*blocks, query_in, grad_in, key_in, value_in)


def home_kernel(
    o_ref,
    dq_ref,
    k_ref,
    g0_ref,
    g1_ref,
    g2_ref,
    g3_ref,
    home,
    wg_out,
    g_vmem,
    k_own,
    g_turned,
    oz,
    kx,
    ks,
    k_row,
    k_pair,
    k_col,
    part,
    px,
    half_send,
    half_recv,
    full_send,
    full_recv,
    send_sem,
    recv_sem,
    load_sem,
    k_send,
    k_recv,
    z_send,
    z_recv,
    p_send,
    p_recv,
    x_send,
    x_recv,
):
    shards, part_rows, _ = o_ref.shape
    slots = k_ref.shape[3]
    me = lax.axis_index("seq")
    core = me % 2
    sibling = me + 1 - 2 * core
    plane_x = me // 2 % 4
    my_z = me // 8
    out_rows, width = wg_out.shape
    my_rows = pl.ds(pl.multiple_of((me % 4) * part_rows, GROUP), part_rows)
    my_cols = pl.ds(pl.multiple_of((me // 4) * DH, DH), DH)
    f32, bf16 = jnp.float32, jnp.bfloat16

    loads = [
        pltpu.make_async_copy(src, dst, load_sem.at[i])
        for i, (src, dst) in enumerate(
            (
                (o_ref.at[me], oz.at[0, my_rows, my_cols]),
                (g0_ref, g_vmem.at[0]),
                (g1_ref, g_vmem.at[1]),
                (g2_ref, g_vmem.at[2]),
                (g3_ref, g_vmem.at[3]),
                (k_ref.at[:, :, core], k_own),
                (dq_ref.at[me], home.at[0, my_rows, my_cols]),
            )
        )
    ]
    for load in loads:
        load.start()
    greet(shards - 1, lambda k: lax.rem(me + k, shards))

    def send_o(k, carry):
        t = lax.rem(me + k, shards)
        send(o_ref.at[t], oz.at[0, my_rows, my_cols], send_sem.at[0], recv_sem.at[0], t)
        return carry

    lax.fori_loop(1, shards, send_o, 0)
    swap = send(k_ref.at[:, :, 1 - core], kx, send_sem.at[1], recv_sem.at[1], sibling)
    for load in loads:
        load.wait()

    tile = 256

    def turn(j, carry):
        cols = pl.ds(pl.multiple_of(j * tile, tile), tile)
        for k in range(4):
            g_turned[k, cols, :] = g_vmem[k, :, cols].T
        return carry

    lax.fori_loop(0, part.shape[0] // tile, turn, 0)
    block_bytes_wait(o_ref.at[pl.ds(0, shards - 1)], recv_sem.at[0])

    chunk = width // CHUNKS
    z_up, z_down = lax.rem(me + 8, shards), lax.rem(me + 24, shards)
    x_up = me + 2 * (lax.rem(plane_x + 1, 4) - plane_x)
    x_down = me + 2 * (lax.rem(plane_x + 3, 4) - plane_x)
    upper, lower = pl.ds(0, slots // 2), pl.ds(slots // 2, slots // 2)
    top, bottom = pl.ds(0, out_rows // 2), pl.ds(out_rows // 2, out_rows // 2)

    def cols_of(c):
        return pl.ds(c * chunk, chunk)

    def start_z(c):
        own = oz.at[0, :, cols_of(c)]
        send(own, oz.at[1, :, cols_of(c)], z_send.at[0], z_recv.at[0, c], z_up)
        send(own, oz.at[3, :, cols_of(c)], z_send.at[1], z_recv.at[1, c], z_down)

    def forward_z(c):
        cols = cols_of(c)
        block_bytes_wait(oz.at[1, :, cols], z_recv.at[0, c])
        send(
            oz.at[1, upper, cols], oz.at[2, upper, cols], z_send.at[2], z_recv.at[2, c], z_up
        )
        block_bytes_wait(oz.at[3, :, cols], z_recv.at[1, c])
        send(
            oz.at[3, lower, cols], oz.at[2, lower, cols], z_send.at[3], z_recv.at[3, c], z_down
        )
        if c + 2 < CHUNKS:
            start_z(c + 2)

    def piece(x, c):
        return pl.ds(pl.multiple_of((2 * x + c) * out_rows, 32), out_rows)

    def product(c):
        cols = cols_of(c)
        block_bytes_wait(oz.at[2, upper, cols], z_recv.at[2, c])
        block_bytes_wait(oz.at[2, lower, cols], z_recv.at[3, c])

        def rows_tile(j, carry):
            rows = pl.ds(pl.multiple_of(j * tile, tile), tile)
            total = jnp.dot(g_turned[0, rows, :], oz[0, :, cols], preferred_element_type=f32)
            for k in (1, 2, 3):
                total += jnp.dot(g_turned[k, rows, :], oz[k, :, cols], preferred_element_type=f32)
            part[rows, cols] = total.astype(bf16)
            return carry

        lax.fori_loop(0, part.shape[0] // tile, rows_tile, 0)
        for x in range(4):
            send(
                part.at[piece(x, 1 - core), cols],
                px.at[x, :, cols],
                p_send,
                p_recv.at[c],
                sibling,
            )

    def pair_sum(x, c):
        cols = cols_of(c)
        return part[piece(x, core), cols].astype(f32) + px[x, :, cols].astype(f32)

    def send_half(c):
        cols = cols_of(c)
        block_bytes_wait(px.at[:, :, cols], p_recv.at[c])
        half_send[:, cols] = pair_sum(lax.rem(plane_x + 2, 4), c).astype(bf16)
        send(
            half_send.at[top, cols], half_recv.at[top, cols], x_send.at[0], x_recv.at[0, c], x_up
        )
        send(
            half_send.at[bottom, cols],
            half_recv.at[bottom, cols],
            x_send.at[1],
            x_recv.at[1, c],
            x_down,
        )

    def send_full(c):
        cols = cols_of(c)
        split = out_rows // 2
        block_bytes_wait(half_recv.at[top, cols], x_recv.at[0, c])
        ahead = pair_sum(lax.rem(plane_x + 1, 4), c)
        full_send[0, top, cols] = (ahead[:split] + half_recv[top, cols].astype(f32)).astype(bf16)
        full_send[0, bottom, cols] = ahead[split:].astype(bf16)
        send(
            full_send.at[0, :, cols], full_recv.at[0, :, cols], x_send.at[2], x_recv.at[2, c], x_up
        )
        block_bytes_wait(half_recv.at[bottom, cols], x_recv.at[1, c])
        behind = pair_sum(lax.rem(plane_x + 3, 4), c)
        full_send[1, top, cols] = behind[:split].astype(bf16)
        full_send[1, bottom, cols] = (behind[split:] + half_recv[bottom, cols].astype(f32)).astype(
            bf16
        )
        send(
            full_send.at[1, :, cols],
            full_recv.at[1, :, cols],
            x_send.at[3],
            x_recv.at[3, c],
            x_down,
        )

    def finish(c):
        cols = cols_of(c)
        block_bytes_wait(full_recv.at[0, :, cols], x_recv.at[2, c])
        block_bytes_wait(full_recv.at[1, :, cols], x_recv.at[3, c])
        wg_out[:, cols] = (
            pair_sum(plane_x, c)
            + full_recv[0, :, cols].astype(f32)
            + full_recv[1, :, cols].astype(f32)
        )

    def k_sum(z, x):
        return (k_own[z, x].astype(f32) + kx[z, x].astype(f32)).astype(bf16)

    def k_along_x():
        for k in (1, 2, 3):
            x = lax.rem(plane_x + k, 4)
            for z in range(4):
                ks[z, x] = k_sum(z, x)
            send(
                ks.at[:, x],
                k_row.at[plane_x],
                k_send.at[k - 1],
                k_recv.at[k - 1],
                me + 2 * (x - plane_x),
            )
        for z in range(4):
            k_row[plane_x, z] = k_sum(z, plane_x)

    def k_along_z():
        for k in range(3):
            block_bytes_wait(k_row.at[0], k_recv.at[k])
        for k in (1, 2, 3, 0):
            z = lax.rem(my_z + k, 4)
            for h in range(2):
                pair = k_row[2 * h, z].astype(f32) + k_row[2 * h + 1, z].astype(f32)
                k_pair[z, h] = pair.astype(bf16)
            if k:
                send(
                    k_pair.at[z],
                    k_col.at[my_z],
                    k_send.at[2 + k],
                    k_recv.at[2 + k],
                    lax.rem(me + 8 * k, shards),
                )
            else:
                k_col[my_z] = k_pair[z]

    def send_dq(k, carry):
        t = lax.rem(me + k, shards)
        send(dq_ref.at[t], home.at[0, my_rows, my_cols], send_sem.at[3], recv_sem.at[3], t)
        return carry

    start_z(0)
    start_z(1)
    swap.wait()
    k_along_x()
    stages = (forward_z, product, send_half, send_full, finish)
    for step in range(CHUNKS + len(stages) - 1):
        if step == K_STEP:
            k_along_z()
        if step == DQ_STEP:
            lax.fori_loop(1, shards, send_dq, 0)
        for i, stage in enumerate(stages):
            if 0 <= step - i < CHUNKS:
                stage(step - i)
    for k in range(3):
        block_bytes_wait(k_col.at[0], k_recv.at[3 + k])
    for z in range(4):
        for h in range(2):
            cols = pl.ds((2 * z + h) * DH, DH)
            home[1, :, cols] = k_col[z, h, :, :DH]
            home[2, :, cols] = k_col[z, h, :, DH:]
    block_bytes_wait(dq_ref.at[pl.ds(0, shards - 1)], recv_sem.at[3])
    block_bytes_wait(o_ref.at[pl.ds(0, shards - 1)], send_sem.at[0])
    for k in range(3):
        block_bytes_wait(ks.at[:, 0], k_send.at[k])
        block_bytes_wait(k_pair.at[0], k_send.at[3 + k])
    block_bytes_wait(dq_ref.at[pl.ds(0, shards - 1)], send_sem.at[3])
    block_bytes_wait(oz.at[0], z_send.at[0])
    block_bytes_wait(oz.at[0], z_send.at[1])
    block_bytes_wait(oz.at[1, upper], z_send.at[2])
    block_bytes_wait(oz.at[3, lower], z_send.at[3])
    block_bytes_wait(px, p_send)
    block_bytes_wait(half_send.at[top], x_send.at[0])
    block_bytes_wait(half_send.at[bottom], x_send.at[1])
    block_bytes_wait(full_send.at[0], x_send.at[2])
    block_bytes_wait(full_send.at[1], x_send.at[3])


def bring_home(o_back, dq_back, key_back, grad_parts, out_rows):
    shards, part_rows, _ = o_back.shape
    slots = key_back.shape[1]
    width = shards // 4 * DH
    rows = grad_parts[0].shape[1]
    key_back = key_back.reshape(4, 4, 2, slots, 2 * DH)
    vmem = pl.BlockSpec(memory_space=pltpu.VMEM)
    bf16 = jnp.bfloat16
    return pl.pallas_call(
        home_kernel,
        out_shape=(
            jax.ShapeDtypeStruct((3, slots, width), bf16),
            jax.ShapeDtypeStruct((out_rows, width), jnp.float32),
        ),
        in_specs=[pl.BlockSpec(memory_space=pltpu.HBM)] * 3
        + [pl.BlockSpec(memory_space=pl.ANY)] * 4,
        out_specs=(vmem,) * 2,
        scratch_shapes=[
            pltpu.VMEM((4, slots, rows), bf16),
            pltpu.VMEM((4, 4, slots, 2 * DH), bf16),
            pltpu.VMEM((4, rows, slots), bf16),
            pltpu.VMEM((4, slots, width), bf16),
            pltpu.VMEM((4, 4, slots, 2 * DH), bf16),
            pltpu.VMEM((4, 4, slots, 2 * DH), bf16),
            pltpu.VMEM((4, 4, slots, 2 * DH), bf16),
            pltpu.VMEM((4, 2, slots, 2 * DH), bf16),
            pltpu.VMEM((4, 2, slots, 2 * DH), bf16),
            pltpu.VMEM((rows, width), bf16),
            pltpu.VMEM((4, out_rows, width), bf16),
            pltpu.VMEM((out_rows, width), bf16),
            pltpu.VMEM((out_rows, width), bf16),
            pltpu.VMEM((2, out_rows, width), bf16),
            pltpu.VMEM((2, out_rows, width), bf16),
            pltpu.SemaphoreType.DMA((4,)),
            pltpu.SemaphoreType.DMA((4,)),
            pltpu.SemaphoreType.DMA((7,)),
            pltpu.SemaphoreType.DMA((6,)),
            pltpu.SemaphoreType.DMA((6,)),
            pltpu.SemaphoreType.DMA((4,)),
            pltpu.SemaphoreType.DMA((4, CHUNKS)),
            pltpu.SemaphoreType.DMA,
            pltpu.SemaphoreType.DMA((CHUNKS,)),
            pltpu.SemaphoreType.DMA((4,)),
            pltpu.SemaphoreType.DMA((4, CHUNKS)),
        ],
        compiler_params=pltpu.CompilerParams(
            collective_id=1, has_side_effects=True, vmem_limit_bytes=VMEM_BYTES
        ),
        name="home",
    )(o_back, dq_back, key_back, *grad_parts)


def scatter_kernel(
    first_ref, kept_ref, packed_ref, weight_ref, out_ref, weight_out, rows_ref, move_sem
):
    slots = rows_ref.shape[0]
    move = pltpu.make_async_copy(weight_ref, weight_out, move_sem)

    @pl.when(pl.program_id(0) == 0)
    def _():
        move.start()
        for g in range(slots // GROUP):
            dealt = dealt_rows(g, first_ref[0], slots // 4)
            rows_ref[g * GROUP : (g + 1) * GROUP, :] = packed_ref[0, dealt, :]

    @pl.when(pl.program_id(0) > 0)
    def _():
        rows_ref[...] = packed_ref[0]

    token = lax.broadcasted_iota(jnp.int32, (out_ref.shape[1], slots), 0)
    select = jnp.where(token == kept_ref[...], 1.0, 0.0).astype(jnp.bfloat16)
    out_ref[0] = jnp.dot(
        select, rows_ref[...], preferred_element_type=jnp.float32
    ).astype(jnp.bfloat16)

    @pl.when(pl.program_id(0) == pl.num_programs(0) - 1)
    def _():
        move.wait()


def scatter(first, kept, packed, weight_grad, tokens):
    parts, slots, width = packed.shape
    return pl.pallas_call(
        scatter_kernel,
        grid=(parts,),
        out_shape=(
            jax.ShapeDtypeStruct((parts, tokens, width), jnp.bfloat16),
            jax.ShapeDtypeStruct(weight_grad.shape, jnp.float32),
        ),
        in_specs=[
            pl.BlockSpec(memory_space=pltpu.SMEM),
            pl.BlockSpec((1, slots), lambda i: (0, 0)),
            pl.BlockSpec((1, slots, width), lambda i: (i, 0, 0)),
            pl.BlockSpec(memory_space=pl.ANY),
        ],
        out_specs=(
            pl.BlockSpec((1, tokens, width), lambda i: (i, 0, 0)),
            pl.BlockSpec(memory_space=pl.ANY),
        ),
        scratch_shapes=[pltpu.VMEM((slots, width), jnp.bfloat16), pltpu.SemaphoreType.DMA],
        compiler_params=pltpu.CompilerParams(vmem_limit_bytes=VMEM_BYTES),
        name="scatter",
    )(first, kept, packed, weight_grad)


def on_device(
    projections,
    output_gradient,
    output_projection_weight,
    kept_token_indices,
    surviving_token_count,
):
    tok_dev = projections.shape[0]
    group_width = projections.shape[2]
    slots = kept_token_indices.shape[1]
    heads_local = group_width // DH
    seq_count = lax.axis_size("seq")
    quarters = seq_count // heads_local
    part_rows = slots // quarters
    me = lax.axis_index("seq")
    my_quarter = (me % quarters).astype(jnp.int32)[None]

    *blocks, query_in, grad_in, key_in, value_in = spread(
        output_gradient,
        kept_token_indices,
        projections.transpose(1, 0, 2),
        output_projection_weight,
        seq_count,
    )

    def along_z(k):
        if k == 0:
            return blocks[0]
        return lax.ppermute(
            blocks[k], "seq", [(i, (i + 8 * k) % seq_count) for i in range(seq_count)]
        )

    grad_parts = [along_z(k) for k in range(4)]
    dq_back, o_back, key_back = attend(
        surviving_token_count, my_quarter, query_in, grad_in, key_in, value_in
    )
    out_rows = output_projection_weight.shape[0] // seq_count
    grad_packed, weight_grad = bring_home(o_back, dq_back, key_back, grad_parts, out_rows)
    projection_grad, weight_grad = scatter(
        my_quarter, kept_token_indices, grad_packed, weight_grad, tok_dev
    )
    projection_grad = projection_grad.transpose(1, 0, 2)
    return (projection_grad, weight_grad)


def solution(mesh):
    return jax.shard_map(
        on_device,
        mesh=mesh,
        in_specs=(P("seq", None, "head"), P("seq", "head"), P(None, "head"), P("seq", None), P()),
        out_specs=(P("seq", None, "head"), P("seq", "head")),
        check_vma=False,
    )
```

```python
import math

import jax
import jax.numpy as jnp
from jax import lax
from jax.experimental import pallas as pl
from jax.experimental.pallas import tpu as pltpu
from jax.sharding import PartitionSpec as P

DH = 128
BQ = 256
BK = 1536
TAIL = 512
GROUP = 16
NEG = -1e30
CHUNKS = 4
VMEM_BYTES = 63 * 1024 * 1024 + 640 * 1024
K_STEP = 4
DQ_STEP = 4


def contract_rows(left, right):
    return lax.dot_general(
        left, right, (((0,), (0,)), ((), ())), preferred_element_type=jnp.float32
    )


def attend_kernel(
    count_ref,
    quarter_ref,
    q_hbm,
    g_hbm,
    k_hbm,
    v_hbm,
    dq_out,
    o_out,
    k_out,
    q_ref,
    g_ref,
    k_ref,
    v_ref,
    k_stage,
    qc,
    gc,
    kc,
    vc,
    k_turned,
    v_turned,
    q_turned,
    dkc,
    dvc,
    oc,
    s_scr,
    p_scr,
    qpos,
    acc,
    group_pos,
    load_sem,
    store_sem,
):
    shards, part_rows, _ = q_ref.shape
    slots = k_ref.shape[1]
    quarter = quarter_ref[0]
    groups = part_rows // GROUP
    score_scale = 1.0 / math.sqrt(DH)
    log2e = score_scale * math.log2(math.e)
    bf16 = jnp.bfloat16
    loads = [
        pltpu.make_async_copy(src, dst, load_sem.at[i])
        for i, (src, dst) in enumerate(
            ((q_hbm, q_ref), (g_hbm, g_ref), (k_hbm, k_ref), (v_hbm, v_ref))
        )
    ]
    for load in loads:
        load.start()

    def clear(i, carry):
        rows = pl.ds(pl.multiple_of(i * slots, slots), slots)
        dkc[rows, :] = jnp.zeros((slots, DH), jnp.float32)
        dvc[rows, :] = jnp.zeros((slots, DH), jnp.float32)
        return carry

    lax.fori_loop(0, shards, clear, 0)
    q_turned[DH:, :] = jnp.where(
        lax.broadcasted_iota(jnp.int32, (DH, BQ), 0) == 0, 1.0, 0.0
    ).astype(bf16)
    for load in loads:
        load.wait()

    def dead_marks(rows, live):
        row = lax.broadcasted_iota(jnp.int32, (rows, DH), 0)
        lane = lax.broadcasted_iota(jnp.int32, (rows, DH), 1)
        return jnp.where((row >= live) & (lane == 0), NEG, 0.0).astype(bf16)

    def live_groups(s):
        live = (count_ref[s] + GROUP - 1) // GROUP
        first = lax.rem(quarter + s, 4)
        return live, first, (live - first + 3) // 4

    rows_live = GROUP * lax.fori_loop(0, shards, lambda s, n: n + live_groups(s)[2], jnp.int32(0))
    blocks = (rows_live + BQ - 1) // BQ
    end_q = blocks * BQ
    start_q = pl.multiple_of(end_q - rows_live, GROUP)
    qc[pl.ds(0, BQ), :] = jnp.zeros((BQ, DH), bf16)
    gc[pl.ds(0, BQ), :] = jnp.zeros((BQ, DH), bf16)
    qpos[pl.ds(0, BQ), :] = jnp.zeros((BQ, DH), jnp.int32)
    group_pos[0] = 0

    def pack(s, carry):
        at_k, at_q = carry
        live, first, mine = live_groups(s)
        at_k = pl.multiple_of(at_k, GROUP)
        at_q = pl.multiple_of(at_q, GROUP)
        kc[pl.ds(at_k, slots), :DH] = k_ref[s]
        kc[pl.ds(at_k, slots), DH:] = dead_marks(slots, count_ref[s])
        vc[pl.ds(at_k, slots), :] = v_ref[s]
        qc[pl.ds(at_q, part_rows), :] = q_ref[s]
        gc[pl.ds(at_q, part_rows), :] = g_ref[s]
        rows = lax.broadcasted_iota(jnp.int32, (GROUP, DH), 0)
        for i in range(groups):
            base = at_k + (first + 4 * i) * GROUP
            qpos[pl.ds(at_q + i * GROUP, GROUP), :] = base + rows
            group_pos[at_q // GROUP + i] = base
        return at_k + live * GROUP, at_q + mine * GROUP

    end_k, _ = lax.fori_loop(0, shards, pack, (jnp.int32(0), start_q))
    end_k = pl.multiple_of(end_k, GROUP)
    kc[pl.ds(end_k, BK), :DH] = jnp.zeros((BK, DH), bf16)
    kc[pl.ds(end_k, BK), DH:] = dead_marks(BK, 0)
    vc[pl.ds(end_k, BK), :] = jnp.zeros((BK, DH), bf16)
    oc[pl.ds(pl.multiple_of(end_q, BQ), part_rows), :] = jnp.zeros(
        (part_rows, 2 * DH), bf16
    )

    def turn(c, carry):
        keys = pl.ds(pl.multiple_of(c * BK, BK), BK)
        k_turned[:, keys] = kc[keys, :DH].T
        v_turned[:, keys] = vc[keys, :].T
        return carry

    lax.fori_loop(0, (end_k + BK - 1) // BK, turn, 0)

    def block(b, carry):
        rows = pl.ds(pl.multiple_of(b * BQ, BQ), BQ)
        key_end = group_pos[(b + 1) * (BQ // GROUP) - 1] + GROUP
        chunks = (key_end + TAIL - 1) // BK
        tails = (jnp.maximum(key_end - chunks * BK, 0) + TAIL - 1) // TAIL
        first_end = jnp.where(b == 0, 0, group_pos[b * (BQ // GROUP)] + 1)
        clear_chunks = jnp.minimum(first_end // BK, chunks)

        def over(body, carry):
            carry = lax.fori_loop(0, chunks, lambda c, x: body(c * BK, BK, x), carry)
            return lax.fori_loop(
                0, tails, lambda c, x: body(chunks * BK + c * TAIL, TAIL, x), carry
            )

        q_turned[:DH, :] = qc[rows, :].T
        last_key = qpos[rows, :].T[0:1, :]

        def score(at, size, top, masked):
            at = pl.multiple_of(at, TAIL)
            keys = pl.ds(at, size)
            s = jnp.dot(kc[keys, :], q_turned[...], preferred_element_type=jnp.float32)
            if masked:
                key = at + lax.broadcasted_iota(jnp.int32, (size, BQ), 0)
                s = jnp.where(key <= last_key, s, NEG)
            s_scr[keys, :] = s
            return jnp.maximum(top, jnp.max(s, axis=0, keepdims=True))

        top = jnp.full((1, BQ), NEG, jnp.float32)
        top = lax.fori_loop(0, clear_chunks, lambda c, t: score(c * BK, BK, t, False), top)
        top = lax.fori_loop(clear_chunks, chunks, lambda c, t: score(c * BK, BK, t, True), top)
        top = lax.fori_loop(
            0, tails, lambda c, t: score(chunks * BK + c * TAIL, TAIL, t, True), top
        )
        acc[...] = jnp.zeros((DH, BQ), jnp.float32)

        def weigh(at, size, total):
            keys = pl.ds(pl.multiple_of(at, TAIL), size)
            p = jnp.exp2((s_scr[keys, :] - top) * log2e)
            p_low = p.astype(bf16)
            p_scr[keys, :] = p_low
            acc[...] += jnp.dot(v_turned[:, keys], p_low, preferred_element_type=jnp.float32)
            return total + jnp.sum(p, axis=0, keepdims=True)

        total = over(weigh, jnp.zeros((1, BQ), jnp.float32))
        inverse = 1.0 / total
        attended = acc[...] * inverse
        oc[rows, DH:] = attended.T.astype(bf16)
        g_turned = (gc[rows, :].astype(jnp.float32).T * inverse).astype(bf16)
        row_dot = jnp.sum(g_turned.astype(jnp.float32) * attended, axis=0, keepdims=True)
        g_part = g_turned.T
        acc[...] = jnp.zeros((DH, BQ), jnp.float32)

        def back(at, size, carry):
            keys = pl.ds(pl.multiple_of(at, TAIL), size)
            p_low = p_scr[keys, :]
            grad_probs = jnp.dot(vc[keys, :], g_turned, preferred_element_type=jnp.float32)
            ds = (p_low.astype(jnp.float32) * (grad_probs - row_dot)).astype(bf16)
            acc[...] += jnp.dot(k_turned[:, keys], ds, preferred_element_type=jnp.float32)
            dkc[keys, :] += jnp.dot(ds, qc[rows, :], preferred_element_type=jnp.float32)
            dvc[keys, :] += jnp.dot(p_low, g_part, preferred_element_type=jnp.float32)
            return carry

        over(back, 0)
        oc[rows, :DH] = (acc[...] * score_scale).T.astype(bf16)
        return carry

    lax.fori_loop(0, blocks, block, 0)

    def unpack(s, carry):
        at_k, at_q = carry
        live, first, mine = live_groups(s)
        at_k = pl.multiple_of(at_k, GROUP)
        at_q = pl.multiple_of(at_q, GROUP)
        q_ref[s] = oc[pl.ds(at_q, part_rows), :DH]
        g_ref[s] = oc[pl.ds(at_q, part_rows), DH:]
        k_stage[s, :, :DH] = (dkc[pl.ds(at_k, slots), :] * score_scale).astype(bf16)
        k_stage[s, :, DH:] = dvc[pl.ds(at_k, slots), :].astype(bf16)
        pltpu.make_async_copy(k_stage.at[s], k_out.at[s], store_sem.at[0]).start()
        return at_k + live * GROUP, at_q + mine * GROUP

    lax.fori_loop(0, shards, unpack, (jnp.int32(0), start_q))
    stores = [
        pltpu.make_async_copy(q_ref, dq_out, store_sem.at[1]),
        pltpu.make_async_copy(g_ref, o_out, store_sem.at[2]),
    ]
    for store in stores:
        store.start()
    pltpu.make_async_copy(k_stage, k_out, store_sem.at[0]).wait()
    for store in stores:
        store.wait()


def attend(counts, quarter, query_in, grad_in, key_in, value_in):
    shards, part_rows, _ = query_in.shape
    slots = key_in.shape[1]
    keys = shards * slots
    queries = shards * part_rows
    bf16 = jnp.bfloat16
    smem = pl.BlockSpec(memory_space=pltpu.SMEM)
    hbm = pl.BlockSpec(memory_space=pltpu.HBM)
    return pl.pallas_call(
        attend_kernel,
        out_shape=(
            jax.ShapeDtypeStruct((shards, part_rows, DH), bf16),
            jax.ShapeDtypeStruct((shards, part_rows, DH), bf16),
            jax.ShapeDtypeStruct((shards, slots, 2 * DH), bf16),
        ),
        in_specs=[smem, smem, hbm, hbm, hbm, hbm],
        out_specs=(hbm, hbm, hbm),
        scratch_shapes=[
            pltpu.VMEM((shards, part_rows, DH), bf16),
            pltpu.VMEM((shards, part_rows, DH), bf16),
            pltpu.VMEM((shards, slots, DH), bf16),
            pltpu.VMEM((shards, slots, DH), bf16),
            pltpu.VMEM((shards, slots, 2 * DH), bf16),
            pltpu.VMEM((queries + BQ, DH), bf16),
            pltpu.VMEM((queries + BQ, DH), bf16),
            pltpu.VMEM((keys + BK, 2 * DH), bf16),
            pltpu.VMEM((keys + BK, DH), bf16),
            pltpu.VMEM((DH, keys), bf16),
            pltpu.VMEM((DH, keys), bf16),
            pltpu.VMEM((2 * DH, BQ), bf16),
            pltpu.VMEM((keys, DH), jnp.float32),
            pltpu.VMEM((keys, DH), jnp.float32),
            pltpu.VMEM((queries + BQ, 2 * DH), bf16),
            pltpu.VMEM((keys, BQ), jnp.float32),
            pltpu.VMEM((keys, BQ), bf16),
            pltpu.VMEM((queries + BQ, DH), jnp.int32),
            pltpu.VMEM((DH, BQ), jnp.float32),
            pltpu.SMEM((queries // GROUP + 8,), jnp.int32),
            pltpu.SemaphoreType.DMA((4,)),
            pltpu.SemaphoreType.DMA((3,)),
        ],
        compiler_params=pltpu.CompilerParams(vmem_limit_bytes=VMEM_BYTES),
        cost_estimate=pl.CostEstimate(
            flops=6 * queries * keys * DH, bytes_accessed=16 * 1024 * 1024, transcendentals=0
        ),
        name="attend",
    )(counts, quarter, query_in, grad_in, key_in, value_in)


def block_bytes_wait(ref, sem):
    pltpu.make_async_copy(ref, ref, sem).wait()


def greet(peers, peer_of, ring=0, meanwhile=None):
    barrier = pltpu.get_barrier_semaphore()

    def signal(k, carry):
        pl.semaphore_signal(
            barrier, inc=1, device_id={"seq": peer_of(k)}, device_id_type=pl.DeviceIdType.MESH
        )
        return carry

    lax.fori_loop(1, peers + 1, signal, 0)
    if ring:
        row = lax.axis_index("head")
        for k in range(1, ring):
            pl.semaphore_signal(
                barrier,
                inc=1,
                device_id={"head": lax.rem(row + k, ring)},
                device_id_type=pl.DeviceIdType.MESH,
            )
        peers = peers + ring - 1
    if meanwhile is not None:
        meanwhile()
    pl.semaphore_wait(barrier, peers)


def send(src, dst, send_sem, recv_sem, target, axis="seq"):
    copy = pltpu.make_async_remote_copy(
        src_ref=src,
        dst_ref=dst,
        send_sem=send_sem,
        recv_sem=recv_sem,
        device_id={axis: target},
        device_id_type=pl.DeviceIdType.MESH,
    )
    copy.start()
    return copy


def dealt_rows(group, first, part_rows):
    at = lax.rem(group + 4 - first, 4) * part_rows + group // 4 * GROUP
    return pl.ds(pl.multiple_of(at, GROUP), GROUP)


def spread_kernel(
    all_grad_ref,
    kept_ref,
    p_hbm,
    w_hbm,
    g0_out,
    g1_out,
    g2_out,
    g3_out,
    q_in,
    g_in,
    k_in,
    v_in,
    w_ref,
    p_ref,
    select,
    grad_ref,
    q_ref,
    k_ref,
    v_ref,
    acc,
    g_local,
    gblk,
    k_col,
    v_col,
    w_sem,
    p_sem,
    copy_sem,
    y_send,
    y_recv,
    z_send,
    z_recv,
    x_send,
    x_recv,
    own_sem,
    pass_send,
    pass_recv,
    q_send,
    q_recv,
    q_own,
):
    shards, part_rows, _ = q_in.shape
    slots, cols = grad_ref.shape
    half = cols // 2
    me = lax.axis_index("seq")
    row = lax.axis_index("head")
    core = me % 2
    sibling = me + 1 - 2 * core
    my_z = me // 8
    my_x = me // 2 % 4
    my_head = me // 4
    my_rows = pl.ds(pl.multiple_of((me % 4) * part_rows, GROUP), part_rows)

    load_w = pltpu.make_async_copy(w_hbm, w_ref, w_sem)
    load_p = pltpu.make_async_copy(p_hbm, p_ref, p_sem)
    load_p.start()
    load_w.start()
    width = 256
    tiles = acc.shape[1] // width

    def pick():
        token = lax.broadcasted_iota(jnp.int32, select.shape, 0)
        select[...] = jnp.where(token == kept_ref[...], 1.0, 0.0).astype(jnp.bfloat16)

        def deal(out, at, values):
            for g in range(slots // GROUP):
                out[dealt_rows(g, me % 4, part_rows), at] = values[g * GROUP : (g + 1) * GROUP]

        def grad_tile(j, carry):
            at = pl.ds(pl.multiple_of(j * width, width), width)
            picked = contract_rows(select[...], all_grad_ref[:, at])
            deal(grad_ref, at, picked.astype(jnp.bfloat16))
            return carry

        lax.fori_loop(0, cols // width, grad_tile, 0)
        load_p.wait()

        def tile(j, carry):
            at = pl.ds(pl.multiple_of(j * width, width), width)
            picked = [
                contract_rows(select[...], p_ref[i, :, at]).astype(jnp.bfloat16) for i in range(3)
            ]
            deal(q_ref, at, picked[0])
            k_ref[:, at] = picked[1]
            v_ref[:, at] = picked[2]
            return carry

        lax.fori_loop(0, tiles, tile, 0)

    greet(shards - 1, lambda k: lax.rem(me + k, shards), 4, pick)

    def head_cols(head):
        return pl.ds(pl.multiple_of(head * DH, DH), DH)

    def pair_cols(z):
        return pl.ds(pl.multiple_of(z * 2 * DH, 2 * DH), 2 * DH)

    def slot_of(y):
        return lax.rem(y - my_z + 4, 4)

    right, left, across = lax.rem(row + 1, 4), lax.rem(row + 3, 4), lax.rem(row + 2, 4)
    to_right = send(grad_ref, gblk.at[slot_of(row)], y_send.at[0], y_recv.at[0], right, "head")
    to_left = send(grad_ref, gblk.at[slot_of(row)], y_send.at[1], y_recv.at[1], left, "head")

    sides = ((k_ref, k_col, k_in), (v_ref, v_col, v_in))
    for k in (1, 3, 2):
        target = lax.rem(me + 8 * k, shards)
        for i, (src, col, _) in enumerate(sides):
            send(
                src.at[:, pair_cols(lax.rem(my_z + k, 4))],
                col.at[my_z],
                z_send.at[i],
                z_recv.at[i, k],
                target,
            )

    def fan(k):
        z = lax.rem(my_z - k + 4, 4)
        for i, (src, col, out) in enumerate(sides):
            if k:
                block_bytes_wait(col.at[z], z_recv.at[i, k])
            else:
                col[z] = src[:, pair_cols(my_z)]
            for d in (1, 3, 2):
                x = lax.rem(my_x + d, 4)
                send(
                    col.at[z, :, head_cols(x // 2)],
                    out.at[z, my_x, core],
                    x_send.at[i],
                    x_recv.at[i, k],
                    me + 2 * (x - my_x),
                )
            pltpu.make_async_copy(
                col.at[z, :, head_cols(my_x // 2)], out.at[z, my_x, core], own_sem.at[i, k]
            ).start()

    def pass_on(k):
        z = lax.rem(my_z - k + 4, 4)
        for i, (_, _, out) in enumerate(sides):
            block_bytes_wait(out.at[z, pl.ds(0, 3), core], x_recv.at[i, k])
            block_bytes_wait(out.at[z, my_x, core], own_sem.at[i, k])
            send(out.at[z, :, core], out.at[z, :, core], pass_send.at[i], pass_recv.at[i], sibling)

    fan(0)

    def send_q(k, carry):
        t = lax.rem(me + k, shards)
        rows = pl.ds(pl.multiple_of((t % 4) * part_rows, GROUP), part_rows)
        send(q_ref.at[rows, head_cols(t // 4)], q_in.at[me], q_send.at[0], q_recv.at[0], t)
        return carry

    lax.fori_loop(1, shards, send_q, 0)
    own_q = pltpu.make_async_copy(q_ref.at[my_rows, head_cols(my_head)], q_in.at[me], q_own.at[0])
    own_q.start()

    gblk[slot_of(row)] = grad_ref[...]
    load_w.wait()

    def multiply(y, first):
        def tile(j, carry):
            at = pl.ds(pl.multiple_of(j * width, width), width)
            rows = pl.ds(pl.multiple_of(y * cols, width), cols)
            part = jnp.dot(gblk[slot_of(y)], w_ref[rows, at], preferred_element_type=jnp.float32)
            acc[:, at] = part if first else acc[:, at] + part
            return carry

        lax.fori_loop(0, tiles, tile, 0)

    multiply(row, True)
    for k in (1, 3, 2):
        fan(k)
    to_right.wait_recv()
    from_left = gblk.at[slot_of(left), :, pl.ds(0, half)]
    on_right = send(from_left, from_left, y_send.at[2], y_recv.at[2], right, "head")
    to_left.wait_recv()
    from_right = gblk.at[slot_of(right), :, pl.ds(half, half)]
    on_left = send(from_right, from_right, y_send.at[3], y_recv.at[3], left, "head")
    pass_on(0)
    multiply(left, False)
    pass_on(1)
    multiply(right, False)
    pass_on(3)
    on_right.wait_recv()
    on_left.wait_recv()

    def finish(step, carry):
        j = lax.rem(my_head // 2 + step, tiles)
        at = pl.ds(pl.multiple_of(j * width, width), width)
        rows = pl.ds(pl.multiple_of(across * cols, width), cols)
        part = jnp.dot(gblk[slot_of(across)], w_ref[rows, at], preferred_element_type=jnp.float32)
        g_local[:, at] = (acc[:, at] + part).astype(jnp.bfloat16)
        for i in range(8):
            t = j * 8 + i
            part_at = (i % 4) * part_rows

            @pl.when(t != me)
            def _():
                send(
                    g_local.at[pl.ds(part_at, part_rows), head_cols(t // 4)],
                    g_in.at[me],
                    q_send.at[1],
                    q_recv.at[1],
                    t,
                )

        return carry

    lax.fori_loop(0, tiles, finish, 0)
    own_g = pltpu.make_async_copy(
        g_local.at[my_rows, head_cols(my_head)], g_in.at[me], q_own.at[1]
    )
    own_g.start()
    copies = [
        pltpu.make_async_copy(gblk.at[k], out, copy_sem.at[k])
        for k, out in enumerate((g0_out, g1_out, g2_out, g3_out))
    ]
    for copy in copies:
        copy.start()
    pass_on(2)
    for copy in copies:
        copy.wait()
    own_q.wait()
    own_g.wait()

    others = pl.ds(0, shards - 1)
    block_bytes_wait(q_in.at[others], q_recv.at[0])
    block_bytes_wait(q_in.at[others], q_send.at[0])
    for i, (_, col, out) in enumerate(sides):
        block_bytes_wait(out.at[:, :, core], pass_recv.at[i])
        block_bytes_wait(out.at[:, :, core], pass_send.at[i])
        block_bytes_wait(col.at[pl.ds(0, 3)], z_send.at[i])
        block_bytes_wait(out.at[:, pl.ds(0, 3), core], x_send.at[i])
    for copy in (to_right, to_left, on_right, on_left):
        copy.wait_send()
    block_bytes_wait(g_in.at[others], q_recv.at[1])
    block_bytes_wait(g_in.at[others], q_send.at[1])


def spread(output_gradient, kept, projections, weight, shards):
    tokens, cols = output_gradient.shape
    slots = kept.shape[1]
    depth, width = weight.shape
    part_rows = slots // 4
    bf16 = jnp.bfloat16
    vmem = pl.BlockSpec(memory_space=pltpu.VMEM)
    block = jax.ShapeDtypeStruct((slots, cols), bf16)
    small = jax.ShapeDtypeStruct((shards, part_rows, DH), bf16)
    large = jax.ShapeDtypeStruct((4, 4, 2, slots, DH), bf16)
    *blocks, query_in, grad_in, key_in, value_in = pl.pallas_call(
        spread_kernel,
        out_shape=(block,) * 4 + (small,) * 2 + (large,) * 2,
        in_specs=[vmem] * 2 + [pl.BlockSpec(memory_space=pltpu.HBM)] * 2,
        out_specs=(pl.BlockSpec(memory_space=pltpu.HBM),) * 8,
        scratch_shapes=[
            pltpu.VMEM((depth, width), bf16),
            pltpu.VMEM(projections.shape, bf16),
            pltpu.VMEM((tokens, slots), bf16),
            pltpu.VMEM((slots, cols), bf16),
            pltpu.VMEM((slots, width), bf16),
            pltpu.VMEM((slots, width), bf16),
            pltpu.VMEM((slots, width), bf16),
            pltpu.VMEM((slots, width), jnp.float32),
            pltpu.VMEM((slots, width), bf16),
            pltpu.VMEM((4, slots, cols), bf16),
            pltpu.VMEM((4, slots, 2 * DH), bf16),
            pltpu.VMEM((4, slots, 2 * DH), bf16),
            pltpu.SemaphoreType.DMA,
            pltpu.SemaphoreType.DMA,
            pltpu.SemaphoreType.DMA((4,)),
            pltpu.SemaphoreType.DMA((4,)),
            pltpu.SemaphoreType.DMA((4,)),
            pltpu.SemaphoreType.DMA((2,)),
            pltpu.SemaphoreType.DMA((2, 4)),
            pltpu.SemaphoreType.DMA((2,)),
            pltpu.SemaphoreType.DMA((2, 4)),
            pltpu.SemaphoreType.DMA((2, 4)),
            pltpu.SemaphoreType.DMA((2,)),
            pltpu.SemaphoreType.DMA((2,)),
            pltpu.SemaphoreType.DMA((2,)),
            pltpu.SemaphoreType.DMA((2,)),
            pltpu.SemaphoreType.DMA((2,)),
        ],
        compiler_params=pltpu.CompilerParams(
            collective_id=2, has_side_effects=True, vmem_limit_bytes=VMEM_BYTES
        ),
        name="spread",
    )(output_gradient, kept, projections, weight)
    key_in = key_in.reshape(shards, slots, DH)
    value_in = value_in.reshape(shards, slots, DH)
    return (*blocks, query_in, grad_in, key_in, value_in)


def home_kernel(
    o_ref,
    dq_ref,
    k_ref,
    g0_ref,
    g1_ref,
    g2_ref,
    g3_ref,
    home,
    wg_out,
    g_vmem,
    k_own,
    g_turned,
    oz,
    kx,
    ks,
    k_row,
    k_pair,
    k_col,
    part,
    px,
    half_send,
    half_recv,
    full_send,
    full_recv,
    send_sem,
    recv_sem,
    load_sem,
    k_send,
    k_recv,
    z_send,
    z_recv,
    p_send,
    p_recv,
    x_send,
    x_recv,
):
    shards, part_rows, _ = o_ref.shape
    slots = k_ref.shape[3]
    me = lax.axis_index("seq")
    core = me % 2
    sibling = me + 1 - 2 * core
    plane_x = me // 2 % 4
    my_z = me // 8
    out_rows, width = wg_out.shape
    my_rows = pl.ds(pl.multiple_of((me % 4) * part_rows, GROUP), part_rows)
    my_cols = pl.ds(pl.multiple_of((me // 4) * DH, DH), DH)
    f32, bf16 = jnp.float32, jnp.bfloat16

    loads = [
        pltpu.make_async_copy(src, dst, load_sem.at[i])
        for i, (src, dst) in enumerate(
            (
                (o_ref.at[me], oz.at[0, my_rows, my_cols]),
                (g0_ref, g_vmem.at[0]),
                (g1_ref, g_vmem.at[1]),
                (g2_ref, g_vmem.at[2]),
                (g3_ref, g_vmem.at[3]),
                (k_ref.at[:, :, core], k_own),
                (dq_ref.at[me], home.at[0, my_rows, my_cols]),
            )
        )
    ]
    for load in loads:
        load.start()
    greet(shards - 1, lambda k: lax.rem(me + k, shards))

    def send_o(k, carry):
        t = lax.rem(me + k, shards)
        send(o_ref.at[t], oz.at[0, my_rows, my_cols], send_sem.at[0], recv_sem.at[0], t)
        return carry

    lax.fori_loop(1, shards, send_o, 0)
    swap = send(k_ref.at[:, :, 1 - core], kx, send_sem.at[1], recv_sem.at[1], sibling)
    for load in loads:
        load.wait()

    tile = 256

    def turn(j, carry):
        cols = pl.ds(pl.multiple_of(j * tile, tile), tile)
        for k in range(4):
            g_turned[k, cols, :] = g_vmem[k, :, cols].T
        return carry

    lax.fori_loop(0, part.shape[0] // tile, turn, 0)
    block_bytes_wait(o_ref.at[pl.ds(0, shards - 1)], recv_sem.at[0])

    chunk = width // CHUNKS
    z_up, z_down = lax.rem(me + 8, shards), lax.rem(me + 24, shards)
    x_up = me + 2 * (lax.rem(plane_x + 1, 4) - plane_x)
    x_down = me + 2 * (lax.rem(plane_x + 3, 4) - plane_x)
    upper, lower = pl.ds(0, slots // 2), pl.ds(slots // 2, slots // 2)
    top, bottom = pl.ds(0, out_rows // 2), pl.ds(out_rows // 2, out_rows // 2)

    def cols_of(c):
        return pl.ds(c * chunk, chunk)

    def start_z(c):
        own = oz.at[0, :, cols_of(c)]
        send(own, oz.at[1, :, cols_of(c)], z_send.at[0], z_recv.at[0, c], z_up)
        send(own, oz.at[3, :, cols_of(c)], z_send.at[1], z_recv.at[1, c], z_down)

    def forward_z(c):
        cols = cols_of(c)
        block_bytes_wait(oz.at[1, :, cols], z_recv.at[0, c])
        send(
            oz.at[1, upper, cols], oz.at[2, upper, cols], z_send.at[2], z_recv.at[2, c], z_up
        )
        block_bytes_wait(oz.at[3, :, cols], z_recv.at[1, c])
        send(
            oz.at[3, lower, cols], oz.at[2, lower, cols], z_send.at[3], z_recv.at[3, c], z_down
        )
        if c + 2 < CHUNKS:
            start_z(c + 2)

    def piece(x, c):
        return pl.ds(pl.multiple_of((2 * x + c) * out_rows, 32), out_rows)

    def product(c):
        cols = cols_of(c)
        block_bytes_wait(oz.at[2, upper, cols], z_recv.at[2, c])
        block_bytes_wait(oz.at[2, lower, cols], z_recv.at[3, c])

        def rows_tile(j, carry):
            rows = pl.ds(pl.multiple_of(j * tile, tile), tile)
            total = jnp.dot(g_turned[0, rows, :], oz[0, :, cols], preferred_element_type=f32)
            for k in (1, 2, 3):
                total += jnp.dot(g_turned[k, rows, :], oz[k, :, cols], preferred_element_type=f32)
            part[rows, cols] = total.astype(bf16)
            return carry

        lax.fori_loop(0, part.shape[0] // tile, rows_tile, 0)
        for x in range(4):
            send(
                part.at[piece(x, 1 - core), cols],
                px.at[x, :, cols],
                p_send,
                p_recv.at[c],
                sibling,
            )

    def pair_sum(x, c):
        cols = cols_of(c)
        return part[piece(x, core), cols].astype(f32) + px[x, :, cols].astype(f32)

    def send_half(c):
        cols = cols_of(c)
        block_bytes_wait(px.at[:, :, cols], p_recv.at[c])
        half_send[:, cols] = pair_sum(lax.rem(plane_x + 2, 4), c).astype(bf16)
        send(
            half_send.at[top, cols], half_recv.at[top, cols], x_send.at[0], x_recv.at[0, c], x_up
        )
        send(
            half_send.at[bottom, cols],
            half_recv.at[bottom, cols],
            x_send.at[1],
            x_recv.at[1, c],
            x_down,
        )

    def send_full(c):
        cols = cols_of(c)
        split = out_rows // 2
        block_bytes_wait(half_recv.at[top, cols], x_recv.at[0, c])
        ahead = pair_sum(lax.rem(plane_x + 1, 4), c)
        full_send[0, top, cols] = (ahead[:split] + half_recv[top, cols].astype(f32)).astype(bf16)
        full_send[0, bottom, cols] = ahead[split:].astype(bf16)
        send(
            full_send.at[0, :, cols], full_recv.at[0, :, cols], x_send.at[2], x_recv.at[2, c], x_up
        )
        block_bytes_wait(half_recv.at[bottom, cols], x_recv.at[1, c])
        behind = pair_sum(lax.rem(plane_x + 3, 4), c)
        full_send[1, top, cols] = behind[:split].astype(bf16)
        full_send[1, bottom, cols] = (behind[split:] + half_recv[bottom, cols].astype(f32)).astype(
            bf16
        )
        send(
            full_send.at[1, :, cols],
            full_recv.at[1, :, cols],
            x_send.at[3],
            x_recv.at[3, c],
            x_down,
        )

    def finish(c):
        cols = cols_of(c)
        block_bytes_wait(full_recv.at[0, :, cols], x_recv.at[2, c])
        block_bytes_wait(full_recv.at[1, :, cols], x_recv.at[3, c])
        wg_out[:, cols] = (
            pair_sum(plane_x, c)
            + full_recv[0, :, cols].astype(f32)
            + full_recv[1, :, cols].astype(f32)
        )

    def k_sum(z, x):
        return (k_own[z, x].astype(f32) + kx[z, x].astype(f32)).astype(bf16)

    def k_along_x():
        for k in (1, 2, 3):
            x = lax.rem(plane_x + k, 4)
            for z in range(4):
                ks[z, x] = k_sum(z, x)
            send(
                ks.at[:, x],
                k_row.at[plane_x],
                k_send.at[k - 1],
                k_recv.at[k - 1],
                me + 2 * (x - plane_x),
            )
        for z in range(4):
            k_row[plane_x, z] = k_sum(z, plane_x)

    def k_along_z():
        for k in range(3):
            block_bytes_wait(k_row.at[0], k_recv.at[k])
        for k in (1, 2, 3, 0):
            z = lax.rem(my_z + k, 4)
            for h in range(2):
                pair = k_row[2 * h, z].astype(f32) + k_row[2 * h + 1, z].astype(f32)
                k_pair[z, h] = pair.astype(bf16)
            if k:
                send(
                    k_pair.at[z],
                    k_col.at[my_z],
                    k_send.at[2 + k],
                    k_recv.at[2 + k],
                    lax.rem(me + 8 * k, shards),
                )
            else:
                k_col[my_z] = k_pair[z]

    def send_dq(k, carry):
        t = lax.rem(me + k, shards)
        send(dq_ref.at[t], home.at[0, my_rows, my_cols], send_sem.at[3], recv_sem.at[3], t)
        return carry

    start_z(0)
    start_z(1)
    swap.wait()
    k_along_x()
    stages = (forward_z, product, send_half, send_full, finish)
    for step in range(CHUNKS + len(stages) - 1):
        if step == K_STEP:
            k_along_z()
        if step == DQ_STEP:
            lax.fori_loop(1, shards, send_dq, 0)
        for i, stage in enumerate(stages):
            if 0 <= step - i < CHUNKS:
                stage(step - i)
    for k in range(3):
        block_bytes_wait(k_col.at[0], k_recv.at[3 + k])
    for z in range(4):
        for h in range(2):
            cols = pl.ds((2 * z + h) * DH, DH)
            home[1, :, cols] = k_col[z, h, :, :DH]
            home[2, :, cols] = k_col[z, h, :, DH:]
    block_bytes_wait(dq_ref.at[pl.ds(0, shards - 1)], recv_sem.at[3])
    block_bytes_wait(o_ref.at[pl.ds(0, shards - 1)], send_sem.at[0])
    for k in range(3):
        block_bytes_wait(ks.at[:, 0], k_send.at[k])
        block_bytes_wait(k_pair.at[0], k_send.at[3 + k])
    block_bytes_wait(dq_ref.at[pl.ds(0, shards - 1)], send_sem.at[3])
    block_bytes_wait(oz.at[0], z_send.at[0])
    block_bytes_wait(oz.at[0], z_send.at[1])
    block_bytes_wait(oz.at[1, upper], z_send.at[2])
    block_bytes_wait(oz.at[3, lower], z_send.at[3])
    block_bytes_wait(px, p_send)
    block_bytes_wait(half_send.at[top], x_send.at[0])
    block_bytes_wait(half_send.at[bottom], x_send.at[1])
    block_bytes_wait(full_send.at[0], x_send.at[2])
    block_bytes_wait(full_send.at[1], x_send.at[3])


def bring_home(o_back, dq_back, key_back, grad_parts, out_rows):
    shards, part_rows, _ = o_back.shape
    slots = key_back.shape[1]
    width = shards // 4 * DH
    rows = grad_parts[0].shape[1]
    key_back = key_back.reshape(4, 4, 2, slots, 2 * DH)
    vmem = pl.BlockSpec(memory_space=pltpu.VMEM)
    bf16 = jnp.bfloat16
    return pl.pallas_call(
        home_kernel,
        out_shape=(
            jax.ShapeDtypeStruct((3, slots, width), bf16),
            jax.ShapeDtypeStruct((out_rows, width), jnp.float32),
        ),
        in_specs=[pl.BlockSpec(memory_space=pltpu.HBM)] * 3
        + [pl.BlockSpec(memory_space=pl.ANY)] * 4,
        out_specs=(vmem,) * 2,
        scratch_shapes=[
            pltpu.VMEM((4, slots, rows), bf16),
            pltpu.VMEM((4, 4, slots, 2 * DH), bf16),
            pltpu.VMEM((4, rows, slots), bf16),
            pltpu.VMEM((4, slots, width), bf16),
            pltpu.VMEM((4, 4, slots, 2 * DH), bf16),
            pltpu.VMEM((4, 4, slots, 2 * DH), bf16),
            pltpu.VMEM((4, 4, slots, 2 * DH), bf16),
            pltpu.VMEM((4, 2, slots, 2 * DH), bf16),
            pltpu.VMEM((4, 2, slots, 2 * DH), bf16),
            pltpu.VMEM((rows, width), bf16),
            pltpu.VMEM((4, out_rows, width), bf16),
            pltpu.VMEM((out_rows, width), bf16),
            pltpu.VMEM((out_rows, width), bf16),
            pltpu.VMEM((2, out_rows, width), bf16),
            pltpu.VMEM((2, out_rows, width), bf16),
            pltpu.SemaphoreType.DMA((4,)),
            pltpu.SemaphoreType.DMA((4,)),
            pltpu.SemaphoreType.DMA((7,)),
            pltpu.SemaphoreType.DMA((6,)),
            pltpu.SemaphoreType.DMA((6,)),
            pltpu.SemaphoreType.DMA((4,)),
            pltpu.SemaphoreType.DMA((4, CHUNKS)),
            pltpu.SemaphoreType.DMA,
            pltpu.SemaphoreType.DMA((CHUNKS,)),
            pltpu.SemaphoreType.DMA((4,)),
            pltpu.SemaphoreType.DMA((4, CHUNKS)),
        ],
        compiler_params=pltpu.CompilerParams(
            collective_id=1, has_side_effects=True, vmem_limit_bytes=VMEM_BYTES
        ),
        name="home",
    )(o_back, dq_back, key_back, *grad_parts)


def scatter_kernel(
    first_ref, kept_ref, packed_ref, weight_ref, out_ref, weight_out, rows_ref, move_sem
):
    slots = rows_ref.shape[0]
    move = pltpu.make_async_copy(weight_ref, weight_out, move_sem)

    @pl.when(pl.program_id(0) == 0)
    def _():
        move.start()
        for g in range(slots // GROUP):
            dealt = dealt_rows(g, first_ref[0], slots // 4)
            rows_ref[g * GROUP : (g + 1) * GROUP, :] = packed_ref[0, dealt, :]

    @pl.when(pl.program_id(0) > 0)
    def _():
        rows_ref[...] = packed_ref[0]

    token = lax.broadcasted_iota(jnp.int32, (out_ref.shape[1], slots), 0)
    select = jnp.where(token == kept_ref[...], 1.0, 0.0).astype(jnp.bfloat16)
    out_ref[0] = jnp.dot(
        select, rows_ref[...], preferred_element_type=jnp.float32
    ).astype(jnp.bfloat16)

    @pl.when(pl.program_id(0) == pl.num_programs(0) - 1)
    def _():
        move.wait()


def scatter(first, kept, packed, weight_grad, tokens):
    parts, slots, width = packed.shape
    return pl.pallas_call(
        scatter_kernel,
        grid=(parts,),
        out_shape=(
            jax.ShapeDtypeStruct((parts, tokens, width), jnp.bfloat16),
            jax.ShapeDtypeStruct(weight_grad.shape, jnp.float32),
        ),
        in_specs=[
            pl.BlockSpec(memory_space=pltpu.SMEM),
            pl.BlockSpec((1, slots), lambda i: (0, 0)),
            pl.BlockSpec((1, slots, width), lambda i: (i, 0, 0)),
            pl.BlockSpec(weight_grad.shape, lambda i: (0, 0)),
        ],
        out_specs=(
            pl.BlockSpec((1, tokens, width), lambda i: (i, 0, 0)),
            pl.BlockSpec(memory_space=pl.ANY),
        ),
        scratch_shapes=[pltpu.VMEM((slots, width), jnp.bfloat16), pltpu.SemaphoreType.DMA],
        compiler_params=pltpu.CompilerParams(vmem_limit_bytes=VMEM_BYTES),
        name="scatter",
    )(first, kept, packed, weight_grad)


def on_device(
    projections,
    output_gradient,
    output_projection_weight,
    kept_token_indices,
    surviving_token_count,
):
    tok_dev = projections.shape[0]
    group_width = projections.shape[2]
    slots = kept_token_indices.shape[1]
    heads_local = group_width // DH
    seq_count = lax.axis_size("seq")
    quarters = seq_count // heads_local
    part_rows = slots // quarters
    me = lax.axis_index("seq")
    my_quarter = (me % quarters).astype(jnp.int32)[None]

    *blocks, query_in, grad_in, key_in, value_in = spread(
        output_gradient,
        kept_token_indices,
        projections.transpose(1, 0, 2),
        output_projection_weight,
        seq_count,
    )

    def along_z(k):
        if k == 0:
            return blocks[0]
        return lax.ppermute(
            blocks[k], "seq", [(i, (i + 8 * k) % seq_count) for i in range(seq_count)]
        )

    grad_parts = [along_z(k) for k in range(4)]
    dq_back, o_back, key_back = attend(
        surviving_token_count, my_quarter, query_in, grad_in, key_in, value_in
    )
    out_rows = output_projection_weight.shape[0] // seq_count
    grad_packed, weight_grad = bring_home(o_back, dq_back, key_back, grad_parts, out_rows)
    projection_grad, weight_grad = scatter(
        my_quarter, kept_token_indices, grad_packed, weight_grad, tok_dev
    )
    projection_grad = projection_grad.transpose(1, 0, 2)
    return (projection_grad, weight_grad)


def solution(mesh):
    return jax.shard_map(
        on_device,
        mesh=mesh,
        in_specs=(P("seq", None, "head"), P("seq", "head"), P(None, "head"), P("seq", None), P()),
        out_specs=(P("seq", None, "head"), P("seq", "head")),
        check_vma=False,
    )
```
